32 devices in a mesh: rep: 2 (over y), grid: 8 (over z, x), eig: 2 (over core).
Axes of the slice: x: 2, y: 2, z: 4, core: 2. Of those that a mesh axis runs over, the one named last changes fastest.
Arguments:
- eigvecs: bfloat16 [3584, 32768], P('eig', ('rep', 'grid')), parts along dimension 1, may hold values from -0.046875 to 0.046875
- lanczos: bfloat16 [8, 32768], P(None, ('rep', 'grid')), parts along dimension 1, may hold values from -6 to 6
- bands: bfloat16 [64, 32768], P('eig', ('rep', 'grid')), parts along dimension 1, may hold values from -6 to 6
- band_order: int32 [128], P('rep'), parts along dimension 0, may hold values from 0 to 63, each once
Outputs:
- brakets: float32 [128, 8, 3584], P(('rep', 'grid'), None, 'eig'), parts along dimension 0
The draws below stay inside these ranges and needn't reach their ends.
There are 2 independent parts, one for each index of `rep`. The reference program is written for one: setup_inputs(seed, part) draws one part's arguments, and reference() takes and returns one part's arrays. A program takes and returns all parts, laid end to end along the dimension named above; each array names one. Nothing has to cross between parts.
Inputs may be any that keep to these rules, and one draw needn't show every extreme that they name: `band_order`: each occupied band index appears exactly once.
All inputs are finite; a program needn't handle non-finite values.
Results may differ from the reference program's by a relative error of at most 0.0029.
Values may be sent and summed in bfloat16 or wider, within the bound.
No kernel may reach another device: no remote copies, remote signals or barrier semaphores. Data moves between devices by JAX's collectives and lax.ppermute only.
A program may use at most 64 MiB of HBM per device.

```python
import jax
import jax.numpy as jnp
from jax import lax

NEIG = 3584
LANC = 8
NV = 64
NPTS = 16384


def raised(entries, rng, source, target, blocks, factor):
    def block_of(axis_at):
        return (jnp.arange(entries.shape[axis_at]) // (entries.shape[axis_at] // blocks)).reshape((-1,) + (1,) * (entries.ndim - 1 - axis_at))

    one_side = jax.random.permutation(rng, blocks)[block_of(target)]
    far = (block_of(target) + blocks // 2) % blocks
    return jnp.where((block_of(source) == one_side) | (block_of(source) == far), factor * entries, entries)


def block_scale(key, dims, pieces, least, top_value):
    factor_of, own = 1.0, jax.random.fold_in(key, 6)
    for position, blocks in pieces:
        steps = jnp.exp(jax.random.uniform(jax.random.fold_in(own, position), (blocks,), jnp.float32, least / len(pieces), top_value / len(pieces)))
        factor_of = factor_of * jnp.repeat(steps, dims[position] // blocks).reshape([-1 if axis == position else 1 for axis in range(len(dims))])
    return factor_of


def noise(key, dims, scale, most, split=(), held_as=jnp.bfloat16):
    factor_of = block_scale(key, dims, split, -0.22, 0.18) if split else 1.0
    values = jax.random.normal(key, dims, jnp.float32) * scale * factor_of
    return jnp.minimum(jnp.maximum(values, -most), most).astype(held_as)


def gaussian_with(key, dims, scale, bound, split, heavy, dtype=jnp.bfloat16):
    array = scale * jax.random.normal(key, dims, jnp.float32)
    if split:
        array = array * block_scale(key, dims, split, -0.22, 0.18)
    return jnp.clip(raised(array, jax.random.fold_in(key, 3), *heavy), -bound, bound).astype(dtype)


def setup_inputs(seed: int = 0, part: int = 0) -> dict:
    arg_keys = jax.random.split(jax.random.key(seed), 5)
    part_keys = jax.random.split(jax.random.fold_in(arg_keys[4], part), 5)
    eigvecs = noise(part_keys[0], (NEIG, NPTS), NPTS ** -0.5, 0.046875, ((0, 2), (1, 8)))
    lanczos = noise(part_keys[1], (LANC, NPTS), 1.0, 6.0, ((1, 8),))
    bands = gaussian_with(part_keys[2], (NV, NPTS), 1.0, 6.0, ((0, 2), (1, 8)), (1, 0, 8, 2.0))
    band_order = jax.random.permutation(part_keys[3], NV).astype(jnp.int32)
    return {"eigvecs": eigvecs, "lanczos": lanczos, "bands": bands, "band_order": band_order}


def reference(eigvecs, lanczos, bands, band_order):
    selected = jnp.take(bands, band_order.astype(jnp.int32), axis=0)
    products = (selected[:, None, :].astype(jnp.float32) * lanczos[None, :, :].astype(jnp.float32)).astype(jnp.bfloat16)
    flat = products.reshape(NV * LANC, NPTS)
    result = lax.dot_general(flat, eigvecs, (((1,), (1,)), ((), ())), preferred_element_type=jnp.float32)
    return result.reshape(NV, LANC, NEIG)
```

```python
import functools

import jax
import jax.numpy as jnp
from jax import lax
from jax.experimental import pallas as pl
from jax.experimental.pallas import tpu as pltpu
from jax.sharding import PartitionSpec as P

TILE = 256
VMEM_LIMIT = 40 * 1024 * 1024


def ranked(bits, fixed):
    out = [fixed]
    for b in reversed(bits):
        out = [c | (1 << b) for c in out] + out
    return out


def row_slots(n):
    rest = list(range(2, n.bit_length() - 1))
    a, b, c, d = (ranked(rest, f) for f in (1, 3, 2, 0))
    return a + b + c + d + a


def products_kernel(n, per_chunk, order_ref, own_ref, other_ref, lanc_ref, out_ref, held):
    me = lax.axis_index("grid")
    core = lax.axis_index("eig")
    half = own_ref.shape[0]
    held[:half, :] = own_ref[...].astype(jnp.float32)
    held[half:, :] = other_ref[...].astype(jnp.float32)
    lanc = lanc_ref[...].astype(jnp.float32)
    slots = [(r, j) for r in row_slots(n) for j in range(per_chunk)]

    def rows(slot):
        r, j = slot
        band = order_ref[(me ^ r) * per_chunk + j]
        band = lax.rem(band + core * half, 2 * half)
        return held[pl.ds(band, 1), :] * lanc

    step = 2 * lanc.shape[0]
    for at in range(0, len(slots), 2):
        pair = jnp.concatenate([rows(slots[at]), rows(slots[at + 1])], axis=0)
        out_ref[at // 2 * step : (at // 2 + 1) * step, :] = pair.astype(jnp.bfloat16)


def matmul_kernel(p_ref, e_ref, o_ref):
    o_ref[...] = lax.dot_general(
        p_ref[...], e_ref[...], (((1,), (1,)), ((), ())), preferred_element_type=jnp.float32
    ).astype(o_ref.dtype)


def matmul_piece(products, eigvecs, first, rows, piece, dtype):
    depth = products.shape[1]
    unit = rows // 2
    return pl.pallas_call(
        matmul_kernel,
        grid=(1,),
        out_shape=jax.ShapeDtypeStruct((rows, TILE), dtype),
        in_specs=[
            pl.BlockSpec((pl.Element(rows), pl.Element(depth)), lambda i: (first, 0)),
            pl.BlockSpec((TILE, depth), lambda i: (piece, 0)),
        ],
        out_specs=pl.BlockSpec((rows, TILE), lambda i: (0, 0)),
        compiler_params=pltpu.CompilerParams(vmem_limit_bytes=VMEM_LIMIT),
        cost_estimate=pl.CostEstimate(
            flops=2 * rows * TILE * depth,
            bytes_accessed=2 * depth * (rows + TILE) + 4 * rows * TILE,
            transcendentals=0,
        ),
    )(products, eigvecs)


def per_device(n, eigvecs, lanczos, bands, band_order):
    lanc = lanczos.shape[0]
    per_chunk = band_order.shape[0] // n
    cols, depth = eigvecs.shape
    rows = band_order.shape[0] * lanc
    other = lax.ppermute(bands, "eig", [(0, 1), (1, 0)])
    total = rows + rows // 4
    products = pl.pallas_call(
        functools.partial(products_kernel, n, per_chunk),
        out_shape=jax.ShapeDtypeStruct((total, depth), jnp.bfloat16),
        in_specs=[pl.BlockSpec(memory_space=pltpu.SMEM)]
        + [pl.BlockSpec(memory_space=pltpu.VMEM)] * 3,
        out_specs=pl.BlockSpec(memory_space=pltpu.VMEM),
        scratch_shapes=[pltpu.VMEM((2 * bands.shape[0], depth), jnp.float32)],
        compiler_params=pltpu.CompilerParams(vmem_limit_bytes=VMEM_LIMIT),
    )(band_order, bands, other, lanczos)

    def exchange(value, bit):
        return lax.ppermute(value, "grid", [(i, i ^ (1 << bit)) for i in range(n)])

    half, quarter = rows // 2, rows // 4
    pieces = cols // TILE
    z_first = {1, 4} if pieces >= 6 else set()
    sent = []
    for p in range(pieces):
        if p in z_first:
            send = matmul_piece(products, eigvecs, quarter, half, p, jnp.bfloat16)
        else:
            send = matmul_piece(products, eigvecs, 0, half, p, jnp.bfloat16)
        sent.append(exchange(send, 1 if p in z_first else 0))
    kept = []
    for p in range(pieces):
        first = 3 * quarter if p in z_first else half
        kept.append(matmul_piece(products, eigvecs, first, half, p, jnp.float32))
    outs = []
    for p in range(pieces):
        top = kept[p][:quarter] + sent[p][quarter:].astype(jnp.float32)
        low = kept[p][quarter:] + sent[p][:quarter].astype(jnp.float32)
        keep, send = (top, low) if p in z_first else (low, top)
        got = exchange(send.astype(jnp.bfloat16), 0 if p in z_first else 1)
        value = keep + got.astype(jnp.float32)
        for bit in range(2, n.bit_length() - 1):
            mid = value.shape[0] // 2
            dtype = jnp.bfloat16 if bit < 3 else jnp.float32
            got = exchange(value[:mid].astype(dtype), bit)
            value = value[mid:] + got.astype(jnp.float32)
        outs.append(value)
    result = jnp.concatenate(outs, axis=1)
    return result.reshape(per_chunk, lanc, cols)


def solution(mesh):
    in_specs = (
        P("eig", ("rep", "grid")),
        P(None, ("rep", "grid")),
        P("eig", ("rep", "grid")),
        P("rep"),
    )
    out_specs = P(("rep", "grid"), None, "eig")
    return jax.shard_map(
        functools.partial(per_device, mesh.shape["grid"]),
        mesh=mesh,
        in_specs=in_specs,
        out_specs=out_specs,
        check_vma=False,
    )
```

```python
import functools

import jax
import jax.numpy as jnp
from jax import lax
from jax.experimental import pallas as pl
from jax.experimental.pallas import tpu as pltpu
from jax.sharding import PartitionSpec as P

TILE = 256
VMEM_LIMIT = 24 * 1024 * 1024


def ranked(bits, fixed):
    out = [fixed]
    for b in reversed(bits):
        out = [c | (1 << b) for c in out] + out
    return out


def project_kernel(
    n, per_chunk, sets, pieces, order_hbm, own_hbm, lanc_hbm, other_ref, eig_hbm, *rest
):
    outs = rest[: len(pieces)]
    order, own, lanc16, held, prod, eig, small_sem, eig_sem = rest[len(pieces) :]
    small = [
        pltpu.make_async_copy(src, dst, small_sem.at[i])
        for i, (src, dst) in enumerate(
            [(order_hbm, order), (own_hbm, own), (lanc_hbm, lanc16)]
        )
    ]
    for copy in small:
        copy.start()
    loads = []
    at = 0
    for i, (width, _) in enumerate(pieces):
        loads.append(
            pltpu.make_async_copy(
                eig_hbm.at[pl.ds(at, width)], eig.at[pl.ds(at, width)], eig_sem.at[i]
            )
        )
        loads[-1].start()
        at += width
    me = lax.axis_index("grid")
    core = lax.axis_index("eig")
    half = own.shape[0]
    held[half:, :] = other_ref[...].astype(jnp.float32)
    for copy in small:
        copy.wait()
    held[:half, :] = own[...].astype(jnp.float32)
    lanc = lanc16[...].astype(jnp.float32)
    rest_bits = list(range(2, n.bit_length() - 1))
    slots = [(r, j) for s in sets for r in ranked(rest_bits, s) for j in range(per_chunk)]

    def rows(slot):
        r, j = slot
        band = order[(me ^ r) * per_chunk + j]
        band = lax.rem(band + core * half, 2 * half)
        return held[pl.ds(band, 1), :] * lanc

    step = 2 * lanc.shape[0]
    for i in range(0, len(slots), 2):
        pair = jnp.concatenate([rows(slots[i]), rows(slots[i + 1])], axis=0)
        prod[i // 2 * step : (i // 2 + 1) * step, :] = pair.astype(jnp.bfloat16)

    quarter = prod.shape[0] // 3
    at = 0
    for i, (width, z_first) in enumerate(pieces):
        loads[i].wait()
        first = quarter if z_first else 0
        for col in range(0, width, TILE):
            size = min(TILE, width - col)
            outs[i][:, col : col + size] = lax.dot_general(
                prod[first : first + 2 * quarter, :],
                eig[at + col : at + col + size, :],
                (((1,), (1,)), ((), ())),
                preferred_element_type=jnp.float32,
            ).astype(outs[i].dtype)
        at += width


def project(n, sets, pieces, dtype, order, own, lanczos, other, eigvecs):
    lanc = lanczos.shape[0]
    per_chunk = order.shape[0] // n
    cols, depth = eigvecs.shape
    half = order.shape[0] * lanc // 2
    any_spec = pl.BlockSpec(memory_space=pl.ANY)
    vmem_spec = pl.BlockSpec(memory_space=pltpu.VMEM)
    return pl.pallas_call(
        functools.partial(project_kernel, n, per_chunk, sets, pieces),
        out_shape=[jax.ShapeDtypeStruct((half, w), dtype) for w, _ in pieces],
        in_specs=[any_spec, any_spec, any_spec, vmem_spec, any_spec],
        out_specs=[vmem_spec] * len(pieces),
        scratch_shapes=[
            pltpu.SMEM(order.shape, jnp.int32),
            pltpu.VMEM(own.shape, jnp.bfloat16),
            pltpu.VMEM(lanczos.shape, jnp.bfloat16),
            pltpu.VMEM((2 * own.shape[0], depth), jnp.float32),
            pltpu.VMEM((half // 2 * 3, depth), jnp.bfloat16),
            pltpu.VMEM((cols, depth), jnp.bfloat16),
            pltpu.SemaphoreType.DMA((3,)),
            pltpu.SemaphoreType.DMA((len(pieces),)),
        ],
        compiler_params=pltpu.CompilerParams(vmem_limit_bytes=VMEM_LIMIT),
        cost_estimate=pl.CostEstimate(
            flops=2 * half * cols * depth,
            bytes_accessed=2 * depth * cols + 4 * half * cols,
            transcendentals=0,
        ),
    )(order, own, lanczos, other, eigvecs)


def per_device(n, eigvecs, lanczos, bands, band_order):
    lanc = lanczos.shape[0]
    per_chunk = band_order.shape[0] // n
    cols = eigvecs.shape[0]
    quarter = band_order.shape[0] * lanc // 4
    unit = cols // 7 // 128 * 128
    pieces = [(2 * unit, False), (2 * unit, True), (2 * unit, False)]
    pieces.append((cols - 6 * unit, False))

    def exchange(value, bit):
        return lax.ppermute(value, "grid", [(i, i ^ (1 << bit)) for i in range(n)])

    other = lax.ppermute(bands, "eig", [(0, 1), (1, 0)])
    args = (band_order, bands, lanczos, other, eigvecs)
    send = project(n, (1, 3, 2), pieces, jnp.bfloat16, *args)
    got = [exchange(s, 1 if z else 0) for s, (_, z) in zip(send, pieces)]
    kept = project(n, (2, 0, 1), pieces, jnp.float32, *args)
    outs = []
    for p, (_, z_first) in enumerate(pieces):
        top = kept[p][:quarter] + got[p][quarter:].astype(jnp.float32)
        low = kept[p][quarter:] + got[p][:quarter].astype(jnp.float32)
        keep, leave = (top, low) if z_first else (low, top)
        came = exchange(leave.astype(jnp.bfloat16), 0 if z_first else 1)
        value = keep + came.astype(jnp.float32)
        for bit in range(2, n.bit_length() - 1):
            mid = value.shape[0] // 2
            dtype = jnp.bfloat16 if bit < 3 else jnp.float32
            came = exchange(value[:mid].astype(dtype), bit)
            value = value[mid:] + came.astype(jnp.float32)
        outs.append(value)
    result = jnp.concatenate(outs, axis=1)
    return result.reshape(per_chunk, lanc, cols)


def solution(mesh):
    in_specs = (
        P("eig", ("rep", "grid")),
        P(None, ("rep", "grid")),
        P("eig", ("rep", "grid")),
        P("rep"),
    )
    out_specs = P(("rep", "grid"), None, "eig")
    return jax.shard_map(
        functools.partial(per_device, mesh.shape["grid"]),
        mesh=mesh,
        in_specs=in_specs,
        out_specs=out_specs,
        check_vma=False,
    )
```

```python
import functools

import jax
import jax.numpy as jnp
from jax import lax
from jax.experimental import pallas as pl
from jax.experimental.pallas import tpu as pltpu
from jax.sharding import PartitionSpec as P

TILE = 256
VMEM_LIMIT = 32 * 1024 * 1024
PLAN = [(2, (0, 1, 2)), (1.5, (2, 0, 1)), (2, (1, 0, 2)), (1.5, (0, 1, 2))]


def ranked(bits, fixed=0):
    out = [fixed]
    for b in reversed(bits):
        out = [c | (1 << b) for c in out] + out
    return out


def split_columns(cols):
    unit = 128
    total = sum(share for share, _ in PLAN)
    ends, done = [], 0
    for share, _ in PLAN[:-1]:
        done += share
        ends.append(int(round(cols * done / total / unit)) * unit)
    ends.append(cols)
    return list(zip([0] + ends[:-1], ends))


def halves(bits):
    keep = ranked(bits[1:])
    return keep, [c | (1 << bits[0]) for c in keep]


def dot_into(out, prod, eig, classes, at, width):
    block = prod.shape[0] // 8
    rows = jnp.concatenate([prod[c * block : (c + 1) * block, :] for c in classes], axis=0)
    for col in range(0, width, TILE):
        size = min(TILE, width - col)
        out[:, col : col + size] = lax.dot_general(
            rows,
            eig[at + col : at + col + size, :],
            (((1,), (1,)), ((), ())),
            preferred_element_type=jnp.float32,
        ).astype(out.dtype)


def send_kernel(n, per_chunk, spans, order_hbm, own_hbm, lanc_hbm, other_ref, eig_hbm, *rest):
    count = len(spans)
    outs, (prod, eig) = rest[:count], rest[count : count + 2]
    order, own, lanc16, held, small_sem, eig_sem = rest[count + 2 :]
    small = [
        pltpu.make_async_copy(src, dst, small_sem.at[i])
        for i, (src, dst) in enumerate(
            [(order_hbm, order), (own_hbm, own), (lanc_hbm, lanc16)]
        )
    ]
    for copy in small:
        copy.start()
    loads = []
    for i, (at, end) in enumerate(spans):
        part = pl.ds(at, end - at)
        loads.append(pltpu.make_async_copy(eig_hbm.at[part], eig.at[part], eig_sem.at[i]))
        loads[-1].start()
    me = lax.axis_index("grid")
    core = lax.axis_index("eig")
    half = own.shape[0]
    held[half:, :] = other_ref[...].astype(jnp.float32)
    for copy in small:
        copy.wait()
    held[:half, :] = own[...].astype(jnp.float32)
    lanc = lanc16[...].astype(jnp.float32)
    rest_bits = list(range(3, n.bit_length() - 1))

    def row_group(r, j):
        band = order[(me ^ r) * per_chunk + j]
        band = lax.rem(band + core * half, 2 * half)
        return held[pl.ds(band, 1), :] * lanc

    block = prod.shape[0] // 8
    step = 2 * lanc.shape[0]

    def make_class(c):
        slots = [(r, j) for r in ranked(rest_bits, c) for j in range(per_chunk)]
        for i in range(0, len(slots), 2):
            pair = jnp.concatenate([row_group(*slots[i]), row_group(*slots[i + 1])], axis=0)
            first = c * block + i // 2 * step
            prod[first : first + step, :] = pair.astype(jnp.bfloat16)

    made = set()
    for i, (at, end) in enumerate(spans):
        leave = halves(PLAN[i][1])[1]
        for c in leave:
            if c not in made:
                make_class(c)
                made.add(c)
        loads[i].wait()
        dot_into(outs[i], prod, eig, leave, at, end - at)
    for c in set(range(8)) - made:
        make_class(c)


def keep_kernel(classes, at, width, prod, eig, out):
    dot_into(out, prod, eig, classes, at, width)


VMEM_SPEC = pl.BlockSpec(memory_space=pltpu.VMEM)
PARAMS = pltpu.CompilerParams(vmem_limit_bytes=VMEM_LIMIT)


def cost(rows, cols, depth):
    return pl.CostEstimate(
        flops=2 * rows * cols * depth,
        bytes_accessed=2 * depth * (cols + rows) + 4 * rows * cols,
        transcendentals=0,
    )


def send_half(n, spans, order, own, lanczos, other, eigvecs):
    lanc = lanczos.shape[0]
    cols, depth = eigvecs.shape
    rows = order.shape[0] * lanc
    hbm = pl.BlockSpec(memory_space=pltpu.HBM)
    order, own, lanczos, eigvecs = (
        pltpu.with_memory_space_constraint(x, pltpu.HBM) for x in (order, own, lanczos, eigvecs)
    )
    shapes = [jax.ShapeDtypeStruct((rows // 2, end - at), jnp.bfloat16) for at, end in spans]
    shapes.append(jax.ShapeDtypeStruct((rows, depth), jnp.bfloat16))
    shapes.append(jax.ShapeDtypeStruct((cols, depth), jnp.bfloat16))
    return pl.pallas_call(
        functools.partial(send_kernel, n, order.shape[0] // n, spans),
        out_shape=shapes,
        in_specs=[hbm, hbm, hbm, VMEM_SPEC, hbm],
        out_specs=[VMEM_SPEC] * len(shapes),
        scratch_shapes=[
            pltpu.SMEM(order.shape, jnp.int32),
            pltpu.VMEM(own.shape, jnp.bfloat16),
            pltpu.VMEM(lanczos.shape, jnp.bfloat16),
            pltpu.VMEM((2 * own.shape[0], depth), jnp.float32),
            pltpu.SemaphoreType.DMA((3,)),
            pltpu.SemaphoreType.DMA((len(spans),)),
        ],
        compiler_params=PARAMS,
        cost_estimate=cost(rows // 2, cols, depth),
    )(order, own, lanczos, other, eigvecs)


def keep_half(classes, span, prod, eig):
    at, end = span
    rows, depth = prod.shape
    return pl.pallas_call(
        functools.partial(keep_kernel, classes, at, end - at),
        out_shape=jax.ShapeDtypeStruct((rows // 2, end - at), jnp.float32),
        in_specs=[VMEM_SPEC, VMEM_SPEC],
        out_specs=VMEM_SPEC,
        compiler_params=PARAMS,
        cost_estimate=cost(rows // 2, end - at, depth),
    )(prod, eig)


def per_device(n, eigvecs, lanczos, bands, band_order):
    cols = eigvecs.shape[0]
    spans = split_columns(cols)

    def exchange(value, bit):
        return lax.ppermute(value, "grid", [(i, i ^ (1 << bit)) for i in range(n)])

    other = lax.ppermute(bands, "eig", [(0, 1), (1, 0)])
    *send, prod, eig = send_half(n, spans, band_order, bands, lanczos, other, eigvecs)
    got = [exchange(s, bits[0]) for s, (_, bits) in zip(send, PLAN)]
    outs = []
    for p, (_, bits) in enumerate(PLAN):
        kept = keep_half(halves(bits)[0], spans[p], prod, eig)
        value = kept + got[p].astype(jnp.float32)
        for stage, bit in enumerate(list(bits[1:]) + list(range(3, n.bit_length() - 1))):
            mid = value.shape[0] // 2
            dtype = jnp.bfloat16 if stage < 2 else jnp.float32
            came = exchange(value[:mid].astype(dtype), bit)
            value = value[mid:] + came.astype(jnp.float32)
        outs.append(value)
    result = jnp.concatenate(outs, axis=1)
    return result.reshape(band_order.shape[0] // n, lanczos.shape[0], cols)


def solution(mesh):
    in_specs = (
        P("eig", ("rep", "grid")),
        P(None, ("rep", "grid")),
        P("eig", ("rep", "grid")),
        P("rep"),
    )
    out_specs = P(("rep", "grid"), None, "eig")
    return jax.shard_map(
        functools.partial(per_device, mesh.shape["grid"]),
        mesh=mesh,
        in_specs=in_specs,
        out_specs=out_specs,
        check_vma=False,
    )
```

```python
import functools

import jax
import jax.numpy as jnp
from jax import lax
from jax.experimental import pallas as pl
from jax.experimental.pallas import tpu as pltpu
from jax.sharding import PartitionSpec as P

TILE = 256
VMEM_LIMIT = 32 * 1024 * 1024
PLAN = [(1.5, (0, 1, 2)), (2, (1, 0, 2)), (2, (0, 1, 2)), (1.5, (0, 1, 2))]


def ranked(bits, fixed=0):
    out = [fixed]
    for b in reversed(bits):
        out = [c | (1 << b) for c in out] + out
    return out


def split_columns(cols):
    unit = 128
    total = sum(share for share, _ in PLAN)
    ends, done = [], 0
    for share, _ in PLAN[:-1]:
        done += share
        ends.append(int(round(cols * done / total / unit)) * unit)
    ends.append(cols)
    return list(zip([0] + ends[:-1], ends))


def halves(bits):
    keep = ranked(bits[1:])
    return keep, [c | (1 << bits[0]) for c in keep]


def dot_into(out, prod, eig, classes):
    block = prod.shape[0] // 8
    rows = jnp.concatenate([prod[c * block : (c + 1) * block, :] for c in classes], axis=0)
    width = eig.shape[0]
    for col in range(0, width, TILE):
        size = min(TILE, width - col)
        out[:, col : col + size] = lax.dot_general(
            rows,
            eig[col : col + size, :],
            (((1,), (1,)), ((), ())),
            preferred_element_type=jnp.float32,
        ).astype(out.dtype)


def setup_kernel(n, per_chunk, lanc, span, order_hbm, own_hbm, lanc_hbm, eig_hbm, *rest):
    pick, own, lanc16, eig, order, sem = rest
    copies = [
        pltpu.make_async_copy(src, dst, sem.at[i])
        for i, (src, dst) in enumerate(
            [
                (order_hbm, order),
                (own_hbm, own),
                (lanc_hbm, lanc16),
                (eig_hbm.at[pl.ds(span[0], span[1] - span[0])], eig),
            ]
        )
    ]
    for copy in copies:
        copy.start()
    me = lax.axis_index("grid")
    core = lax.axis_index("eig")
    bands = pick.shape[1]
    rest_bits = list(range(3, n.bit_length() - 1))
    slots = [(r, j) for c in range(8) for r in ranked(rest_bits, c) for j in range(per_chunk)]
    col = lax.broadcasted_iota(jnp.int32, (2 * lanc, bands), 1)
    upper = lax.broadcasted_iota(jnp.int32, (2 * lanc, bands), 0) < lanc
    copies[0].wait()
    for i in range(0, len(slots), 2):
        want = []
        for r, j in slots[i : i + 2]:
            band = order[(me ^ r) * per_chunk + j]
            want.append(lax.rem(band + core * (bands // 2), bands))
        hit = col == jnp.where(upper, want[0], want[1])
        pick[i * lanc : (i + 2) * lanc, :] = hit.astype(jnp.float32).astype(jnp.bfloat16)
    for copy in copies[1:]:
        copy.wait()


def first_kernel(bits, span, pick, own, other, lanc16, eig, eig_hbm, out, prod, eig_next, sem):
    load = pltpu.make_async_copy(
        eig_hbm.at[pl.ds(span[0], span[1] - span[0])], eig_next, sem.at[0]
    )
    load.start()
    half = own.shape[0]
    lanc = lanc16[...].astype(jnp.float32)
    block = prod.shape[0] // 8
    groups = block // lanc.shape[0]
    bands = jnp.concatenate([own[...], other[...]], axis=0)

    def make_classes(classes):
        for c in classes:
            chosen = lax.dot_general(
                pick[c * block : (c + 1) * block, :],
                bands,
                (((1,), (0,)), ((), ())),
                preferred_element_type=jnp.float32,
            )
            value = chosen.reshape(groups, lanc.shape[0], lanc.shape[1]) * lanc[None]
            prod[c * block : (c + 1) * block, :] = value.reshape(chosen.shape).astype(
                jnp.bfloat16
            )

    keep, leave = halves(bits)
    make_classes(leave)
    dot_into(out, prod, eig, leave)
    make_classes(keep)
    load.wait()


def send_kernel(plan, spans, prod, eig, eig_hbm, *rest):
    count = len(plan)
    outs, later, sem = rest[:count], rest[count:-1], rest[-1]
    loads = [
        pltpu.make_async_copy(eig_hbm.at[pl.ds(at, end - at)], ref, sem.at[i])
        for i, ((at, end), ref) in enumerate(zip(spans[1:], later))
    ]
    for load in loads:
        load.start()
    for i, bits in enumerate(plan):
        if i > 0:
            loads[i - 1].wait()
        dot_into(outs[i], prod, later[i - 1] if i > 0 else eig, halves(bits)[1])


def keep_kernel(classes, prod, eig, out):
    dot_into(out, prod, eig, classes)


VMEM_SPEC = pl.BlockSpec(memory_space=pltpu.VMEM)
HBM_SPEC = pl.BlockSpec(memory_space=pltpu.HBM)


def kernel_call(body, ins, outs, scratch, cost):
    flops, moved = cost
    return pl.pallas_call(
        body,
        out_shape=[jax.ShapeDtypeStruct(*out) for out in outs],
        in_specs=[HBM_SPEC if far else VMEM_SPEC for _, far in ins],
        out_specs=[VMEM_SPEC] * len(outs),
        scratch_shapes=scratch,
        compiler_params=pltpu.CompilerParams(vmem_limit_bytes=VMEM_LIMIT),
        cost_estimate=pl.CostEstimate(flops=flops, bytes_accessed=moved, transcendentals=0),
    )(
        *(
            pltpu.with_memory_space_constraint(x, pltpu.HBM) if far else x
            for x, far in ins
        )
    )


def per_device(n, eigvecs, lanczos, bands, band_order):
    cols, depth = eigvecs.shape
    lanc = lanczos.shape[0]
    per_chunk = band_order.shape[0] // n
    rows = band_order.shape[0] * lanc
    spans = split_columns(cols)
    widths = [end - at for at, end in spans]
    orders = [bits for _, bits in PLAN]
    bf16 = jnp.bfloat16

    def exchange(value, bit):
        return lax.ppermute(value, "grid", [(i, i ^ (1 << bit)) for i in range(n)])

    def flops(width):
        return rows * width * depth

    other = lax.ppermute(bands, "eig", [(0, 1), (1, 0)])
    pick, own, lanc16, eig = kernel_call(
        functools.partial(setup_kernel, n, per_chunk, lanc, spans[0]),
        [(band_order, True), (bands, True), (lanczos, True), (eigvecs, True)],
        [
            ((rows, 2 * bands.shape[0]), bf16),
            (bands.shape, bf16),
            (lanczos.shape, bf16),
            ((widths[0], depth), bf16),
        ],
        [pltpu.SMEM(band_order.shape, jnp.int32), pltpu.SemaphoreType.DMA((4,))],
        (0, 2 * widths[0] * depth),
    )
    eigs = [eig]
    send, prod, eig = kernel_call(
        functools.partial(first_kernel, orders[0], spans[1]),
        [(pick, False), (own, False), (other, False), (lanc16, False), (eig, False)]
        + [(eigvecs, True)],
        [((rows // 2, widths[0]), bf16), ((rows, depth), bf16), ((widths[1], depth), bf16)],
        [pltpu.SemaphoreType.DMA((1,))],
        (flops(widths[0]), 2 * widths[1] * depth),
    )
    eigs.append(eig)
    sends = [send]
    more = kernel_call(
        functools.partial(send_kernel, orders[1:], spans[1:]),
        [(prod, False), (eig, False), (eigvecs, True)],
        [((rows // 2, w), bf16) for w in widths[1:]] + [((w, depth), bf16) for w in widths[2:]],
        [pltpu.SemaphoreType.DMA((len(PLAN) - 2,))],
        (flops(sum(widths[1:])), 2 * sum(widths[2:]) * depth),
    )
    sends += more[: len(PLAN) - 1]
    eigs += more[len(PLAN) - 1 :]
    got = [exchange(s, bits[0]) for s, bits in zip(sends, orders)]
    outs = []
    for p, bits in enumerate(orders):
        (kept,) = kernel_call(
            functools.partial(keep_kernel, halves(bits)[0]),
            [(prod, False), (eigs[p], False)],
            [((rows // 2, widths[p]), jnp.float32)],
            [],
            (flops(widths[p]), 2 * widths[p] * depth),
        )
        value = kept + got[p].astype(jnp.float32)
        for stage, bit in enumerate(list(bits[1:]) + list(range(3, n.bit_length() - 1))):
            mid = value.shape[0] // 2
            dtype = bf16 if stage < 2 else jnp.float32
            came = exchange(value[:mid].astype(dtype), bit)
            value = value[mid:] + came.astype(jnp.float32)
        outs.append(value)
    result = jnp.concatenate(outs, axis=1)
    return result.reshape(per_chunk, lanc, cols)


def solution(mesh):
    in_specs = (
        P("eig", ("rep", "grid")),
        P(None, ("rep", "grid")),
        P("eig", ("rep", "grid")),
        P("rep"),
    )
    out_specs = P(("rep", "grid"), None, "eig")
    return jax.shard_map(
        functools.partial(per_device, mesh.shape["grid"]),
        mesh=mesh,
        in_specs=in_specs,
        out_specs=out_specs,
        check_vma=False,
    )
```

```python
import functools

import jax
import jax.numpy as jnp
from jax import lax
from jax.experimental import pallas as pl
from jax.experimental.pallas import tpu as pltpu
from jax.sharding import PartitionSpec as P

TILE = 256
VMEM_LIMIT = 32 * 1024 * 1024
PLAN = [1.5, 2, 2, 1.5]


def split_columns(cols):
    unit = 128
    ends, done = [], 0
    for share in PLAN[:-1]:
        done += share
        ends.append(int(round(cols * done / sum(PLAN) / unit)) * unit)
    ends.append(cols)
    return list(zip([0] + ends[:-1], ends))


def dot_into(out, prod, eig, first):
    rows = prod[first : first + out.shape[0], :]
    width = eig.shape[0]
    for col in range(0, width, TILE):
        size = min(TILE, width - col)
        out[:, col : col + size] = lax.dot_general(
            rows,
            eig[col : col + size, :],
            (((1,), (1,)), ((), ())),
            preferred_element_type=jnp.float32,
        ).astype(out.dtype)


def setup_kernel(n, per_chunk, lanc, span, order_hbm, own_hbm, lanc_hbm, eig_hbm, *rest):
    pick, own, lanc16, eig, order, sem = rest
    copies = [
        pltpu.make_async_copy(src, dst, sem.at[i])
        for i, (src, dst) in enumerate(
            [
                (order_hbm, order),
                (own_hbm, own),
                (lanc_hbm, lanc16),
                (eig_hbm.at[pl.ds(span[0], span[1] - span[0])], eig),
            ]
        )
    ]
    for copy in copies:
        copy.start()
    me = lax.axis_index("grid")
    core = lax.axis_index("eig")
    bands = pick.shape[1]
    slots = [(r, j) for half in (1, 0) for r in range(half, n, 2) for j in range(per_chunk)]
    col = lax.broadcasted_iota(jnp.int32, (2 * lanc, bands), 1)
    upper = lax.broadcasted_iota(jnp.int32, (2 * lanc, bands), 0) < lanc
    copies[0].wait()
    for i in range(0, len(slots), 2):
        want = []
        for r, j in slots[i : i + 2]:
            band = order[((me & 1) ^ r) * per_chunk + j]
            want.append(lax.rem(band + core * (bands // 2), bands))
        hit = col == jnp.where(upper, want[0], want[1])
        pick[i * lanc : (i + 2) * lanc, :] = hit.astype(jnp.float32).astype(jnp.bfloat16)
    for copy in copies[1:]:
        copy.wait()


def first_kernel(span, pick, own, other, lanc16, eig, eig_hbm, out, prod, eig_next, sem):
    load = pltpu.make_async_copy(
        eig_hbm.at[pl.ds(span[0], span[1] - span[0])], eig_next, sem.at[0]
    )
    load.start()
    half = own.shape[0]
    lanc = lanc16[...].astype(jnp.float32)
    block = prod.shape[0] // 2
    groups = block // lanc.shape[0]
    bands = jnp.concatenate([own[...], other[...]], axis=0)

    def make_rows(first):
        chosen = lax.dot_general(
            pick[first : first + block, :],
            bands,
            (((1,), (0,)), ((), ())),
            preferred_element_type=jnp.float32,
        )
        value = chosen.reshape(groups, lanc.shape[0], lanc.shape[1]) * lanc[None]
        prod[first : first + block, :] = value.reshape(chosen.shape).astype(jnp.bfloat16)

    make_rows(0)
    dot_into(out, prod, eig, 0)
    make_rows(block)
    load.wait()


def send_kernel(spans, prod, eig, eig_hbm, *rest):
    count = len(spans)
    outs, later, sem = rest[:count], rest[count:-1], rest[-1]
    loads = [
        pltpu.make_async_copy(eig_hbm.at[pl.ds(at, end - at)], ref, sem.at[i])
        for i, ((at, end), ref) in enumerate(zip(spans[1:], later))
    ]
    for load in loads:
        load.start()
    for i in range(count):
        if i > 0:
            loads[i - 1].wait()
        dot_into(outs[i], prod, later[i - 1] if i > 0 else eig, 0)


def keep_kernel(prod, eig, out):
    dot_into(out, prod, eig, out.shape[0])


def finish_kernel(spans, *refs):
    came, out = refs[:-1], refs[-1]
    rows = out.shape[0]
    for (at, end), ref in zip(spans, came):
        total = ref[:rows, :].astype(jnp.float32)
        for i in range(1, ref.shape[0] // rows):
            total += ref[i * rows : (i + 1) * rows, :].astype(jnp.float32)
        out[:, at:end] = total


VMEM_SPEC = pl.BlockSpec(memory_space=pltpu.VMEM)
HBM_SPEC = pl.BlockSpec(memory_space=pltpu.HBM)


def kernel_call(body, ins, outs, scratch, cost):
    flops, moved = cost
    return pl.pallas_call(
        body,
        out_shape=[jax.ShapeDtypeStruct(*out) for out in outs],
        in_specs=[HBM_SPEC if far else VMEM_SPEC for _, far in ins],
        out_specs=[VMEM_SPEC] * len(outs),
        scratch_shapes=scratch,
        compiler_params=pltpu.CompilerParams(vmem_limit_bytes=VMEM_LIMIT),
        cost_estimate=pl.CostEstimate(flops=flops, bytes_accessed=moved, transcendentals=0),
    )(
        *(
            pltpu.with_memory_space_constraint(x, pltpu.HBM) if far else x
            for x, far in ins
        )
    )


def per_device(n, eigvecs, lanczos, bands, band_order):
    cols, depth = eigvecs.shape
    lanc = lanczos.shape[0]
    per_chunk = band_order.shape[0] // n
    rows = band_order.shape[0] * lanc
    spans = split_columns(cols)
    widths = [end - at for at, end in spans]
    lines = [list(range(first, n, 2)) for first in (0, 1)]
    bf16 = jnp.bfloat16

    def exchange(value):
        return lax.ppermute(value, "grid", [(i, i ^ 1) for i in range(n)])

    def spread(value):
        return lax.all_to_all(value, "grid", 0, 0, axis_index_groups=lines, tiled=True)

    def flops(width):
        return rows * width * depth

    other = lax.ppermute(bands, "eig", [(0, 1), (1, 0)])
    pick, own, lanc16, eig = kernel_call(
        functools.partial(setup_kernel, n, per_chunk, lanc, spans[0]),
        [(band_order, True), (bands, True), (lanczos, True), (eigvecs, True)],
        [
            ((rows, 2 * bands.shape[0]), bf16),
            (bands.shape, bf16),
            (lanczos.shape, bf16),
            ((widths[0], depth), bf16),
        ],
        [pltpu.SMEM(band_order.shape, jnp.int32), pltpu.SemaphoreType.DMA((4,))],
        (0, 2 * widths[0] * depth),
    )
    eigs = [eig]
    send, prod, eig = kernel_call(
        functools.partial(first_kernel, spans[1]),
        [(pick, False), (own, False), (other, False), (lanc16, False), (eig, False)]
        + [(eigvecs, True)],
        [((rows // 2, widths[0]), bf16), ((rows, depth), bf16), ((widths[1], depth), bf16)],
        [pltpu.SemaphoreType.DMA((1,))],
        (flops(widths[0]), 2 * widths[1] * depth),
    )
    eigs.append(eig)
    sends = [send]
    more = kernel_call(
        functools.partial(send_kernel, spans[1:]),
        [(prod, False), (eig, False), (eigvecs, True)],
        [((rows // 2, w), bf16) for w in widths[1:]] + [((w, depth), bf16) for w in widths[2:]],
        [pltpu.SemaphoreType.DMA((len(PLAN) - 2,))],
        (flops(sum(widths[1:])), 2 * sum(widths[2:]) * depth),
    )
    sends += more[: len(PLAN) - 1]
    eigs += more[len(PLAN) - 1 :]
    got = [exchange(s) for s in sends]
    came = []
    for p, width in enumerate(widths):
        (kept,) = kernel_call(
            keep_kernel,
            [(prod, False), (eigs[p], False)],
            [((rows // 2, width), jnp.float32)],
            [],
            (flops(width), 2 * width * depth),
        )
        came.append(spread((kept + got[p].astype(jnp.float32)).astype(bf16)))
    (result,) = kernel_call(
        functools.partial(finish_kernel, spans),
        [(c, False) for c in came],
        [((rows // n, cols), jnp.float32)],
        [],
        (rows * cols // 2, (rows + 4 * rows // n) * cols),
    )
    return result.reshape(per_chunk, lanc, cols)


def solution(mesh):
    in_specs = (
        P("eig", ("rep", "grid")),
        P(None, ("rep", "grid")),
        P("eig", ("rep", "grid")),
        P("rep"),
    )
    out_specs = P(("rep", "grid"), None, "eig")
    return jax.shard_map(
        functools.partial(per_device, mesh.shape["grid"]),
        mesh=mesh,
        in_specs=in_specs,
        out_specs=out_specs,
        check_vma=False,
    )
```

```python
import functools

import jax
import jax.numpy as jnp
from jax import lax
from jax.experimental import pallas as pl
from jax.experimental.pallas import tpu as pltpu
from jax.sharding import PartitionSpec as P

TILE = 256
VMEM_LIMIT = 32 * 1024 * 1024
WAYS = ((1, 0, 2), (0, 2, 1))
PLAN = [(3.5, (0, 1, 2)), (2, (1, 0, 2)), (1.5, (0, 1, 2))]


def ranked(bits, fixed=0):
    out = [fixed]
    for b in reversed(bits):
        out = [c | (1 << b) for c in out] + out
    return out


def split_columns(cols):
    unit = 128
    total = sum(share for share, _ in PLAN)
    ends, done = [], 0
    for share, _ in PLAN[:-1]:
        done += share
        ends.append(int(round(cols * done / total / unit)) * unit)
    ends.append(cols)
    return list(zip([0] + ends[:-1], ends))


def halves(bits):
    keep = ranked(bits[1:])
    return keep, [c | (1 << bits[0]) for c in keep]


def grid_offset(c, core):
    return sum(((c >> s) & 1) << bit for s, bit in enumerate(WAYS[core])) + (c >> 3 << 3)


def dot_into(out, prod, eig, classes):
    block = prod.shape[0] // 8
    rows = jnp.concatenate([prod[c * block : (c + 1) * block, :] for c in classes], axis=0)
    width = eig.shape[0]
    for col in range(0, width, TILE):
        size = min(TILE, width - col)
        out[:, col : col + size] = lax.dot_general(
            rows,
            eig[col : col + size, :],
            (((1,), (1,)), ((), ())),
            preferred_element_type=jnp.float32,
        ).astype(out.dtype)


def setup_kernel(n, per_chunk, lanc, span, order_hbm, own_hbm, lanc_hbm, eig_hbm, *rest):
    pick, own, lanc16, eig, order, sem = rest
    copies = [
        pltpu.make_async_copy(src, dst, sem.at[i])
        for i, (src, dst) in enumerate(
            [
                (order_hbm, order),
                (own_hbm, own),
                (lanc_hbm, lanc16),
                (eig_hbm.at[pl.ds(span[0], span[1] - span[0])], eig),
            ]
        )
    ]
    for copy in copies:
        copy.start()
    me = lax.axis_index("grid")
    core = lax.axis_index("eig")
    bands = pick.shape[1]
    rest_bits = list(range(3, n.bit_length() - 1))
    slots = [(r, j) for c in range(8) for r in ranked(rest_bits, c) for j in range(per_chunk)]
    col = lax.broadcasted_iota(jnp.int32, (2 * lanc, bands), 1)
    upper = lax.broadcasted_iota(jnp.int32, (2 * lanc, bands), 0) < lanc
    copies[0].wait()
    for i in range(0, len(slots), 2):
        want = []
        for r, j in slots[i : i + 2]:
            offset = jnp.where(core == 0, grid_offset(r, 0), grid_offset(r, 1))
            band = order[(me ^ offset) * per_chunk + j]
            want.append(lax.rem(band + core * (bands // 2), bands))
        hit = col == jnp.where(upper, want[0], want[1])
        pick[i * lanc : (i + 2) * lanc, :] = hit.astype(jnp.float32).astype(jnp.bfloat16)
    for copy in copies[1:]:
        copy.wait()


def first_kernel(bits, span, pick, own, other, lanc16, eig, eig_hbm, out, prod, eig_next, sem):
    load = pltpu.make_async_copy(
        eig_hbm.at[pl.ds(span[0], span[1] - span[0])], eig_next, sem.at[0]
    )
    load.start()
    half = own.shape[0]
    lanc = lanc16[...].astype(jnp.float32)
    block = prod.shape[0] // 8
    groups = block // lanc.shape[0]
    bands = jnp.concatenate([own[...], other[...]], axis=0)

    def make_classes(classes):
        for c in classes:
            chosen = lax.dot_general(
                pick[c * block : (c + 1) * block, :],
                bands,
                (((1,), (0,)), ((), ())),
                preferred_element_type=jnp.float32,
            )
            value = chosen.reshape(groups, lanc.shape[0], lanc.shape[1]) * lanc[None]
            prod[c * block : (c + 1) * block, :] = value.reshape(chosen.shape).astype(
                jnp.bfloat16
            )

    keep, leave = halves(bits)
    make_classes(leave)
    dot_into(out, prod, eig, leave)
    make_classes(keep)
    load.wait()


def send_kernel(plan, spans, prod, eig, eig_hbm, *rest):
    count = len(plan)
    outs, later, sem = rest[:count], rest[count:-1], rest[-1]
    loads = [
        pltpu.make_async_copy(eig_hbm.at[pl.ds(at, end - at)], ref, sem.at[i])
        for i, ((at, end), ref) in enumerate(zip(spans[1:], later))
    ]
    for load in loads:
        load.start()
    for i, bits in enumerate(plan):
        if i > 0:
            loads[i - 1].wait()
        dot_into(outs[i], prod, later[i - 1] if i > 0 else eig, halves(bits)[1])


def keep_kernel(classes, prod, eig, out):
    dot_into(out, prod, eig, classes)


def add_kernel(kept, got, _, leave, keep):
    mid = leave.shape[0]
    leave[...] = (kept[:mid, :] + got[:mid, :].astype(jnp.float32)).astype(leave.dtype)
    keep[...] = kept[mid:, :] + got[mid:, :].astype(jnp.float32)


def finish_kernel(spans, *refs):
    count = len(spans)
    kept, came, out = refs[:count], refs[count : 2 * count], refs[-1]
    for (at, end), a, b in zip(spans, kept, came):
        out[:, at:end] = a[a.shape[0] - out.shape[0] :, :] + b[...].astype(jnp.float32)


VMEM_SPEC = pl.BlockSpec(memory_space=pltpu.VMEM)
SPECS = {
    True: pl.BlockSpec(memory_space=pltpu.HBM),
    False: VMEM_SPEC,
    None: pl.BlockSpec(memory_space=pl.ANY),
}


def kernel_call(body, ins, outs, scratch, cost):
    flops, moved = cost
    return pl.pallas_call(
        body,
        out_shape=[jax.ShapeDtypeStruct(*out) for out in outs],
        in_specs=[SPECS[far] for _, far in ins],
        out_specs=[VMEM_SPEC] * len(outs),
        scratch_shapes=scratch,
        compiler_params=pltpu.CompilerParams(vmem_limit_bytes=VMEM_LIMIT),
        cost_estimate=pl.CostEstimate(flops=flops, bytes_accessed=moved, transcendentals=0),
    )(
        *(
            pltpu.with_memory_space_constraint(x, pltpu.HBM) if far else x
            for x, far in ins
        )
    )


def per_device(n, eigvecs, lanczos, bands, band_order):
    cols, depth = eigvecs.shape
    lanc = lanczos.shape[0]
    per_chunk = band_order.shape[0] // n
    rows = band_order.shape[0] * lanc
    spans = split_columns(cols)
    widths = [end - at for at, end in spans]
    orders = [bits for _, bits in PLAN]
    bf16 = jnp.bfloat16

    def exchange(value, stage):
        pairs = []
        for i in range(n):
            for core in range(2):
                bit = WAYS[core][stage] if stage < 3 else stage
                pairs.append((2 * i + core, 2 * (i ^ (1 << bit)) + core))
        return lax.ppermute(value, ("grid", "eig"), pairs)

    def flops(width):
        return rows * width * depth

    other = lax.ppermute(bands, "eig", [(0, 1), (1, 0)])
    pick, own, lanc16, eig = kernel_call(
        functools.partial(setup_kernel, n, per_chunk, lanc, spans[0]),
        [(band_order, True), (bands, True), (lanczos, True), (eigvecs, True)],
        [
            ((rows, 2 * bands.shape[0]), bf16),
            (bands.shape, bf16),
            (lanczos.shape, bf16),
            ((widths[0], depth), bf16),
        ],
        [pltpu.SMEM(band_order.shape, jnp.int32), pltpu.SemaphoreType.DMA((4,))],
        (0, 2 * widths[0] * depth),
    )
    eigs = [eig]
    send, prod, eig = kernel_call(
        functools.partial(first_kernel, orders[0], spans[1]),
        [(pick, False), (own, False), (other, False), (lanc16, False), (eig, False)]
        + [(eigvecs, True)],
        [((rows // 2, widths[0]), bf16), ((rows, depth), bf16), ((widths[1], depth), bf16)],
        [pltpu.SemaphoreType.DMA((1,))],
        (flops(widths[0]), 2 * widths[1] * depth),
    )
    eigs.append(eig)
    sends = [send]
    more = kernel_call(
        functools.partial(send_kernel, orders[1:], spans[1:]),
        [(prod, False), (eig, False), (eigvecs, True)],
        [((rows // 2, w), bf16) for w in widths[1:]] + [((w, depth), bf16) for w in widths[2:]],
        [pltpu.SemaphoreType.DMA((len(PLAN) - 2,))],
        (flops(sum(widths[1:])), 2 * sum(widths[2:]) * depth),
    )
    sends += more[: len(PLAN) - 1]
    eigs += more[len(PLAN) - 1 :]
    got = [exchange(s, bits[0]) for s, bits in zip(sends, orders)]
    value = []
    for p, bits in enumerate(orders):
        value += kernel_call(
            functools.partial(keep_kernel, halves(bits)[0]),
            [(prod, False), (eigs[p], False)],
            [((rows // 2, widths[p]), jnp.float32)],
            [],
            (flops(widths[p]), 2 * widths[p] * depth),
        )
    later = range(3, n.bit_length() - 1)
    token = prod
    for stage in range(1, 3 + len(later)):
        for p, bits in enumerate(orders):
            half = value[p].shape[0] // 2
            size = half * widths[p]
            leave, value[p] = kernel_call(
                add_kernel,
                [(value[p], False), (got[p], False), (token, None)],
                [((half, widths[p]), bf16 if stage < 3 else jnp.float32)]
                + [((half, widths[p]), jnp.float32)],
                [],
                (2 * size, 18 * size),
            )
            token = leave
            got[p] = exchange(leave, (*bits, *later)[stage])
    outs = list(zip(value, got))
    (result,) = kernel_call(
        functools.partial(finish_kernel, spans),
        [(value, False) for value, _ in outs] + [(came, False) for _, came in outs],
        [((rows // n, cols), jnp.float32)],
        [],
        (rows // n * cols, 12 * rows // n * cols),
    )
    return result.reshape(per_chunk, lanc, cols)


def solution(mesh):
    in_specs = (
        P("eig", ("rep", "grid")),
        P(None, ("rep", "grid")),
        P("eig", ("rep", "grid")),
        P("rep"),
    )
    out_specs = P(("rep", "grid"), None, "eig")
    return jax.shard_map(
        functools.partial(per_device, mesh.shape["grid"]),
        mesh=mesh,
        in_specs=in_specs,
        out_specs=out_specs,
        check_vma=False,
    )
```

```python
import functools

import jax
import jax.numpy as jnp
from jax import lax
from jax.experimental import pallas as pl
from jax.experimental.pallas import tpu as pltpu
from jax.sharding import PartitionSpec as P

TILE = 256
VMEM_LIMIT = 32 * 1024 * 1024
WAYS = ((0, 1, 2), (1, 2, 0))
PLAN = [(3, (0, 2, 1)), (2, (2, 0, 1)), (2, (0, 1, 2))]
ORDER = [(piece, stage) for stage in range(3) for piece in range(len(PLAN))]


def ranked(bits, fixed=0):
    out = [fixed]
    for b in reversed(bits):
        out = [c | (1 << b) for c in out] + out
    return out


def split_columns(cols):
    unit = 128
    total = sum(share for share, _ in PLAN)
    ends, done = [], 0
    for share, _ in PLAN[:-1]:
        done += share
        ends.append(int(round(cols * done / total / unit)) * unit)
    ends.append(cols)
    return list(zip([0] + ends[:-1], ends))


def halves(bits):
    keep = ranked(bits[1:])
    return keep, [c | (1 << bits[0]) for c in keep]


def grid_offset(c, core):
    return sum(((c >> s) & 1) << bit for s, bit in enumerate(WAYS[core])) + (c >> 3 << 3)


def tiles_of(spans, p):
    at, end = spans[p]
    head = min(TILE, end - at)
    before = end_of_rest(spans, p - 1) if p else 0
    tiles = [(p, before, head, 0)]
    for col in range(head, end - at, TILE):
        tiles.append((p + 1, col - head, min(TILE, end - at - col), col))
    return tiles


def end_of_rest(spans, p):
    return max(0, spans[p][1] - spans[p][0] - TILE)


def fetched(spans, p):
    first = spans[p][1] - end_of_rest(spans, p)
    head = min(TILE, spans[p + 1][1] - spans[p + 1][0]) if p + 1 < len(spans) else 0
    return first, spans[p][1] + head


def dot_tile(out, rows, eig, tile):
    _, first, size, col = tile
    out[:, col : col + size] = lax.dot_general(
        rows,
        eig[first : first + size, :],
        (((1,), (1,)), ((), ())),
        preferred_element_type=jnp.float32,
    ).astype(out.dtype)


def classes_made(orders):
    last = next(i for i, (_, stage) in enumerate(ORDER) if stage > 0) - 1
    made, seen = [], []
    for i, bits in enumerate(orders):
        new = [c for c in halves(bits)[1] if c not in seen]
        if i == last:
            new += [c for c in range(8) if c not in seen + new]
        seen += new
        made.append(new)
    return made


def pick_rows(prods, made, classes, block):
    parts = []
    for c in classes:
        i = next(i for i, group in enumerate(made) if c in group)
        at = made[i].index(c) * block
        parts.append(prods[i][at : at + block, :])
    return jnp.concatenate(parts, axis=0)


def setup_kernel(n, per_chunk, lanc, span, order_hbm, own_hbm, lanc_hbm, eig_hbm, *rest):
    pick, own, lanc16, eig, order, sem = rest
    copies = [
        pltpu.make_async_copy(src, dst, sem.at[i])
        for i, (src, dst) in enumerate(
            [
                (order_hbm, order),
                (own_hbm, own),
                (lanc_hbm, lanc16),
                (eig_hbm.at[pl.ds(span[0], span[1] - span[0])], eig),
            ]
        )
    ]
    for copy in copies:
        copy.start()
    me = lax.axis_index("grid")
    core = lax.axis_index("eig")
    bands = pick.shape[1]
    rest_bits = list(range(3, n.bit_length() - 1))
    slots = [(r, j) for c in range(8) for r in ranked(rest_bits, c) for j in range(per_chunk)]
    col = lax.broadcasted_iota(jnp.int32, (2 * lanc, bands), 1)
    upper = lax.broadcasted_iota(jnp.int32, (2 * lanc, bands), 0) < lanc
    copies[0].wait()
    for i in range(0, len(slots), 2):
        want = []
        for r, j in slots[i : i + 2]:
            offset = jnp.where(core == 0, grid_offset(r, 0), grid_offset(r, 1))
            band = order[(me ^ offset) * per_chunk + j]
            want.append(lax.rem(band + core * (bands // 2), bands))
        hit = col == jnp.where(upper, want[0], want[1])
        pick[i * lanc : (i + 2) * lanc, :] = hit.astype(jnp.float32).astype(jnp.bfloat16)
    for copy in copies[1:]:
        copy.wait()


def send_kernel(spans, orders, p, pick, own, other, lanc16, eig_hbm, _, head, *rest):
    made = classes_made(orders)
    prods = rest[: sum(1 for group in made[:p] if group)]
    out, *rest = rest[len(prods) :]
    block = pick.shape[0] // 8
    new = rest.pop(0) if made[p] else None
    loads = []
    if len(rest) > 1:
        eig, sem = rest
        first, last = fetched(spans, p)
        cuts = [t[1:3] for t in tiles_of(spans, p)[1:]]
        rest_end = end_of_rest(spans, p)
        if last - first > rest_end:
            cuts.append((rest_end, last - first - rest_end))
        for i, (at, size) in enumerate(cuts):
            loads.append(
                pltpu.make_async_copy(
                    eig_hbm.at[pl.ds(first + at, size)], eig.at[pl.ds(at, size)], sem.at[i]
                )
            )
            loads[-1].start()
    lanc = lanc16[...].astype(jnp.float32)
    bands = jnp.concatenate([own[...], other[...]], axis=0)

    def make(classes, at):
        rows = [pick[c * block : (c + 1) * block, :] for c in classes]
        chosen = lax.dot_general(
            jnp.concatenate(rows, axis=0),
            bands,
            (((1,), (0,)), ((), ())),
            preferred_element_type=jnp.float32,
        )
        value = chosen.reshape(-1, *lanc.shape) * lanc[None]
        new[at * block : (at + len(classes)) * block, :] = value.reshape(chosen.shape).astype(
            jnp.bfloat16
        )

    needed = [c for c in made[p] if c in halves(orders[p])[1]]
    if needed:
        make(needed, 0)
    found, at = [], 0
    for i, group in enumerate(made[: p + 1]):
        found.append(new if i == p else prods[at] if group else None)
        at += 1 if group else 0
    rows = pick_rows(found, made, halves(orders[p])[1], block)
    for i, tile in enumerate(tiles_of(spans, p)):
        if i > 0:
            loads[i - 1].wait()
        dot_tile(out, rows, head if i == 0 else eig, tile)
    if len(made[p]) > len(needed):
        make(made[p][len(needed) :], len(needed))
    for load in loads[len(tiles_of(spans, p)) - 1 :]:
        load.wait()


def keep_kernel(spans, orders, p, *refs):
    made = classes_made(orders)
    out = refs[-1]
    found, at = [], 0
    for group in made:
        found.append(refs[at] if group else None)
        at += 1 if group else 0
    eigs = refs[at:-1]
    block = out.shape[0] // 4
    rows = pick_rows(found, made, halves(orders[p])[0], block)
    for tile in tiles_of(spans, p):
        dot_tile(out, rows, eigs[tile[0] - p], tile)


def add_kernel(kept, got, _, leave, keep):
    mid = leave.shape[0]
    leave[...] = (kept[:mid, :] + got[:mid, :].astype(jnp.float32)).astype(leave.dtype)
    keep[...] = kept[mid:, :] + got[mid:, :].astype(jnp.float32)


def finish_kernel(spans, *refs):
    count = len(spans)
    kept, came, out = refs[:count], refs[count : 2 * count], refs[-1]
    for (at, end), a, b in zip(spans, kept, came):
        out[:, at:end] = a[a.shape[0] - out.shape[0] :, :] + b[...].astype(jnp.float32)


VMEM_SPEC = pl.BlockSpec(memory_space=pltpu.VMEM)
SPECS = {
    True: pl.BlockSpec(memory_space=pltpu.HBM),
    False: VMEM_SPEC,
    None: pl.BlockSpec(memory_space=pl.ANY),
}


def kernel_call(body, ins, outs, scratch, cost):
    flops, moved = cost
    return pl.pallas_call(
        body,
        out_shape=[jax.ShapeDtypeStruct(*out) for out in outs],
        in_specs=[SPECS[far] for _, far in ins],
        out_specs=[VMEM_SPEC] * len(outs),
        scratch_shapes=scratch,
        compiler_params=pltpu.CompilerParams(vmem_limit_bytes=VMEM_LIMIT),
        cost_estimate=pl.CostEstimate(flops=flops, bytes_accessed=moved, transcendentals=0),
    )(
        *(
            pltpu.with_memory_space_constraint(x, pltpu.HBM) if far else x
            for x, far in ins
        )
    )


def per_device(n, eigvecs, lanczos, bands, band_order):
    cols, depth = eigvecs.shape
    lanc = lanczos.shape[0]
    per_chunk = band_order.shape[0] // n
    rows = band_order.shape[0] * lanc
    spans = split_columns(cols)
    widths = [end - at for at, end in spans]
    orders = [bits for _, bits in PLAN]
    bf16 = jnp.bfloat16

    def exchange(value, stage):
        pairs = []
        for i in range(n):
            for core in range(2):
                bit = WAYS[core][stage] if stage < 3 else stage
                pairs.append((2 * i + core, 2 * (i ^ (1 << bit)) + core))
        return lax.ppermute(value, ("grid", "eig"), pairs)

    def flops(width):
        return rows * width * depth

    other = lax.ppermute(bands, "eig", [(0, 1), (1, 0)])
    head = min(TILE, widths[0])
    pick, own, lanc16, eig = kernel_call(
        functools.partial(setup_kernel, n, per_chunk, lanc, (0, head)),
        [(band_order, True), (bands, True), (lanczos, True), (eigvecs, True)],
        [
            ((rows, 2 * bands.shape[0]), bf16),
            (bands.shape, bf16),
            (lanczos.shape, bf16),
            ((head, depth), bf16),
        ],
        [pltpu.SMEM(band_order.shape, jnp.int32), pltpu.SemaphoreType.DMA((4,))],
        (0, 2 * head * depth),
    )
    made = classes_made(orders)
    eigs, prods, value, got = [eig], [], {}, {}
    token = other
    later = range(3, n.bit_length() - 1)

    def kept(p):
        tiles = sorted({tile[0] for tile in tiles_of(spans, p)})
        return kernel_call(
            functools.partial(keep_kernel, spans, orders, p),
            [(x, False) for x in prods] + [(eigs[i], False) for i in tiles],
            [((rows // 2, widths[p]), jnp.float32)],
            [],
            (0, 0),
        )[0]

    events = ORDER + [(p, stage) for stage in later for p in range(len(PLAN))]
    for p, stage in events:
        if stage == 0:
            first, last = fetched(spans, p)
            outs = [((rows // 2, widths[p]), bf16)]
            if made[p]:
                outs.append(((len(made[p]) * (rows // 8), depth), bf16))
            if last > first:
                outs.append(((last - first, depth), bf16))
            copies = len(tiles_of(spans, p))
            leave, *new = kernel_call(
                functools.partial(send_kernel, spans, orders, p),
                [(x, False) for x in (pick, own, other, lanc16)]
                + [(eigvecs, True), (token, None), (eigs[p], False)]
                + [(x, False) for x in prods],
                outs,
                [pltpu.SemaphoreType.DMA((copies,))],
                (0, 0),
            )
            if made[p]:
                prods.append(new.pop(0))
            eigs += new
        else:
            half = rows // 2 >> stage
            size = half * widths[p]
            leave, value[p] = kernel_call(
                add_kernel,
                [(kept(p) if stage == 1 else value[p], False), (got[p], False), (token, None)],
                [((half, widths[p]), bf16 if stage < 3 else jnp.float32)]
                + [((half, widths[p]), jnp.float32)],
                [],
                (2 * size, 18 * size),
            )
        token = leave
        got[p] = exchange(leave, (*orders[p], *later)[stage])
    outs = [(value[p], got[p]) for p in range(len(PLAN))]
    (result,) = kernel_call(
        functools.partial(finish_kernel, spans),
        [(value, False) for value, _ in outs] + [(came, False) for _, came in outs],
        [((rows // n, cols), jnp.float32)],
        [],
        (rows // n * cols, 12 * rows // n * cols),
    )
    return result.reshape(per_chunk, lanc, cols)


def solution(mesh):
    in_specs = (
        P("eig", ("rep", "grid")),
        P(None, ("rep", "grid")),
        P("eig", ("rep", "grid")),
        P("rep"),
    )
    out_specs = P(("rep", "grid"), None, "eig")
    return jax.shard_map(
        functools.partial(per_device, mesh.shape["grid"]),
        mesh=mesh,
        in_specs=in_specs,
        out_specs=out_specs,
        check_vma=False,
    )
```

```python
import functools

import jax
import jax.numpy as jnp
from jax import lax
from jax.experimental import pallas as pl
from jax.experimental.pallas import tpu as pltpu
from jax.sharding import PartitionSpec as P

TILE = 256
SETUP = 512
VMEM_LIMIT = 32 * 1024 * 1024
WAYS = ((1, 0, 2), (0, 2, 1))
PLAN = [(3.5, (0, 1, 2)), (2, (1, 0, 2)), (1.5, (0, 1, 2))]


def ranked(bits, fixed=0):
    out = [fixed]
    for b in reversed(bits):
        out = [c | (1 << b) for c in out] + out
    return out


def split_columns(cols):
    unit = 128
    total = sum(share for share, _ in PLAN)
    ends, done = [], 0
    for share, _ in PLAN[:-1]:
        done += share
        ends.append(int(round(cols * done / total / unit)) * unit)
    ends.append(cols)
    return list(zip([0] + ends[:-1], ends))


def halves(bits):
    keep = ranked(bits[1:])
    return keep, [c | (1 << bits[0]) for c in keep]


def grid_offset(c, core):
    return sum(((c >> s) & 1) << bit for s, bit in enumerate(WAYS[core])) + (c >> 3 << 3)


def rows_of(prods, made, classes):
    if classes in made:
        return prods[made.index(classes)][...]
    parts = []
    for c in classes:
        i = next(i for i, group in enumerate(made) if c in group)
        block = prods[i].shape[0] // len(made[i])
        at = made[i].index(c) * block
        parts.append(prods[i][at : at + block, :])
    return jnp.concatenate(parts, axis=0)


def dot_span(out, rows, eigs, cuts, span):
    col = span[0]
    while col < span[1]:
        i = max(i for i, cut in enumerate(cuts) if cut <= col)
        size = min(TILE, span[1] - col, cuts[i + 1] - col)
        out[:, col - span[0] : col - span[0] + size] = lax.dot_general(
            rows,
            eigs[i][col - cuts[i] : col - cuts[i] + size, :],
            (((1,), (1,)), ((), ())),
            preferred_element_type=jnp.float32,
        )
        col += size


def setup_kernel(n, per_chunk, lanc, classes, width, order_hbm, own_hbm, lanc_hbm, eig_hbm, *rest):
    pick, own, lanc16, eig, order, sem = rest
    copies = [
        pltpu.make_async_copy(src, dst, sem.at[i])
        for i, (src, dst) in enumerate(
            [
                (order_hbm, order),
                (own_hbm, own),
                (lanc_hbm, lanc16),
                (eig_hbm.at[pl.ds(0, width)], eig),
            ]
        )
    ]
    for copy in copies:
        copy.start()
    me = lax.axis_index("grid")
    core = lax.axis_index("eig")
    bands = pick.shape[1]
    rest_bits = list(range(3, n.bit_length() - 1))
    slots = [(r, j) for c in classes for r in ranked(rest_bits, c) for j in range(per_chunk)]
    col = lax.broadcasted_iota(jnp.int32, (2 * lanc, bands), 1)
    upper = lax.broadcasted_iota(jnp.int32, (2 * lanc, bands), 0) < lanc
    copies[0].wait()
    for i in range(0, len(slots), 2):
        want = []
        for r, j in slots[i : i + 2]:
            offset = jnp.where(core == 0, grid_offset(r, 0), grid_offset(r, 1))
            band = order[(me ^ offset) * per_chunk + j]
            want.append(lax.rem(band + core * (bands // 2), bands))
        hit = col == jnp.where(upper, want[0], want[1])
        pick[i * lanc : (i + 2) * lanc, :] = hit.astype(jnp.float32).astype(jnp.bfloat16)
    for copy in copies[1:]:
        copy.wait()


def fetch(eig_hbm, eig, sem, cuts):
    copies = []
    for i, (at, end) in enumerate(zip(cuts, cuts[1:])):
        if at == end:
            copies.append(None)
            continue
        part = pl.ds(at - cuts[0], end - at)
        copy = pltpu.make_async_copy(eig_hbm.at[pl.ds(at, end - at)], eig.at[part], sem.at[i])
        copy.start()
        copies.append(copy)
    return copies


def make_rows(prod, pick, own, other, lanc16, first):
    lanc = lanc16[...].astype(jnp.float32)
    chosen = lax.dot_general(
        pick[first : first + prod.shape[0], :],
        jnp.concatenate([own[...], other[...]], axis=0),
        (((1,), (0,)), ((), ())),
        preferred_element_type=jnp.float32,
    )
    value = chosen.reshape(-1, *lanc.shape) * lanc[None]
    prod[...] = value.reshape(chosen.shape).astype(jnp.bfloat16)


def first_kernel(
    cuts, span, pick, own, other, lanc16, eig, eig_hbm, out, prod, eig_next, acc, sem
):
    copies = fetch(eig_hbm, eig_next, sem, [cuts[1], max(cuts[1], span[1]), cuts[2]])
    make_rows(prod, pick, own, other, lanc16, 0)
    rows = prod[...]
    dot_span(acc, rows, [eig], cuts, (0, min(cuts[1], span[1])))
    if span[1] > cuts[1]:
        copies[0].wait()
        late = acc.at[:, cuts[1] : span[1]]
        dot_span(late, rows, [eig, eig_next], cuts, (cuts[1], span[1]))
    out[...] = acc[...].astype(out.dtype)
    copies[1].wait()


def send_kernel(
    cuts, orders, made, spans, pick, own, other, lanc16, prod, eig, eig_hbm, *rest
):
    count = len(spans)
    outs, (more, eig_next, acc, sem) = rest[:count], rest[count:]
    ends = [end for _, end in spans[1:]]
    copies = fetch(eig_hbm, eig_next, sem, [cuts[2], *ends])
    make_rows(more, pick, own, other, lanc16, prod.shape[0])
    for i, (out, span) in enumerate(zip(outs, spans)):
        if i > 0:
            copies[i - 1].wait()
        rows = rows_of([prod, more], made, halves(orders[i])[1])
        part = acc.at[:, : span[1] - span[0]]
        dot_span(part, rows, [None, eig, eig_next], cuts, span)
        out[...] = part[...].astype(out.dtype)


def keep_kernel(cuts, classes, made, span, prod, more, *refs):
    used = arrays_of(cuts, span)
    eigs = [refs[used.index(i)] if i in used else None for i in range(len(cuts) - 1)]
    dot_span(refs[-1], rows_of([prod, more], made, classes), eigs, cuts, span)


def arrays_of(cuts, span):
    return [i for i in range(len(cuts) - 1) if cuts[i] < span[1] and span[0] < cuts[i + 1]]


def add_kernel(kept, got, _, leave, keep):
    mid = leave.shape[0]
    leave[...] = (kept[:mid, :] + got[:mid, :].astype(jnp.float32)).astype(leave.dtype)
    keep[...] = kept[mid:, :] + got[mid:, :].astype(jnp.float32)


def finish_kernel(spans, *refs):
    count = len(spans)
    kept, came, out = refs[:count], refs[count : 2 * count], refs[-1]
    for (at, end), a, b in zip(spans, kept, came):
        out[:, at:end] = a[a.shape[0] - out.shape[0] :, :] + b[...].astype(jnp.float32)


VMEM_SPEC = pl.BlockSpec(memory_space=pltpu.VMEM)
SPECS = {
    True: pl.BlockSpec(memory_space=pltpu.HBM),
    False: VMEM_SPEC,
    None: pl.BlockSpec(memory_space=pl.ANY),
}


def kernel_call(body, ins, outs, scratch, cost):
    flops, moved = cost
    return pl.pallas_call(
        body,
        out_shape=[jax.ShapeDtypeStruct(*out) for out in outs],
        in_specs=[SPECS[far] for _, far in ins],
        out_specs=[VMEM_SPEC] * len(outs),
        scratch_shapes=scratch,
        compiler_params=pltpu.CompilerParams(vmem_limit_bytes=VMEM_LIMIT),
        cost_estimate=pl.CostEstimate(flops=flops, bytes_accessed=moved, transcendentals=0),
    )(
        *(
            pltpu.with_memory_space_constraint(x, pltpu.HBM) if far else x
            for x, far in ins
        )
    )


def per_device(n, eigvecs, lanczos, bands, band_order):
    cols, depth = eigvecs.shape
    lanc = lanczos.shape[0]
    per_chunk = band_order.shape[0] // n
    rows = band_order.shape[0] * lanc
    spans = split_columns(cols)
    widths = [end - at for at, end in spans]
    orders = [bits for _, bits in PLAN]
    bf16 = jnp.bfloat16

    def exchange(value, stage):
        pairs = []
        for i in range(n):
            for core in range(2):
                bit = WAYS[core][stage] if stage < 3 else stage
                pairs.append((2 * i + core, 2 * (i ^ (1 << bit)) + core))
        return lax.ppermute(value, ("grid", "eig"), pairs)

    def flops(width):
        return rows * width * depth

    made = list(reversed(halves(orders[0])))
    cuts = [0, min(SETUP, widths[0]), spans[1][1], cols]
    other = lax.ppermute(bands, "eig", [(0, 1), (1, 0)])
    pick, own, lanc16, eig = kernel_call(
        functools.partial(setup_kernel, n, per_chunk, lanc, made[0] + made[1], cuts[1]),
        [(band_order, True), (bands, True), (lanczos, True), (eigvecs, True)],
        [
            ((rows, 2 * bands.shape[0]), bf16),
            (bands.shape, bf16),
            (lanczos.shape, bf16),
            ((cuts[1], depth), bf16),
        ],
        [pltpu.SMEM(band_order.shape, jnp.int32), pltpu.SemaphoreType.DMA((4,))],
        (0, 2 * cuts[1] * depth),
    )
    eigs = [eig]
    sources = [(x, False) for x in (pick, own, other, lanc16)]
    send, prod, eig = kernel_call(
        functools.partial(first_kernel, cuts, spans[0]),
        sources + [(eig, False), (eigvecs, True)],
        [((rows // 2, widths[0]), bf16), ((rows // 2, depth), bf16)]
        + [((cuts[2] - cuts[1], depth), bf16)],
        [pltpu.VMEM((rows // 2, widths[0]), jnp.float32), pltpu.SemaphoreType.DMA((2,))],
        (flops(widths[0]), 2 * widths[1] * depth),
    )
    eigs.append(eig)
    *sends, more, eig = kernel_call(
        functools.partial(send_kernel, cuts, orders[1:], made, spans[1:]),
        sources + [(prod, False), (eig, False), (eigvecs, True)],
        [((rows // 2, w), bf16) for w in widths[1:]]
        + [((rows // 2, depth), bf16), ((cuts[3] - cuts[2], depth), bf16)],
        [
            pltpu.VMEM((rows // 2, max(widths[1:])), jnp.float32),
            pltpu.SemaphoreType.DMA((len(PLAN) - 2,)),
        ],
        (flops(sum(widths[1:])), 2 * sum(widths[2:]) * depth),
    )
    eigs.append(eig)
    got = [exchange(s, bits[0]) for s, bits in zip([send, *sends], orders)]
    value = []
    for p, bits in enumerate(orders):
        value += kernel_call(
            functools.partial(keep_kernel, cuts, halves(bits)[0], made, spans[p]),
            [(prod, False), (more, False)]
            + [(eigs[i], False) for i in arrays_of(cuts, spans[p])],
            [((rows // 2, widths[p]), jnp.float32)],
            [],
            (flops(widths[p]), 2 * widths[p] * depth),
        )
    later = range(3, n.bit_length() - 1)
    token = prod
    for stage in range(1, 3 + len(later)):
        for p, bits in enumerate(orders):
            half = value[p].shape[0] // 2
            size = half * widths[p]
            leave, value[p] = kernel_call(
                add_kernel,
                [(value[p], False), (got[p], False), (token, None)],
                [((half, widths[p]), bf16 if stage < 3 else jnp.float32)]
                + [((half, widths[p]), jnp.float32)],
                [],
                (2 * size, 18 * size),
            )
            token = leave
            got[p] = exchange(leave, (*bits, *later)[stage])
    outs = list(zip(value, got))
    (result,) = kernel_call(
        functools.partial(finish_kernel, spans),
        [(value, False) for value, _ in outs] + [(came, False) for _, came in outs],
        [((rows // n, cols), jnp.float32)],
        [],
        (rows // n * cols, 12 * rows // n * cols),
    )
    return result.reshape(per_chunk, lanc, cols)


def solution(mesh):
    in_specs = (
        P("eig", ("rep", "grid")),
        P(None, ("rep", "grid")),
        P("eig", ("rep", "grid")),
        P("rep"),
    )
    out_specs = P(("rep", "grid"), None, "eig")
    return jax.shard_map(
        functools.partial(per_device, mesh.shape["grid"]),
        mesh=mesh,
        in_specs=in_specs,
        out_specs=out_specs,
        check_vma=False,
    )
```

```python
import functools

import jax
import jax.numpy as jnp
from jax import lax
from jax.experimental import pallas as pl
from jax.experimental.pallas import tpu as pltpu
from jax.sharding import PartitionSpec as P

TILE = 256
VMEM_LIMIT = 32 * 1024 * 1024
X, NEAR, FAR = 0, 1, 2
PLAN = [
    (3, (X, FAR, NEAR), (NEAR, X, FAR)),
    (2.5, (X, NEAR, FAR), (NEAR, X, FAR)),
    (1.5, (FAR, X, NEAR), (X, FAR, NEAR)),
]
ORDER = [(piece, stage) for stage in (1, 2) for piece in range(len(PLAN))]


def ranked(bits, fixed=0):
    out = [fixed]
    for b in reversed(bits):
        out = [c | (1 << b) for c in out] + out
    return out


def split_columns(cols):
    unit = 128
    total = sum(plan[0] for plan in PLAN)
    ends, done = [], 0
    for share, *_ in PLAN[:-1]:
        done += share
        ends.append(int(round(cols * done / total / unit)) * unit)
    ends.append(cols)
    return list(zip([0] + ends[:-1], ends))


def halves(bits):
    keep = ranked(bits[1:])
    return keep, [c | (1 << bits[0]) for c in keep]


def places(p, core, kept):
    keep, leave = halves(PLAN[0][1 + core])
    return [(leave + keep).index(c) for c in halves(PLAN[p][1 + core])[0 if kept else 1]]


def rows_of(prod, p, kept):
    block = prod.shape[0] // 8
    core = lax.axis_index("eig")
    parts = []
    for a, b in zip(places(p, 0, kept), places(p, 1, kept)):
        at = a * block if a == b else pl.multiple_of(jnp.where(core == 0, a, b) * block, block)
        parts.append(prod[pl.ds(at, block), :])
    return jnp.concatenate(parts, axis=0)


def dot_span(out, rows, eigs, cuts, span):
    col = span[0]
    while col < span[1]:
        i = max(i for i, cut in enumerate(cuts) if cut <= col)
        size = min(TILE, span[1] - col, cuts[i + 1] - col)
        out[:, col - span[0] : col - span[0] + size] = lax.dot_general(
            rows,
            eigs[i][col - cuts[i] : col - cuts[i] + size, :],
            (((1,), (1,)), ((), ())),
            preferred_element_type=jnp.float32,
        )
        col += size


def setup_kernel(n, per_chunk, lanc, width, order_hbm, own_hbm, lanc_hbm, eig_hbm, *rest):
    pick, own, lanc16, eig, order, sem = rest
    copies = [
        pltpu.make_async_copy(src, dst, sem.at[i])
        for i, (src, dst) in enumerate(
            [
                (order_hbm, order),
                (own_hbm, own),
                (lanc_hbm, lanc16),
                (eig_hbm.at[pl.ds(0, width)], eig),
            ]
        )
    ]
    for copy in copies:
        copy.start()
    me = lax.axis_index("grid")
    core = lax.axis_index("eig")
    bands = pick.shape[1]
    rest_bits = list(range(3, n.bit_length() - 1))
    classes = zip(*(sum(reversed(halves(PLAN[0][1 + i])), []) for i in range(2)))
    slots = []
    for pair in classes:
        for both in zip(*(ranked(rest_bits, c) for c in pair)):
            slots += [(both, j) for j in range(per_chunk)]
    col = lax.broadcasted_iota(jnp.int32, (2 * lanc, bands), 1)
    upper = lax.broadcasted_iota(jnp.int32, (2 * lanc, bands), 0) < lanc
    copies[0].wait()
    for i in range(0, len(slots), 2):
        want = []
        for r, j in slots[i : i + 2]:
            offset = jnp.where(core == 0, r[0], r[1])
            band = order[(me ^ offset) * per_chunk + j]
            want.append(lax.rem(band + core * (bands // 2), bands))
        hit = col == jnp.where(upper, want[0], want[1])
        pick[i * lanc : (i + 2) * lanc, :] = hit.astype(jnp.float32).astype(jnp.bfloat16)
    for copy in copies[1:]:
        copy.wait()


def fetch(eig_hbm, eig, sem, cuts):
    copies = []
    for i, (at, end) in enumerate(zip(cuts, cuts[1:])):
        if at == end:
            copies.append(None)
            continue
        part = pl.ds(at - cuts[0], end - at)
        copy = pltpu.make_async_copy(eig_hbm.at[pl.ds(at, end - at)], eig.at[part], sem.at[i])
        copy.start()
        copies.append(copy)
    return copies


def make_rows(prod, pick, own, other, lanc16, first):
    lanc = lanc16[...].astype(jnp.float32)
    chosen = lax.dot_general(
        pick[first : first + prod.shape[0], :],
        jnp.concatenate([own[...], other[...]], axis=0),
        (((1,), (0,)), ((), ())),
        preferred_element_type=jnp.float32,
    )
    value = chosen.reshape(-1, *lanc.shape) * lanc[None]
    prod[...] = value.reshape(chosen.shape).astype(jnp.bfloat16)


def first_kernel(width, pick, own, other, lanc16, eig, out, prod, acc):
    make_rows(prod, pick, own, other, lanc16, 0)
    dot_span(acc, prod[...], [eig], [0, width], (0, width))
    out[...] = acc[...].astype(out.dtype)


def send_kernel(cuts, pick, own, other, lanc16, half, eig_hbm, *rest):
    count = len(cuts) - 2
    outs, (prod, eig, acc, sem) = rest[:count], rest[count:]
    copies = fetch(eig_hbm, eig, sem, cuts[1:])
    first = half.shape[0]
    prod[:first, :] = half[...]
    make_rows(prod.at[first:, :], pick, own, other, lanc16, first)
    for i, out in enumerate(outs):
        rows = rows_of(prod, i + 1, False)
        copies[i].wait()
        part = acc.at[:, : out.shape[1]]
        dot_span(part, rows, [None, eig], [0, cuts[1], cuts[-1]], (cuts[i + 1], cuts[i + 2]))
        out[...] = part[...].astype(out.dtype)


def keep_kernel(p, first, prod, eig, out):
    dot_span(
        out, rows_of(prod, p, True), [eig], [0, eig.shape[0]], (first, first + out.shape[1])
    )


def add_kernel(kept, got, _, leave, keep):
    mid = leave.shape[0]
    leave[...] = (kept[:mid, :] + got[:mid, :].astype(jnp.float32)).astype(leave.dtype)
    keep[...] = kept[mid:, :] + got[mid:, :].astype(jnp.float32)


def finish_kernel(spans, *refs):
    count = len(spans)
    kept, came, out = refs[:count], refs[count : 2 * count], refs[-1]
    for (at, end), a, b in zip(spans, kept, came):
        out[:, at:end] = a[a.shape[0] - out.shape[0] :, :] + b[...].astype(jnp.float32)


VMEM_SPEC = pl.BlockSpec(memory_space=pltpu.VMEM)
SPECS = {
    True: pl.BlockSpec(memory_space=pltpu.HBM),
    False: VMEM_SPEC,
    None: pl.BlockSpec(memory_space=pl.ANY),
}


def kernel_call(body, ins, outs, scratch, cost):
    flops, moved = cost
    return pl.pallas_call(
        body,
        out_shape=[jax.ShapeDtypeStruct(*out) for out in outs],
        in_specs=[SPECS[far] for _, far in ins],
        out_specs=[VMEM_SPEC] * len(outs),
        scratch_shapes=scratch,
        compiler_params=pltpu.CompilerParams(vmem_limit_bytes=VMEM_LIMIT),
        cost_estimate=pl.CostEstimate(flops=flops, bytes_accessed=moved, transcendentals=0),
    )(
        *(
            pltpu.with_memory_space_constraint(x, pltpu.HBM) if far else x
            for x, far in ins
        )
    )


def per_device(n, eigvecs, lanczos, bands, band_order):
    cols, depth = eigvecs.shape
    lanc = lanczos.shape[0]
    per_chunk = band_order.shape[0] // n
    rows = band_order.shape[0] * lanc
    spans = split_columns(cols)
    cuts = [0] + [end for _, end in spans]
    widths = [end - at for at, end in spans]
    bf16 = jnp.bfloat16

    def exchange(value, p, stage):
        pairs = []
        for i in range(n):
            for core in range(2):
                bit = PLAN[p][1 + core][stage] if stage < 3 else stage
                pairs.append((2 * i + core, 2 * (i ^ (1 << bit)) + core))
        return lax.ppermute(value, ("grid", "eig"), pairs)

    def flops(width):
        return rows * width * depth

    other = lax.ppermute(bands, "eig", [(0, 1), (1, 0)])
    pick, own, lanc16, eig = kernel_call(
        functools.partial(setup_kernel, n, per_chunk, lanc, widths[0]),
        [(band_order, True), (bands, True), (lanczos, True), (eigvecs, True)],
        [
            ((rows, 2 * bands.shape[0]), bf16),
            (bands.shape, bf16),
            (lanczos.shape, bf16),
            ((widths[0], depth), bf16),
        ],
        [pltpu.SMEM(band_order.shape, jnp.int32), pltpu.SemaphoreType.DMA((4,))],
        (0, 2 * widths[0] * depth),
    )
    sources = [(x, False) for x in (pick, own, other, lanc16)]
    send, half = kernel_call(
        functools.partial(first_kernel, widths[0]),
        sources + [(eig, False)],
        [((rows // 2, widths[0]), bf16), ((rows // 2, depth), bf16)],
        [pltpu.VMEM((rows // 2, widths[0]), jnp.float32)],
        (flops(widths[0]), 2 * widths[0] * depth),
    )
    *sends, prod, eig_rest = kernel_call(
        functools.partial(send_kernel, cuts),
        sources + [(half, False), (eigvecs, True)],
        [((rows // 2, w), bf16) for w in widths[1:]]
        + [((rows, depth), bf16), ((cols - widths[0], depth), bf16)],
        [
            pltpu.VMEM((rows // 2, max(widths[1:])), jnp.float32),
            pltpu.SemaphoreType.DMA((len(PLAN) - 1,)),
        ],
        (flops(sum(widths[1:])), 2 * sum(widths[1:]) * depth),
    )
    got = [exchange(s, p, 0) for p, s in enumerate([send, *sends])]
    value = []
    for p, width in enumerate(widths):
        value += kernel_call(
            functools.partial(keep_kernel, p, cuts[p] - cuts[min(p, 1)]),
            [(prod, False), (eig_rest if p else eig, False)],
            [((rows // 2, width), jnp.float32)],
            [],
            (flops(width), 2 * width * depth),
        )
    later = range(3, n.bit_length() - 1)
    token = prod
    for p, stage in ORDER + [(p, stage) for stage in later for p in range(len(PLAN))]:
        part = value[p].shape[0] // 2
        size = part * widths[p]
        leave, value[p] = kernel_call(
            add_kernel,
            [(value[p], False), (got[p], False), (token, None)],
            [((part, widths[p]), bf16 if stage < 3 else jnp.float32)]
            + [((part, widths[p]), jnp.float32)],
            [],
            (2 * size, 18 * size),
        )
        token = leave
        got[p] = exchange(leave, p, stage)
    outs = list(zip(value, got))
    (result,) = kernel_call(
        functools.partial(finish_kernel, spans),
        [(value, False) for value, _ in outs] + [(came, False) for _, came in outs],
        [((rows // n, cols), jnp.float32)],
        [],
        (rows // n * cols, 12 * rows // n * cols),
    )
    return result.reshape(per_chunk, lanc, cols)


def solution(mesh):
    in_specs = (
        P("eig", ("rep", "grid")),
        P(None, ("rep", "grid")),
        P("eig", ("rep", "grid")),
        P("rep"),
    )
    out_specs = P(("rep", "grid"), None, "eig")
    return jax.shard_map(
        functools.partial(per_device, mesh.shape["grid"]),
        mesh=mesh,
        in_specs=in_specs,
        out_specs=out_specs,
        check_vma=False,
    )
```

```python
import functools

import jax
import jax.numpy as jnp
from jax import lax
from jax.experimental import pallas as pl
from jax.experimental.pallas import tpu as pltpu
from jax.sharding import PartitionSpec as P

TILE = 256
VMEM_LIMIT = 32 * 1024 * 1024
X, NEAR, FAR = 0, 1, 2
PLAN = [
    (3.5, (NEAR, X, FAR), (X, FAR, NEAR)),
    (2, (X, NEAR, FAR), (FAR, X, NEAR)),
    (1.5, (NEAR, X, FAR), (X, FAR, NEAR)),
]
ORDER = [(piece, stage) for stage in (1, 2) for piece in range(len(PLAN))]


def ranked(bits, fixed=0):
    out = [fixed]
    for b in reversed(bits):
        out = [c | (1 << b) for c in out] + out
    return out


def split_columns(cols):
    unit = 128
    total = sum(plan[0] for plan in PLAN)
    ends, done = [], 0
    for share, *_ in PLAN[:-1]:
        done += share
        ends.append(int(round(cols * done / total / unit)) * unit)
    ends.append(cols)
    return list(zip([0] + ends[:-1], ends))


def halves(bits):
    keep = ranked(bits[1:])
    return keep, [c | (1 << bits[0]) for c in keep]


def places(p, core, kept):
    keep, leave = halves(PLAN[0][1 + core])
    return [(leave + keep).index(c) for c in halves(PLAN[p][1 + core])[0 if kept else 1]]


def rows_of(prod, p, kept):
    block = prod.shape[0] // 8
    core = lax.axis_index("eig")
    parts = []
    for a, b in zip(places(p, 0, kept), places(p, 1, kept)):
        at = a * block if a == b else pl.multiple_of(jnp.where(core == 0, a, b) * block, block)
        parts.append(prod[pl.ds(at, block), :])
    return jnp.concatenate(parts, axis=0)


def tiles_of(width):
    return [(at, min(TILE, width - at)) for at in range(0, width, TILE)]


def dot_tiles(out, rows, eig, first, waits=()):
    for i, (at, size) in enumerate(tiles_of(out.shape[1])):
        if waits:
            waits[i].wait()
        out[:, at : at + size] = lax.dot_general(
            rows,
            eig[first + at : first + at + size, :],
            (((1,), (1,)), ((), ())),
            preferred_element_type=jnp.float32,
        )


def setup_kernel(n, per_chunk, lanc, width, order_hbm, own_hbm, lanc_hbm, eig_hbm, *rest):
    pick, own, lanc16, eig, order, sem = rest
    copies = [
        pltpu.make_async_copy(src, dst, sem.at[i])
        for i, (src, dst) in enumerate(
            [
                (order_hbm, order),
                (own_hbm, own),
                (lanc_hbm, lanc16),
                (eig_hbm.at[pl.ds(0, width)], eig),
            ]
        )
    ]
    for copy in copies:
        copy.start()
    me = lax.axis_index("grid")
    core = lax.axis_index("eig")
    bands = pick.shape[1]
    rest_bits = list(range(3, n.bit_length() - 1))
    classes = zip(*(sum(reversed(halves(PLAN[0][1 + i])), []) for i in range(2)))
    slots = []
    for pair in classes:
        for both in zip(*(ranked(rest_bits, c) for c in pair)):
            slots += [(both, j) for j in range(per_chunk)]
    col = lax.broadcasted_iota(jnp.int32, (2 * lanc, bands), 1)
    upper = lax.broadcasted_iota(jnp.int32, (2 * lanc, bands), 0) < lanc
    copies[0].wait()
    for i in range(0, len(slots), 2):
        want = []
        for r, j in slots[i : i + 2]:
            offset = jnp.where(core == 0, r[0], r[1])
            band = order[(me ^ offset) * per_chunk + j]
            want.append(lax.rem(band + core * (bands // 2), bands))
        hit = col == jnp.where(upper, want[0], want[1])
        pick[i * lanc : (i + 2) * lanc, :] = hit.astype(jnp.float32).astype(jnp.bfloat16)
    for copy in copies[1:]:
        copy.wait()


def make_rows(prod, pick, own, other, lanc16, first):
    lanc = lanc16[...].astype(jnp.float32)
    chosen = lax.dot_general(
        pick[first : first + prod.shape[0], :],
        jnp.concatenate([own[...], other[...]], axis=0),
        (((1,), (0,)), ((), ())),
        preferred_element_type=jnp.float32,
    )
    value = chosen.reshape(-1, *lanc.shape) * lanc[None]
    prod[...] = value.reshape(chosen.shape).astype(jnp.bfloat16)


def first_kernel(pick, own, other, lanc16, eig, out, prod, acc):
    make_rows(prod, pick, own, other, lanc16, 0)
    dot_tiles(acc, prod[...], eig, 0)
    out[...] = acc[...].astype(out.dtype)


def send_kernel(cuts, pick, own, other, lanc16, half, eig_hbm, *rest):
    count = len(cuts) - 2
    outs, (prod, eig, acc, sem) = rest[:count], rest[count:]
    copies = []
    for cut, end in zip(cuts[1:], cuts[2:]):
        copies.append([])
        for at, size in tiles_of(end - cut):
            source = eig_hbm.at[pl.ds(cut + at, size)]
            target = eig.at[pl.ds(cut - cuts[1] + at, size)]
            copy = pltpu.make_async_copy(source, target, sem.at[sum(map(len, copies))])
            copy.start()
            copies[-1].append(copy)
    first = half.shape[0]
    prod[:first, :] = half[...]
    make_rows(prod.at[first:, :], pick, own, other, lanc16, first)
    for i, out in enumerate(outs):
        part = acc.at[:, : out.shape[1]]
        dot_tiles(part, rows_of(prod, i + 1, False), eig, cuts[i + 1] - cuts[1], copies[i])
        out[...] = part[...].astype(out.dtype)


def keep_kernel(p, first, prod, eig, out):
    dot_tiles(out, rows_of(prod, p, True), eig, first)


def add_kernel(kept, got, _, leave, keep):
    mid = leave.shape[0]
    leave[...] = (kept[:mid, :] + got[:mid, :].astype(jnp.float32)).astype(leave.dtype)
    keep[...] = kept[mid:, :] + got[mid:, :].astype(jnp.float32)


def finish_kernel(spans, *refs):
    count = len(spans)
    kept, came, out = refs[:count], refs[count : 2 * count], refs[-1]
    for (at, end), a, b in zip(spans, kept, came):
        out[:, at:end] = a[a.shape[0] - out.shape[0] :, :] + b[...].astype(jnp.float32)


VMEM_SPEC = pl.BlockSpec(memory_space=pltpu.VMEM)
SPECS = {
    True: pl.BlockSpec(memory_space=pltpu.HBM),
    False: VMEM_SPEC,
    None: pl.BlockSpec(memory_space=pl.ANY),
}


def kernel_call(body, ins, outs, scratch, cost):
    flops, moved = cost
    return pl.pallas_call(
        body,
        out_shape=[jax.ShapeDtypeStruct(*out) for out in outs],
        in_specs=[SPECS[far] for _, far in ins],
        out_specs=[VMEM_SPEC] * len(outs),
        scratch_shapes=scratch,
        compiler_params=pltpu.CompilerParams(vmem_limit_bytes=VMEM_LIMIT),
        cost_estimate=pl.CostEstimate(flops=flops, bytes_accessed=moved, transcendentals=0),
    )(
        *(
            pltpu.with_memory_space_constraint(x, pltpu.HBM) if far else x
            for x, far in ins
        )
    )


def per_device(n, eigvecs, lanczos, bands, band_order):
    cols, depth = eigvecs.shape
    lanc = lanczos.shape[0]
    per_chunk = band_order.shape[0] // n
    rows = band_order.shape[0] * lanc
    spans = split_columns(cols)
    cuts = [0] + [end for _, end in spans]
    widths = [end - at for at, end in spans]
    bf16 = jnp.bfloat16

    def exchange(value, p, stage):
        pairs = []
        for i in range(n):
            for core in range(2):
                bit = PLAN[p][1 + core][stage] if stage < 3 else stage
                pairs.append((2 * i + core, 2 * (i ^ (1 << bit)) + core))
        return lax.ppermute(value, ("grid", "eig"), pairs)

    def flops(width):
        return rows * width * depth

    other = lax.ppermute(bands, "eig", [(0, 1), (1, 0)])
    pick, own, lanc16, eig = kernel_call(
        functools.partial(setup_kernel, n, per_chunk, lanc, widths[0]),
        [(band_order, True), (bands, True), (lanczos, True), (eigvecs, True)],
        [
            ((rows, 2 * bands.shape[0]), bf16),
            (bands.shape, bf16),
            (lanczos.shape, bf16),
            ((widths[0], depth), bf16),
        ],
        [pltpu.SMEM(band_order.shape, jnp.int32), pltpu.SemaphoreType.DMA((4,))],
        (0, 2 * widths[0] * depth),
    )
    sources = [(x, False) for x in (pick, own, other, lanc16)]
    send, half = kernel_call(
        first_kernel,
        sources + [(eig, False)],
        [((rows // 2, widths[0]), bf16), ((rows // 2, depth), bf16)],
        [pltpu.VMEM((rows // 2, widths[0]), jnp.float32)],
        (flops(widths[0]), 2 * widths[0] * depth),
    )
    *sends, prod, eig_rest = kernel_call(
        functools.partial(send_kernel, cuts),
        sources + [(half, False), (eigvecs, True)],
        [((rows // 2, w), bf16) for w in widths[1:]]
        + [((rows, depth), bf16), ((cols - widths[0], depth), bf16)],
        [
            pltpu.VMEM((rows // 2, max(widths[1:])), jnp.float32),
            pltpu.SemaphoreType.DMA((sum(len(tiles_of(w)) for w in widths[1:]),)),
        ],
        (flops(sum(widths[1:])), 2 * sum(widths[1:]) * depth),
    )
    got = [exchange(s, p, 0) for p, s in enumerate([send, *sends])]
    value = []
    for p, width in enumerate(widths):
        value += kernel_call(
            functools.partial(keep_kernel, p, cuts[p] - cuts[min(p, 1)]),
            [(prod, False), (eig_rest if p else eig, False)],
            [((rows // 2, width), jnp.float32)],
            [],
            (flops(width), 2 * width * depth),
        )
    later = range(3, n.bit_length() - 1)
    token = prod
    for p, stage in ORDER + [(p, stage) for stage in later for p in range(len(PLAN))]:
        part = value[p].shape[0] // 2
        size = part * widths[p]
        leave, value[p] = kernel_call(
            add_kernel,
            [(value[p], False), (got[p], False), (token, None)],
            [((part, widths[p]), bf16 if stage < 3 else jnp.float32)]
            + [((part, widths[p]), jnp.float32)],
            [],
            (2 * size, 18 * size),
        )
        token = leave
        got[p] = exchange(leave, p, stage)
    outs = list(zip(value, got))
    (result,) = kernel_call(
        functools.partial(finish_kernel, spans),
        [(value, False) for value, _ in outs] + [(came, False) for _, came in outs],
        [((rows // n, cols), jnp.float32)],
        [],
        (rows // n * cols, 12 * rows // n * cols),
    )
    return result.reshape(per_chunk, lanc, cols)


def solution(mesh):
    in_specs = (
        P("eig", ("rep", "grid")),
        P(None, ("rep", "grid")),
        P("eig", ("rep", "grid")),
        P("rep"),
    )
    out_specs = P(("rep", "grid"), None, "eig")
    return jax.shard_map(
        functools.partial(per_device, mesh.shape["grid"]),
        mesh=mesh,
        in_specs=in_specs,
        out_specs=out_specs,
        check_vma=False,
    )
```

```python
import functools

import jax
import jax.numpy as jnp
from jax import lax
from jax.experimental import pallas as pl
from jax.experimental.pallas import tpu as pltpu
from jax.sharding import PartitionSpec as P

TILE = 256
VMEM_LIMIT = 32 * 1024 * 1024
X, NEAR, FAR = 0, 1, 2
PLAN = [
    (3.5, (NEAR, X, FAR), (X, FAR, NEAR)),
    (2, (X, NEAR, FAR), (NEAR, X, FAR)),
    (1.5, (X, NEAR, FAR), (X, NEAR, FAR)),
]
ORDER = [(piece, stage) for stage in (1, 2) for piece in range(len(PLAN))]


def ranked(bits, fixed=0):
    out = [fixed]
    for b in reversed(bits):
        out = [c | (1 << b) for c in out] + out
    return out


def split_columns(cols):
    unit = 128
    total = sum(plan[0] for plan in PLAN)
    ends, done = [], 0
    for share, *_ in PLAN[:-1]:
        done += share
        ends.append(int(round(cols * done / total / unit)) * unit)
    ends.append(cols)
    return list(zip([0] + ends[:-1], ends))


def halves(bits):
    keep = ranked(bits[1:])
    return keep, [c | (1 << bits[0]) for c in keep]


def places(p, core, kept):
    keep, leave = halves(PLAN[0][1 + core])
    return [(leave + keep).index(c) for c in halves(PLAN[p][1 + core])[0 if kept else 1]]


def rows_of(prod, p, kept):
    block = prod.shape[0] // 8
    core = lax.axis_index("eig")
    parts = []
    for a, b in zip(places(p, 0, kept), places(p, 1, kept)):
        at = a * block if a == b else pl.multiple_of(jnp.where(core == 0, a, b) * block, block)
        parts.append(prod[pl.ds(at, block), :])
    return jnp.concatenate(parts, axis=0)


def dot_tiles(out, rows, eig, first):
    width = out.shape[1]
    for at in range(0, width, TILE):
        size = min(TILE, width - at)
        out[:, at : at + size] = lax.dot_general(
            rows,
            eig[first + at : first + at + size, :],
            (((1,), (1,)), ((), ())),
            preferred_element_type=jnp.float32,
        )


def setup_kernel(n, per_chunk, lanc, width, order_hbm, own_hbm, lanc_hbm, eig_hbm, *rest):
    pick, own, lanc16, eig, order, sem = rest
    copies = [
        pltpu.make_async_copy(src, dst, sem.at[i])
        for i, (src, dst) in enumerate(
            [
                (order_hbm, order),
                (own_hbm, own),
                (lanc_hbm, lanc16),
                (eig_hbm.at[pl.ds(0, width)], eig),
            ]
        )
    ]
    for copy in copies:
        copy.start()
    me = lax.axis_index("grid")
    core = lax.axis_index("eig")
    bands = pick.shape[1]
    rest_bits = list(range(3, n.bit_length() - 1))
    classes = zip(*(sum(reversed(halves(PLAN[0][1 + i])), []) for i in range(2)))
    slots = []
    for pair in classes:
        for both in zip(*(ranked(rest_bits, c) for c in pair)):
            slots += [(both, j) for j in range(per_chunk)]
    col = lax.broadcasted_iota(jnp.int32, (2 * lanc, bands), 1)
    upper = lax.broadcasted_iota(jnp.int32, (2 * lanc, bands), 0) < lanc
    copies[0].wait()
    for i in range(0, len(slots), 2):
        want = []
        for r, j in slots[i : i + 2]:
            offset = jnp.where(core == 0, r[0], r[1])
            band = order[(me ^ offset) * per_chunk + j]
            want.append(lax.rem(band + core * (bands // 2), bands))
        hit = col == jnp.where(upper, want[0], want[1])
        pick[i * lanc : (i + 2) * lanc, :] = hit.astype(jnp.float32).astype(jnp.bfloat16)
    for copy in copies[1:]:
        copy.wait()


def make_rows(prod, pick, own, other, lanc16, first):
    lanc = lanc16[...].astype(jnp.float32)
    chosen = lax.dot_general(
        pick[first : first + prod.shape[0], :],
        jnp.concatenate([own[...], other[...]], axis=0),
        (((1,), (0,)), ((), ())),
        preferred_element_type=jnp.float32,
    )
    value = chosen.reshape(-1, *lanc.shape) * lanc[None]
    prod[...] = value.reshape(chosen.shape).astype(jnp.bfloat16)


def first_kernel(cut, pick, own, other, lanc16, eig, eig_hbm, out, prod, eig_next, acc, sem):
    copy = pltpu.make_async_copy(
        eig_hbm.at[pl.ds(cut, eig_next.shape[0])], eig_next, sem.at[0]
    )
    copy.start()
    make_rows(prod, pick, own, other, lanc16, 0)
    dot_tiles(acc, prod[...], eig, 0)
    out[...] = acc[...].astype(out.dtype)
    copy.wait()


def send_kernel(cut, pick, own, other, lanc16, half, eig, eig_hbm, *rest):
    *outs, prod, eig_rest, acc, sem = rest
    copy = pltpu.make_async_copy(
        eig_hbm.at[pl.ds(cut, eig_rest.shape[0])], eig_rest, sem.at[0]
    )
    copy.start()
    first = half.shape[0]
    prod[:first, :] = half[...]
    make_rows(prod.at[first:, :], pick, own, other, lanc16, first)
    at = 0
    for i, out in enumerate(outs):
        part = acc.at[:, : out.shape[1]]
        if i == 1:
            copy.wait()
        dot_tiles(part, rows_of(prod, i + 1, False), eig_rest if i else eig, at)
        out[...] = part[...].astype(out.dtype)
        at += out.shape[1] if i else 0


def keep_kernel(p, first, prod, eig, out):
    dot_tiles(out, rows_of(prod, p, True), eig, first)


def add_kernel(kept, got, _, leave, keep):
    mid = leave.shape[0]
    leave[...] = (kept[:mid, :] + got[:mid, :].astype(jnp.float32)).astype(leave.dtype)
    keep[...] = kept[mid:, :] + got[mid:, :].astype(jnp.float32)


def finish_kernel(spans, *refs):
    count = len(spans)
    kept, came, out = refs[:count], refs[count : 2 * count], refs[-1]
    for (at, end), a, b in zip(spans, kept, came):
        out[:, at:end] = a[a.shape[0] - out.shape[0] :, :] + b[...].astype(jnp.float32)


VMEM_SPEC = pl.BlockSpec(memory_space=pltpu.VMEM)
SPECS = {
    True: pl.BlockSpec(memory_space=pltpu.HBM),
    False: VMEM_SPEC,
    None: pl.BlockSpec(memory_space=pl.ANY),
}


def kernel_call(body, ins, outs, scratch, cost):
    flops, moved = cost
    return pl.pallas_call(
        body,
        out_shape=[jax.ShapeDtypeStruct(*out) for out in outs],
        in_specs=[SPECS[far] for _, far in ins],
        out_specs=[VMEM_SPEC] * len(outs),
        scratch_shapes=scratch,
        compiler_params=pltpu.CompilerParams(vmem_limit_bytes=VMEM_LIMIT),
        cost_estimate=pl.CostEstimate(flops=flops, bytes_accessed=moved, transcendentals=0),
    )(
        *(
            pltpu.with_memory_space_constraint(x, pltpu.HBM) if far else x
            for x, far in ins
        )
    )


def per_device(n, eigvecs, lanczos, bands, band_order):
    cols, depth = eigvecs.shape
    lanc = lanczos.shape[0]
    per_chunk = band_order.shape[0] // n
    rows = band_order.shape[0] * lanc
    spans = split_columns(cols)
    cuts = [0] + [end for _, end in spans]
    widths = [end - at for at, end in spans]
    bf16 = jnp.bfloat16

    def exchange(value, p, stage):
        pairs = []
        for i in range(n):
            for core in range(2):
                bit = PLAN[p][1 + core][stage] if stage < 3 else stage
                pairs.append((2 * i + core, 2 * (i ^ (1 << bit)) + core))
        return lax.ppermute(value, ("grid", "eig"), pairs)

    def flops(width):
        return rows * width * depth

    other = lax.ppermute(bands, "eig", [(0, 1), (1, 0)])
    pick, own, lanc16, eig = kernel_call(
        functools.partial(setup_kernel, n, per_chunk, lanc, widths[0]),
        [(band_order, True), (bands, True), (lanczos, True), (eigvecs, True)],
        [
            ((rows, 2 * bands.shape[0]), bf16),
            (bands.shape, bf16),
            (lanczos.shape, bf16),
            ((widths[0], depth), bf16),
        ],
        [pltpu.SMEM(band_order.shape, jnp.int32), pltpu.SemaphoreType.DMA((4,))],
        (0, 2 * widths[0] * depth),
    )
    sources = [(x, False) for x in (pick, own, other, lanc16)]
    send, half, eig_next = kernel_call(
        functools.partial(first_kernel, cuts[1]),
        sources + [(eig, False), (eigvecs, True)],
        [((rows // 2, widths[0]), bf16), ((rows // 2, depth), bf16), ((widths[1], depth), bf16)],
        [pltpu.VMEM((rows // 2, widths[0]), jnp.float32), pltpu.SemaphoreType.DMA((1,))],
        (flops(widths[0]), 2 * widths[0] * depth),
    )
    *sends, prod, eig_rest = kernel_call(
        functools.partial(send_kernel, cuts[2]),
        sources + [(half, False), (eig_next, False), (eigvecs, True)],
        [((rows // 2, w), bf16) for w in widths[1:]]
        + [((rows, depth), bf16), ((cols - cuts[2], depth), bf16)],
        [pltpu.VMEM((rows // 2, max(widths[1:])), jnp.float32), pltpu.SemaphoreType.DMA((1,))],
        (flops(sum(widths[1:])), 2 * sum(widths[1:]) * depth),
    )
    eigs = [eig, eig_next] + [eig_rest] * (len(PLAN) - 2)
    got = [exchange(s, p, 0) for p, s in enumerate([send, *sends])]
    value = []
    for p, width in enumerate(widths):
        value += kernel_call(
            functools.partial(keep_kernel, p, cuts[p] - cuts[min(p, 2)]),
            [(prod, False), (eigs[p], False)],
            [((rows // 2, width), jnp.float32)],
            [],
            (flops(width), 2 * width * depth),
        )
    later = range(3, n.bit_length() - 1)
    token = prod
    for p, stage in ORDER + [(p, stage) for stage in later for p in range(len(PLAN))]:
        part = value[p].shape[0] // 2
        size = part * widths[p]
        leave, value[p] = kernel_call(
            add_kernel,
            [(value[p], False), (got[p], False), (token, None)],
            [((part, widths[p]), bf16 if stage < 3 else jnp.float32)]
            + [((part, widths[p]), jnp.float32)],
            [],
            (2 * size, 18 * size),
        )
        token = leave
        got[p] = exchange(leave, p, stage)
    outs = list(zip(value, got))
    (result,) = kernel_call(
        functools.partial(finish_kernel, spans),
        [(value, False) for value, _ in outs] + [(came, False) for _, came in outs],
        [((rows // n, cols), jnp.float32)],
        [],
        (rows // n * cols, 12 * rows // n * cols),
    )
    return result.reshape(per_chunk, lanc, cols)


def solution(mesh):
    in_specs = (
        P("eig", ("rep", "grid")),
        P(None, ("rep", "grid")),
        P("eig", ("rep", "grid")),
        P("rep"),
    )
    out_specs = P(("rep", "grid"), None, "eig")
    return jax.shard_map(
        functools.partial(per_device, mesh.shape["grid"]),
        mesh=mesh,
        in_specs=in_specs,
        out_specs=out_specs,
        check_vma=False,
    )
```

```python
import functools

import jax
import jax.numpy as jnp
from jax import lax
from jax.experimental import pallas as pl
from jax.experimental.pallas import tpu as pltpu
from jax.sharding import PartitionSpec as P

TILE = 256
VMEM_LIMIT = 32 * 1024 * 1024
X, NEAR, FAR = 0, 1, 2
PLAN = [
    (3.5, (NEAR, X, FAR), (X, FAR, NEAR)),
    (2, (X, FAR, NEAR), (NEAR, X, FAR)),
    (1.5, (X, FAR, NEAR), (NEAR, X, FAR)),
]
ORDER = [(piece, stage) for stage in (1, 2) for piece in range(len(PLAN))]


def ranked(bits, fixed=0):
    out = [fixed]
    for b in reversed(bits):
        out = [c | (1 << b) for c in out] + out
    return out


def split_columns(cols):
    unit = 128
    total = sum(plan[0] for plan in PLAN)
    ends, done = [], 0
    for share, *_ in PLAN[:-1]:
        done += share
        ends.append(int(round(cols * done / total / unit)) * unit)
    ends.append(cols)
    return list(zip([0] + ends[:-1], ends))


def halves(bits):
    keep = ranked(bits[1:])
    return keep, [c | (1 << bits[0]) for c in keep]


def places(p, core, kept):
    keep, leave = halves(PLAN[0][1 + core])
    return [(leave + keep).index(c) for c in halves(PLAN[p][1 + core])[0 if kept else 1]]


def rows_of(prod, p, kept):
    block = prod.shape[0] // 8
    core = lax.axis_index("eig")
    parts = []
    for a, b in zip(places(p, 0, kept), places(p, 1, kept)):
        at = a * block if a == b else pl.multiple_of(jnp.where(core == 0, a, b) * block, block)
        parts.append(prod[pl.ds(at, block), :])
    return jnp.concatenate(parts, axis=0)


def dot_tiles(out, rows, eig, first):
    width = out.shape[1]
    for at in range(0, width, TILE):
        size = min(TILE, width - at)
        out[:, at : at + size] = lax.dot_general(
            rows,
            eig[first + at : first + at + size, :],
            (((1,), (1,)), ((), ())),
            preferred_element_type=jnp.float32,
        )


def setup_kernel(n, per_chunk, lanc, width, order_hbm, own_hbm, lanc_hbm, eig_hbm, *rest):
    pick, own, lanc16, eig, order, sem = rest
    copies = [
        pltpu.make_async_copy(src, dst, sem.at[i])
        for i, (src, dst) in enumerate(
            [
                (order_hbm, order),
                (own_hbm, own),
                (lanc_hbm, lanc16),
                (eig_hbm.at[pl.ds(0, width)], eig),
            ]
        )
    ]
    for copy in copies:
        copy.start()
    me = lax.axis_index("grid")
    core = lax.axis_index("eig")
    bands = pick.shape[1]
    rest_bits = list(range(3, n.bit_length() - 1))
    classes = zip(*(sum(reversed(halves(PLAN[0][1 + i])), []) for i in range(2)))
    slots = []
    for pair in classes:
        for both in zip(*(ranked(rest_bits, c) for c in pair)):
            slots += [(both, j) for j in range(per_chunk)]
    col = lax.broadcasted_iota(jnp.int32, (2 * lanc, bands), 1)
    upper = lax.broadcasted_iota(jnp.int32, (2 * lanc, bands), 0) < lanc
    copies[0].wait()
    for i in range(0, len(slots), 2):
        want = []
        for r, j in slots[i : i + 2]:
            offset = jnp.where(core == 0, r[0], r[1])
            band = order[(me ^ offset) * per_chunk + j]
            want.append(lax.rem(band + core * (bands // 2), bands))
        hit = col == jnp.where(upper, want[0], want[1])
        pick[i * lanc : (i + 2) * lanc, :] = hit.astype(jnp.float32).astype(jnp.bfloat16)
    for copy in copies[1:]:
        copy.wait()


def make_rows(prod, pick, own, other, lanc16, first):
    lanc = lanc16[...].astype(jnp.float32)
    chosen = lax.dot_general(
        pick[first : first + prod.shape[0], :],
        jnp.concatenate([own[...], other[...]], axis=0),
        (((1,), (0,)), ((), ())),
        preferred_element_type=jnp.float32,
    )
    value = chosen.reshape(-1, *lanc.shape) * lanc[None]
    prod[...] = value.reshape(chosen.shape).astype(jnp.bfloat16)


def first_kernel(cut, pick, own, other, lanc16, eig, eig_hbm, out, prod, eig_next, acc, sem):
    copy = pltpu.make_async_copy(
        eig_hbm.at[pl.ds(cut, eig_next.shape[0])], eig_next, sem.at[0]
    )
    copy.start()
    make_rows(prod, pick, own, other, lanc16, 0)
    dot_tiles(acc, prod[...], eig, 0)
    out[...] = acc[...].astype(out.dtype)
    copy.wait()


def send_kernel(cut, pick, own, other, lanc16, half, eig, eig_hbm, *rest):
    *outs, prod, eig_rest, acc, sem = rest
    copy = pltpu.make_async_copy(
        eig_hbm.at[pl.ds(cut, eig_rest.shape[0])], eig_rest, sem.at[0]
    )
    copy.start()
    first = half.shape[0]
    prod[:first, :] = half[...]
    make_rows(prod.at[first:, :], pick, own, other, lanc16, first)
    at = 0
    for i, out in enumerate(outs):
        part = acc.at[:, : out.shape[1]]
        if i == 1:
            copy.wait()
        dot_tiles(part, rows_of(prod, i + 1, False), eig_rest if i else eig, at)
        out[...] = part[...].astype(out.dtype)
        at += out.shape[1] if i else 0


def keep_kernel(p, first, prod, eig, out):
    dot_tiles(out, rows_of(prod, p, True), eig, first)


def add_kernel(kept, got, _, leave, keep):
    mid = leave.shape[0]
    leave[...] = (kept[:mid, :] + got[:mid, :].astype(jnp.float32)).astype(leave.dtype)
    keep[...] = kept[mid:, :] + got[mid:, :].astype(jnp.float32)


def finish_kernel(spans, *refs):
    count = len(spans)
    kept, came, out = refs[:count], refs[count : 2 * count], refs[-1]
    for (at, end), a, b in zip(spans, kept, came):
        out[:, at:end] = a[a.shape[0] - out.shape[0] :, :] + b[...].astype(jnp.float32)


VMEM_SPEC = pl.BlockSpec(memory_space=pltpu.VMEM)
SPECS = {
    True: pl.BlockSpec(memory_space=pltpu.HBM),
    False: VMEM_SPEC,
    None: pl.BlockSpec(memory_space=pl.ANY),
}


def kernel_call(body, ins, outs, scratch, cost):
    flops, moved = cost
    return pl.pallas_call(
        body,
        out_shape=[jax.ShapeDtypeStruct(*out) for out in outs],
        in_specs=[SPECS[far] for _, far in ins],
        out_specs=[VMEM_SPEC] * len(outs),
        scratch_shapes=scratch,
        compiler_params=pltpu.CompilerParams(vmem_limit_bytes=VMEM_LIMIT),
        cost_estimate=pl.CostEstimate(flops=flops, bytes_accessed=moved, transcendentals=0),
    )(
        *(
            pltpu.with_memory_space_constraint(x, pltpu.HBM) if far else x
            for x, far in ins
        )
    )


def per_device(n, eigvecs, lanczos, bands, band_order):
    cols, depth = eigvecs.shape
    lanc = lanczos.shape[0]
    per_chunk = band_order.shape[0] // n
    rows = band_order.shape[0] * lanc
    spans = split_columns(cols)
    cuts = [0] + [end for _, end in spans]
    widths = [end - at for at, end in spans]
    bf16 = jnp.bfloat16

    def exchange(value, p, stage):
        pairs = []
        for i in range(n):
            for core in range(2):
                bit = PLAN[p][1 + core][stage] if stage < 3 else stage
                pairs.append((2 * i + core, 2 * (i ^ (1 << bit)) + core))
        return lax.ppermute(value, ("grid", "eig"), pairs)

    def flops(width):
        return rows * width * depth

    other = lax.ppermute(bands, "eig", [(0, 1), (1, 0)])
    pick, own, lanc16, eig = kernel_call(
        functools.partial(setup_kernel, n, per_chunk, lanc, widths[0]),
        [(band_order, True), (bands, True), (lanczos, True), (eigvecs, True)],
        [
            ((rows, 2 * bands.shape[0]), bf16),
            (bands.shape, bf16),
            (lanczos.shape, bf16),
            ((widths[0], depth), bf16),
        ],
        [pltpu.SMEM(band_order.shape, jnp.int32), pltpu.SemaphoreType.DMA((4,))],
        (0, 2 * widths[0] * depth),
    )
    sources = [(x, False) for x in (pick, own, other, lanc16)]
    send, half, eig_next = kernel_call(
        functools.partial(first_kernel, cuts[1]),
        sources + [(eig, False), (eigvecs, True)],
        [((rows // 2, widths[0]), bf16), ((rows // 2, depth), bf16), ((widths[1], depth), bf16)],
        [pltpu.VMEM((rows // 2, widths[0]), jnp.float32), pltpu.SemaphoreType.DMA((1,))],
        (flops(widths[0]), 2 * widths[0] * depth),
    )
    *sends, prod, eig_rest = kernel_call(
        functools.partial(send_kernel, cuts[2]),
        sources + [(half, False), (eig_next, False), (eigvecs, True)],
        [((rows // 2, w), bf16) for w in widths[1:]]
        + [((rows, depth), bf16), ((cols - cuts[2], depth), bf16)],
        [pltpu.VMEM((rows // 2, max(widths[1:])), jnp.float32), pltpu.SemaphoreType.DMA((1,))],
        (flops(sum(widths[1:])), 2 * sum(widths[1:]) * depth),
    )
    eigs = [eig, eig_next] + [eig_rest] * (len(PLAN) - 2)
    got = [exchange(s, p, 0) for p, s in enumerate([send, *sends])]
    value = []
    for p, width in enumerate(widths):
        value += kernel_call(
            functools.partial(keep_kernel, p, cuts[p] - cuts[min(p, 2)]),
            [(prod, False), (eigs[p], False)],
            [((rows // 2, width), jnp.float32)],
            [],
            (flops(width), 2 * width * depth),
        )
    later = range(3, n.bit_length() - 1)
    token = prod
    for p, stage in ORDER + [(p, stage) for stage in later for p in range(len(PLAN))]:
        part = value[p].shape[0] // 2
        size = part * widths[p]
        leave, value[p] = kernel_call(
            add_kernel,
            [(value[p], False), (got[p], False), (token, None)],
            [((part, widths[p]), bf16 if stage < 3 else jnp.float32)]
            + [((part, widths[p]), jnp.float32)],
            [],
            (2 * size, 18 * size),
        )
        token = leave
        got[p] = exchange(leave, p, stage)
    outs = list(zip(value, got))
    (result,) = kernel_call(
        functools.partial(finish_kernel, spans),
        [(value, False) for value, _ in outs] + [(came, False) for _, came in outs],
        [((rows // n, cols), jnp.float32)],
        [],
        (rows // n * cols, 12 * rows // n * cols),
    )
    return result.reshape(per_chunk, lanc, cols)


def solution(mesh):
    in_specs = (
        P("eig", ("rep", "grid")),
        P(None, ("rep", "grid")),
        P("eig", ("rep", "grid")),
        P("rep"),
    )
    out_specs = P(("rep", "grid"), None, "eig")
    return jax.shard_map(
        functools.partial(per_device, mesh.shape["grid"]),
        mesh=mesh,
        in_specs=in_specs,
        out_specs=out_specs,
        check_vma=False,
    )
```

```python
import functools

import jax
import jax.numpy as jnp
from jax import lax
from jax.experimental import pallas as pl
from jax.experimental.pallas import tpu as pltpu
from jax.sharding import PartitionSpec as P

TILE = 256
VMEM_LIMIT = 32 * 1024 * 1024
X, NEAR, FAR = 0, 1, 2
PLAN = [
    (2, (NEAR, X, FAR), (X, NEAR, FAR)),
    (2, (X, NEAR, FAR), (NEAR, X, FAR)),
    (2, (NEAR, X, FAR), (X, NEAR, FAR)),
    (1, (X, NEAR, FAR), (X, NEAR, FAR)),
]
ORDER = [(1, 0), (2, 0), (0, 1), (1, 1), (3, 0), (0, 2), (2, 1), (1, 2), (3, 1)]
ORDER += [(0, 3), (2, 2), (1, 3), (3, 2)]


def ranked(bits, fixed=0):
    out = [fixed]
    for b in reversed(bits):
        out = [c | (1 << b) for c in out] + out
    return out


def split_columns(cols):
    unit = 128
    total = sum(plan[0] for plan in PLAN)
    ends, done = [], 0
    for share, *_ in PLAN[:-1]:
        done += share
        ends.append(int(round(cols * done / total / unit)) * unit)
    ends.append(cols)
    return list(zip([0] + ends[:-1], ends))


def halves(bits):
    keep = ranked(bits[1:])
    return keep, [c | (1 << bits[0]) for c in keep]


def places(p, core, kept):
    keep, leave = halves(PLAN[0][1 + core])
    return [(leave + keep).index(c) for c in halves(PLAN[p][1 + core])[0 if kept else 1]]


def rows_of(prod, p, kept):
    block = prod.shape[0] // 8
    core = lax.axis_index("eig")
    parts = []
    for a, b in zip(places(p, 0, kept), places(p, 1, kept)):
        at = a * block if a == b else pl.multiple_of(jnp.where(core == 0, a, b) * block, block)
        parts.append(prod[pl.ds(at, block), :])
    return jnp.concatenate(parts, axis=0)


def dot_tiles(out, rows, eig, first):
    width = out.shape[1]
    for at in range(0, width, TILE):
        size = min(TILE, width - at)
        out[:, at : at + size] = lax.dot_general(
            rows,
            eig[first + at : first + at + size, :],
            (((1,), (1,)), ((), ())),
            preferred_element_type=jnp.float32,
        )


def setup_kernel(n, per_chunk, lanc, width, order_hbm, own_hbm, lanc_hbm, eig_hbm, *rest):
    pick, own, lanc16, eig, order, sem = rest
    copies = [
        pltpu.make_async_copy(src, dst, sem.at[i])
        for i, (src, dst) in enumerate(
            [
                (order_hbm, order),
                (own_hbm, own),
                (lanc_hbm, lanc16),
                (eig_hbm.at[pl.ds(0, width)], eig),
            ]
        )
    ]
    for copy in copies:
        copy.start()
    me = lax.axis_index("grid")
    core = lax.axis_index("eig")
    bands = pick.shape[1]
    rest_bits = list(range(3, n.bit_length() - 1))
    classes = zip(*(sum(reversed(halves(PLAN[0][1 + i])), []) for i in range(2)))
    slots = []
    for pair in classes:
        for both in zip(*(ranked(rest_bits, c) for c in pair)):
            slots += [(both, j) for j in range(per_chunk)]
    col = lax.broadcasted_iota(jnp.int32, (2 * lanc, bands), 1)
    upper = lax.broadcasted_iota(jnp.int32, (2 * lanc, bands), 0) < lanc
    copies[0].wait()
    for i in range(0, len(slots), 2):
        want = []
        for r, j in slots[i : i + 2]:
            offset = jnp.where(core == 0, r[0], r[1])
            band = order[(me ^ offset) * per_chunk + j]
            want.append(lax.rem(band + core * (bands // 2), bands))
        hit = col == jnp.where(upper, want[0], want[1])
        pick[i * lanc : (i + 2) * lanc, :] = hit.astype(jnp.float32).astype(jnp.bfloat16)
    for copy in copies[1:]:
        copy.wait()


def make_rows(prod, pick, own, other, lanc16, first):
    lanc = lanc16[...].astype(jnp.float32)
    chosen = lax.dot_general(
        pick[first : first + prod.shape[0], :],
        jnp.concatenate([own[...], other[...]], axis=0),
        (((1,), (0,)), ((), ())),
        preferred_element_type=jnp.float32,
    )
    value = chosen.reshape(-1, *lanc.shape) * lanc[None]
    prod[...] = value.reshape(chosen.shape).astype(jnp.bfloat16)


def first_kernel(cut, pick, own, other, lanc16, eig, eig_hbm, out, prod, eig_next, acc, sem):
    copy = pltpu.make_async_copy(
        eig_hbm.at[pl.ds(cut, eig_next.shape[0])], eig_next, sem.at[0]
    )
    copy.start()
    make_rows(prod, pick, own, other, lanc16, 0)
    dot_tiles(acc, prod[...], eig, 0)
    out[...] = acc[...].astype(out.dtype)
    copy.wait()


def second_kernel(cut, pick, own, other, lanc16, half, eig, eig_hbm, out, prod, eig_next, acc, sem):
    copy = pltpu.make_async_copy(
        eig_hbm.at[pl.ds(cut, eig_next.shape[0])], eig_next, sem.at[0]
    )
    copy.start()
    first = half.shape[0]
    prod[:first, :] = half[...]
    make_rows(prod.at[first:, :], pick, own, other, lanc16, first)
    dot_tiles(acc, rows_of(prod, 1, False), eig, 0)
    out[...] = acc[...].astype(out.dtype)
    copy.wait()


def send_kernel(p, first, prod, eig, _, out, acc):
    dot_tiles(acc, rows_of(prod, p, False), eig, first)
    out[...] = acc[...].astype(out.dtype)


def keep_kernel(p, first, prod, eig, out):
    dot_tiles(out, rows_of(prod, p, True), eig, first)


def add_kernel(kept, got, _, leave, keep):
    mid = leave.shape[0]
    leave[...] = (kept[:mid, :] + got[:mid, :].astype(jnp.float32)).astype(leave.dtype)
    keep[...] = kept[mid:, :] + got[mid:, :].astype(jnp.float32)


def last_kernel(kept, got, _, out):
    out[...] = kept[...] + got[...].astype(jnp.float32)


def finish_kernel(spans, *refs):
    refs, out = list(refs[:-1]), refs[-1]
    for p, (at, end) in enumerate(spans):
        value = refs.pop(0)[...]
        if (p, 3) not in ORDER:
            value += refs.pop(0)[...].astype(jnp.float32)
        out[:, at:end] = value


VMEM_SPEC = pl.BlockSpec(memory_space=pltpu.VMEM)
SPECS = {
    True: pl.BlockSpec(memory_space=pltpu.HBM),
    False: VMEM_SPEC,
    None: pl.BlockSpec(memory_space=pl.ANY),
}


def kernel_call(body, ins, outs, scratch, cost):
    flops, moved = cost
    return pl.pallas_call(
        body,
        out_shape=[jax.ShapeDtypeStruct(*out) for out in outs],
        in_specs=[SPECS[far] for _, far in ins],
        out_specs=[VMEM_SPEC] * len(outs),
        scratch_shapes=scratch,
        compiler_params=pltpu.CompilerParams(vmem_limit_bytes=VMEM_LIMIT),
        cost_estimate=pl.CostEstimate(flops=flops, bytes_accessed=moved, transcendentals=0),
    )(
        *(
            pltpu.with_memory_space_constraint(x, pltpu.HBM) if far else x
            for x, far in ins
        )
    )


def per_device(n, eigvecs, lanczos, bands, band_order):
    cols, depth = eigvecs.shape
    lanc = lanczos.shape[0]
    per_chunk = band_order.shape[0] // n
    rows = band_order.shape[0] * lanc
    spans = split_columns(cols)
    cuts = [0] + [end for _, end in spans]
    widths = [end - at for at, end in spans]
    bf16 = jnp.bfloat16

    def exchange(value, p, stage):
        pairs = []
        for i in range(n):
            for core in range(2):
                bit = PLAN[p][1 + core][stage] if stage < 3 else stage
                pairs.append((2 * i + core, 2 * (i ^ (1 << bit)) + core))
        return lax.ppermute(value, ("grid", "eig"), pairs)

    def flops(width):
        return rows * width * depth

    other = lax.ppermute(bands, "eig", [(0, 1), (1, 0)])
    pick, own, lanc16, eig = kernel_call(
        functools.partial(setup_kernel, n, per_chunk, lanc, widths[0]),
        [(band_order, True), (bands, True), (lanczos, True), (eigvecs, True)],
        [
            ((rows, 2 * bands.shape[0]), bf16),
            (bands.shape, bf16),
            (lanczos.shape, bf16),
            ((widths[0], depth), bf16),
        ],
        [pltpu.SMEM(band_order.shape, jnp.int32), pltpu.SemaphoreType.DMA((4,))],
        (0, 2 * widths[0] * depth),
    )
    sources = [(x, False) for x in (pick, own, other, lanc16)]
    send, half, eig_next = kernel_call(
        functools.partial(first_kernel, cuts[1]),
        sources + [(eig, False), (eigvecs, True)],
        [((rows // 2, widths[0]), bf16), ((rows // 2, depth), bf16), ((widths[1], depth), bf16)],
        [pltpu.VMEM((rows // 2, widths[0]), jnp.float32), pltpu.SemaphoreType.DMA((1,))],
        (flops(widths[0]), 2 * widths[0] * depth),
    )
    second, prod, eig_rest = kernel_call(
        functools.partial(second_kernel, cuts[2]),
        sources + [(half, False), (eig_next, False), (eigvecs, True)],
        [((rows // 2, widths[1]), bf16), ((rows, depth), bf16), ((cols - cuts[2], depth), bf16)],
        [pltpu.VMEM((rows // 2, widths[1]), jnp.float32), pltpu.SemaphoreType.DMA((1,))],
        (flops(widths[1]), 2 * (cols - cuts[2]) * depth),
    )
    eigs = [eig, eig_next] + [eig_rest] * (len(PLAN) - 2)
    got = {0: exchange(send, 0, 0)}
    value = []
    for p, width in enumerate(widths):
        value += kernel_call(
            functools.partial(keep_kernel, p, cuts[p] - cuts[min(p, 2)]),
            [(prod, False), (eigs[p], False)],
            [((rows // 2, width), jnp.float32)],
            [],
            (flops(width), 2 * width * depth),
        )
    later = range(3, n.bit_length() - 1)
    token = prod
    events = [(p, stage) for p, stage in ORDER if stage < 3]
    events += [(p, stage) for stage in later for p in range(len(PLAN))]
    if not later:
        events = ORDER
    for p, stage in events:
        part = rows // 2 >> stage
        size = part * widths[p]
        if (p, stage) == (1, 0):
            leave = second
        elif stage == 0:
            (leave,) = kernel_call(
                functools.partial(send_kernel, p, cuts[p] - cuts[2]),
                [(prod, False), (eig_rest, False), (token, None)],
                [((part, widths[p]), bf16)],
                [pltpu.VMEM((part, widths[p]), jnp.float32)],
                (flops(widths[p]), 2 * widths[p] * depth),
            )
        elif stage == 3 and not later:
            (value[p],) = kernel_call(
                last_kernel,
                [(value[p], False), (got[p], False), (token, None)],
                [((rows // n, widths[p]), jnp.float32)],
                [],
                (size, 10 * size),
            )
            token = value[p]
            continue
        else:
            leave, value[p] = kernel_call(
                add_kernel,
                [(value[p], False), (got[p], False), (token, None)],
                [((part, widths[p]), bf16 if stage < 3 else jnp.float32)]
                + [((part, widths[p]), jnp.float32)],
                [],
                (2 * size, 18 * size),
            )
        token = leave
        got[p] = exchange(leave, p, stage)
    for p in range(len(PLAN)):
        if later and (p, 3) in ORDER:
            value[p] += got[p]
    parts = []
    for p in range(len(PLAN)):
        parts += [value[p]] if (p, 3) in ORDER else [value[p], got[p]]
    (result,) = kernel_call(
        functools.partial(finish_kernel, spans),
        [(part, False) for part in parts],
        [((rows // n, cols), jnp.float32)],
        [],
        (rows // n * cols, 12 * rows // n * cols),
    )
    return result.reshape(per_chunk, lanc, cols)


def solution(mesh):
    in_specs = (
        P("eig", ("rep", "grid")),
        P(None, ("rep", "grid")),
        P("eig", ("rep", "grid")),
        P("rep"),
    )
    out_specs = P(("rep", "grid"), None, "eig")
    return jax.shard_map(
        functools.partial(per_device, mesh.shape["grid"]),
        mesh=mesh,
        in_specs=in_specs,
        out_specs=out_specs,
        check_vma=False,
    )
```

```python
import functools

import jax
import jax.numpy as jnp
from jax import lax
from jax.experimental import pallas as pl
from jax.experimental.pallas import tpu as pltpu
from jax.sharding import PartitionSpec as P

TILE = 256
VMEM_LIMIT = 32 * 1024 * 1024
X, NEAR, FAR = 0, 1, 2
PLAN = [
    (3.5, (NEAR, X, FAR), (X, FAR, NEAR)),
    (2, (X, NEAR, FAR), (FAR, X, NEAR)),
    (1.5, (NEAR, X, FAR), (X, FAR, NEAR)),
]
ORDER = [(piece, stage) for stage in (1, 2) for piece in range(len(PLAN))]


def ranked(bits, fixed=0):
    out = [fixed]
    for b in reversed(bits):
        out = [c | (1 << b) for c in out] + out
    return out


def split_columns(cols):
    unit = 128
    total = sum(plan[0] for plan in PLAN)
    ends, done = [], 0
    for share, *_ in PLAN[:-1]:
        done += share
        ends.append(int(round(cols * done / total / unit)) * unit)
    ends.append(cols)
    return list(zip([0] + ends[:-1], ends))


def halves(bits):
    keep = ranked(bits[1:])
    return keep, [c | (1 << bits[0]) for c in keep]


def places(p, core, kept):
    keep, leave = halves(PLAN[0][1 + core])
    return [(leave + keep).index(c) for c in halves(PLAN[p][1 + core])[0 if kept else 1]]


def rows_of(prod, p, kept):
    block = prod.shape[0] // 8
    core = lax.axis_index("eig")
    parts = []
    for a, b in zip(places(p, 0, kept), places(p, 1, kept)):
        at = a * block if a == b else pl.multiple_of(jnp.where(core == 0, a, b) * block, block)
        parts.append(prod[pl.ds(at, block), :])
    return jnp.concatenate(parts, axis=0)


def dot_tiles(out, rows, eig, first):
    width = out.shape[1]
    for at in range(0, width, TILE):
        size = min(TILE, width - at)
        out[:, at : at + size] = lax.dot_general(
            rows,
            eig[first + at : first + at + size, :],
            (((1,), (1,)), ((), ())),
            preferred_element_type=jnp.float32,
        )


def setup_kernel(n, per_chunk, lanc, width, order_hbm, own_hbm, lanc_hbm, eig_hbm, *rest):
    pick, own, lanc16, eig, order, sem = rest
    copies = [
        pltpu.make_async_copy(src, dst, sem.at[i])
        for i, (src, dst) in enumerate(
            [
                (order_hbm, order),
                (own_hbm, own),
                (lanc_hbm, lanc16),
                (eig_hbm.at[pl.ds(0, width)], eig),
            ]
        )
    ]
    for copy in copies:
        copy.start()
    me = lax.axis_index("grid")
    core = lax.axis_index("eig")
    bands = pick.shape[1]
    rest_bits = list(range(3, n.bit_length() - 1))
    classes = zip(*(sum(reversed(halves(PLAN[0][1 + i])), []) for i in range(2)))
    slots = []
    for pair in classes:
        for both in zip(*(ranked(rest_bits, c) for c in pair)):
            slots += [(both, j) for j in range(per_chunk)]
    col = lax.broadcasted_iota(jnp.int32, (2 * lanc, bands), 1)
    upper = lax.broadcasted_iota(jnp.int32, (2 * lanc, bands), 0) < lanc
    copies[0].wait()
    for i in range(0, len(slots), 2):
        want = []
        for r, j in slots[i : i + 2]:
            offset = jnp.where(core == 0, r[0], r[1])
            band = order[(me ^ offset) * per_chunk + j]
            want.append(lax.rem(band + core * (bands // 2), bands))
        hit = col == jnp.where(upper, want[0], want[1])
        pick[i * lanc : (i + 2) * lanc, :] = hit.astype(jnp.float32).astype(jnp.bfloat16)
    for copy in copies[1:]:
        copy.wait()


def make_rows(prod, pick, own, other, lanc16, first):
    lanc = lanc16[...].astype(jnp.float32)
    chosen = lax.dot_general(
        pick[first : first + prod.shape[0], :],
        jnp.concatenate([own[...], other[...]], axis=0),
        (((1,), (0,)), ((), ())),
        preferred_element_type=jnp.float32,
    )
    value = chosen.reshape(-1, *lanc.shape) * lanc[None]
    prod[...] = value.reshape(chosen.shape).astype(jnp.bfloat16)


def first_kernel(cut, pick, own, other, lanc16, eig, eig_hbm, out, prod, eig_next, acc, sem):
    copy = pltpu.make_async_copy(
        eig_hbm.at[pl.ds(cut, eig_next.shape[0])], eig_next, sem.at[0]
    )
    copy.start()
    make_rows(prod, pick, own, other, lanc16, 0)
    dot_tiles(acc, prod[...], eig, 0)
    out[...] = acc[...].astype(out.dtype)
    copy.wait()


def send_kernel(cut, pick, own, other, lanc16, half, eig, eig_hbm, *rest):
    *outs, prod, eig_rest, acc, sem = rest
    copy = pltpu.make_async_copy(
        eig_hbm.at[pl.ds(cut, eig_rest.shape[0])], eig_rest, sem.at[0]
    )
    copy.start()
    first = half.shape[0]
    prod[:first, :] = half[...]
    make_rows(prod.at[first:, :], pick, own, other, lanc16, first)
    at = 0
    for i, out in enumerate(outs):
        part = acc.at[:, : out.shape[1]]
        if i == 1:
            copy.wait()
        dot_tiles(part, rows_of(prod, i + 1, False), eig_rest if i else eig, at)
        out[...] = part[...].astype(out.dtype)
        at += out.shape[1] if i else 0


def keep_kernel(p, first, prod, eig, out):
    dot_tiles(out, rows_of(prod, p, True), eig, first)


def add_kernel(kept, got, _, leave, keep):
    mid = leave.shape[0]
    leave[...] = (kept[:mid, :] + got[:mid, :].astype(jnp.float32)).astype(leave.dtype)
    keep[...] = kept[mid:, :] + got[mid:, :].astype(jnp.float32)


def finish_kernel(spans, *refs):
    count = len(spans)
    kept, came, out = refs[:count], refs[count : 2 * count], refs[-1]
    for (at, end), a, b in zip(spans, kept, came):
        out[:, at:end] = a[a.shape[0] - out.shape[0] :, :] + b[...].astype(jnp.float32)


VMEM_SPEC = pl.BlockSpec(memory_space=pltpu.VMEM)
SPECS = {
    True: pl.BlockSpec(memory_space=pltpu.HBM),
    False: VMEM_SPEC,
    None: pl.BlockSpec(memory_space=pl.ANY),
}


def kernel_call(body, ins, outs, scratch, cost):
    flops, moved = cost
    return pl.pallas_call(
        body,
        out_shape=[jax.ShapeDtypeStruct(*out) for out in outs],
        in_specs=[SPECS[far] for _, far in ins],
        out_specs=[VMEM_SPEC] * len(outs),
        scratch_shapes=scratch,
        compiler_params=pltpu.CompilerParams(vmem_limit_bytes=VMEM_LIMIT),
        cost_estimate=pl.CostEstimate(flops=flops, bytes_accessed=moved, transcendentals=0),
    )(
        *(
            pltpu.with_memory_space_constraint(x, pltpu.HBM) if far else x
            for x, far in ins
        )
    )


def per_device(n, eigvecs, lanczos, bands, band_order):
    cols, depth = eigvecs.shape
    lanc = lanczos.shape[0]
    per_chunk = band_order.shape[0] // n
    rows = band_order.shape[0] * lanc
    spans = split_columns(cols)
    cuts = [0] + [end for _, end in spans]
    widths = [end - at for at, end in spans]
    bf16 = jnp.bfloat16

    def exchange(value, p, stage):
        pairs = []
        for i in range(n):
            for core in range(2):
                bit = PLAN[p][1 + core][stage] if stage < 3 else stage
                pairs.append((2 * i + core, 2 * (i ^ (1 << bit)) + core))
        return lax.ppermute(value, ("grid", "eig"), pairs)

    def flops(width):
        return rows * width * depth

    other = lax.ppermute(bands, "eig", [(0, 1), (1, 0)])
    pick, own, lanc16, eig = kernel_call(
        functools.partial(setup_kernel, n, per_chunk, lanc, widths[0]),
        [(band_order, True), (bands, True), (lanczos, True), (eigvecs, True)],
        [
            ((rows, 2 * bands.shape[0]), bf16),
            (bands.shape, bf16),
            (lanczos.shape, bf16),
            ((widths[0], depth), bf16),
        ],
        [pltpu.SMEM(band_order.shape, jnp.int32), pltpu.SemaphoreType.DMA((4,))],
        (0, 2 * widths[0] * depth),
    )
    sources = [(x, False) for x in (pick, own, other, lanc16)]
    send, half, eig_next = kernel_call(
        functools.partial(first_kernel, cuts[1]),
        sources + [(eig, False), (eigvecs, True)],
        [((rows // 2, widths[0]), bf16), ((rows // 2, depth), bf16), ((widths[1], depth), bf16)],
        [pltpu.VMEM((rows // 2, widths[0]), jnp.float32), pltpu.SemaphoreType.DMA((1,))],
        (flops(widths[0]), 2 * widths[0] * depth),
    )
    *sends, prod, eig_rest = kernel_call(
        functools.partial(send_kernel, cuts[2]),
        sources + [(half, False), (eig_next, False), (eigvecs, True)],
        [((rows // 2, w), bf16) for w in widths[1:]]
        + [((rows, depth), bf16), ((cols - cuts[2], depth), bf16)],
        [pltpu.VMEM((rows // 2, max(widths[1:])), jnp.float32), pltpu.SemaphoreType.DMA((1,))],
        (flops(sum(widths[1:])), 2 * sum(widths[1:]) * depth),
    )
    eigs = [eig, eig_next] + [eig_rest] * (len(PLAN) - 2)
    got = [exchange(s, p, 0) for p, s in enumerate([send, *sends])]
    value = []
    for p, width in enumerate(widths):
        value += kernel_call(
            functools.partial(keep_kernel, p, cuts[p] - cuts[min(p, 2)]),
            [(prod, False), (eigs[p], False)],
            [((rows // 2, width), jnp.float32)],
            [],
            (flops(width), 2 * width * depth),
        )
    later = range(3, n.bit_length() - 1)
    token = prod
    for p, stage in ORDER + [(p, stage) for stage in later for p in range(len(PLAN))]:
        part = value[p].shape[0] // 2
        size = part * widths[p]
        leave, value[p] = kernel_call(
            add_kernel,
            [(value[p], False), (got[p], False), (token, None)],
            [((part, widths[p]), bf16 if stage < 3 else jnp.float32)]
            + [((part, widths[p]), jnp.float32)],
            [],
            (2 * size, 18 * size),
        )
        token = leave
        got[p] = exchange(leave, p, stage)
    outs = list(zip(value, got))
    (result,) = kernel_call(
        functools.partial(finish_kernel, spans),
        [(value, False) for value, _ in outs] + [(came, False) for _, came in outs],
        [((rows // n, cols), jnp.float32)],
        [],
        (rows // n * cols, 12 * rows // n * cols),
    )
    return result.reshape(per_chunk, lanc, cols)


def solution(mesh):
    in_specs = (
        P("eig", ("rep", "grid")),
        P(None, ("rep", "grid")),
        P("eig", ("rep", "grid")),
        P("rep"),
    )
    out_specs = P(("rep", "grid"), None, "eig")
    return jax.shard_map(
        functools.partial(per_device, mesh.shape["grid"]),
        mesh=mesh,
        in_specs=in_specs,
        out_specs=out_specs,
        check_vma=False,
    )
```

```python
import functools

import jax
import jax.numpy as jnp
from jax import lax
from jax.experimental import pallas as pl
from jax.experimental.pallas import tpu as pltpu
from jax.sharding import PartitionSpec as P

TILE = 256
VMEM_LIMIT = 32 * 1024 * 1024
X, NEAR, FAR = 0, 1, 2
PLAN = [
    (3, (NEAR, X, FAR), (X, FAR, NEAR)),
    (2, (X, NEAR, FAR), (FAR, X, NEAR)),
    (2, (NEAR, X, FAR), (X, FAR, NEAR)),
]
ORDER = [(piece, stage) for stage in (1, 2) for piece in range(len(PLAN))]


def ranked(bits, fixed=0):
    out = [fixed]
    for b in reversed(bits):
        out = [c | (1 << b) for c in out] + out
    return out


def split_columns(cols):
    unit = 128
    total = sum(plan[0] for plan in PLAN)
    ends, done = [], 0
    for share, *_ in PLAN[:-1]:
        done += share
        ends.append(int(round(cols * done / total / unit)) * unit)
    ends.append(cols)
    return list(zip([0] + ends[:-1], ends))


def halves(bits):
    keep = ranked(bits[1:])
    return keep, [c | (1 << bits[0]) for c in keep]


def places(p, core, kept):
    keep, leave = halves(PLAN[0][1 + core])
    return [(leave + keep).index(c) for c in halves(PLAN[p][1 + core])[0 if kept else 1]]


def rows_of(prod, p, kept):
    block = prod.shape[0] // 8
    core = lax.axis_index("eig")
    parts = []
    for a, b in zip(places(p, 0, kept), places(p, 1, kept)):
        at = a * block if a == b else pl.multiple_of(jnp.where(core == 0, a, b) * block, block)
        parts.append(prod[pl.ds(at, block), :])
    return jnp.concatenate(parts, axis=0)


def dot_tiles(out, rows, eig, first):
    width = out.shape[1]
    for at in range(0, width, TILE):
        size = min(TILE, width - at)
        out[:, at : at + size] = lax.dot_general(
            rows,
            eig[first + at : first + at + size, :],
            (((1,), (1,)), ((), ())),
            preferred_element_type=jnp.float32,
        )


def setup_kernel(n, per_chunk, lanc, width, order_hbm, own_hbm, lanc_hbm, eig_hbm, *rest):
    pick, own, lanc16, eig, order, sem = rest
    copies = [
        pltpu.make_async_copy(src, dst, sem.at[i])
        for i, (src, dst) in enumerate(
            [
                (order_hbm, order),
                (own_hbm, own),
                (lanc_hbm, lanc16),
                (eig_hbm.at[pl.ds(0, width)], eig),
            ]
        )
    ]
    for copy in copies:
        copy.start()
    me = lax.axis_index("grid")
    core = lax.axis_index("eig")
    bands = pick.shape[1]
    rest_bits = list(range(3, n.bit_length() - 1))
    classes = zip(*(sum(reversed(halves(PLAN[0][1 + i])), []) for i in range(2)))
    slots = []
    for pair in classes:
        for both in zip(*(ranked(rest_bits, c) for c in pair)):
            slots += [(both, j) for j in range(per_chunk)]
    col = lax.broadcasted_iota(jnp.int32, (2 * lanc, bands), 1)
    upper = lax.broadcasted_iota(jnp.int32, (2 * lanc, bands), 0) < lanc
    copies[0].wait()
    for i in range(0, len(slots), 2):
        want = []
        for r, j in slots[i : i + 2]:
            offset = jnp.where(core == 0, r[0], r[1])
            band = order[(me ^ offset) * per_chunk + j]
            want.append(lax.rem(band + core * (bands // 2), bands))
        hit = col == jnp.where(upper, want[0], want[1])
        pick[i * lanc : (i + 2) * lanc, :] = hit.astype(jnp.float32).astype(jnp.bfloat16)
    for copy in copies[1:]:
        copy.wait()


def make_rows(prod, pick, own, other, lanc16, first):
    lanc = lanc16[...].astype(jnp.float32)
    chosen = lax.dot_general(
        pick[first : first + prod.shape[0], :],
        jnp.concatenate([own[...], other[...]], axis=0),
        (((1,), (0,)), ((), ())),
        preferred_element_type=jnp.float32,
    )
    value = chosen.reshape(-1, *lanc.shape) * lanc[None]
    prod[...] = value.reshape(chosen.shape).astype(jnp.bfloat16)


def first_kernel(cut, pick, own, other, lanc16, eig, eig_hbm, out, prod, eig_next, acc, sem):
    copy = pltpu.make_async_copy(
        eig_hbm.at[pl.ds(cut, eig_next.shape[0])], eig_next, sem.at[0]
    )
    copy.start()
    make_rows(prod, pick, own, other, lanc16, 0)
    dot_tiles(acc, prod[...], eig, 0)
    out[...] = acc[...].astype(out.dtype)
    copy.wait()


def send_kernel(cut, pick, own, other, lanc16, half, eig, eig_hbm, *rest):
    *outs, prod, eig_rest, acc, sem = rest
    copy = pltpu.make_async_copy(
        eig_hbm.at[pl.ds(cut, eig_rest.shape[0])], eig_rest, sem.at[0]
    )
    copy.start()
    first = half.shape[0]
    prod[:first, :] = half[...]
    make_rows(prod.at[first:, :], pick, own, other, lanc16, first)
    at = 0
    for i, out in enumerate(outs):
        part = acc.at[:, : out.shape[1]]
        if i == 1:
            copy.wait()
        dot_tiles(part, rows_of(prod, i + 1, False), eig_rest if i else eig, at)
        out[...] = part[...].astype(out.dtype)
        at += out.shape[1] if i else 0


def keep_kernel(p, first, prod, eig, out):
    dot_tiles(out, rows_of(prod, p, True), eig, first)


def add_kernel(kept, got, _, leave, keep):
    mid = leave.shape[0]
    leave[...] = (kept[:mid, :] + got[:mid, :].astype(jnp.float32)).astype(leave.dtype)
    keep[...] = kept[mid:, :] + got[mid:, :].astype(jnp.float32)


def finish_kernel(spans, *refs):
    count = len(spans)
    kept, came, out = refs[:count], refs[count : 2 * count], refs[-1]
    for (at, end), a, b in zip(spans, kept, came):
        out[:, at:end] = a[a.shape[0] - out.shape[0] :, :] + b[...].astype(jnp.float32)


VMEM_SPEC = pl.BlockSpec(memory_space=pltpu.VMEM)
SPECS = {
    True: pl.BlockSpec(memory_space=pltpu.HBM),
    False: VMEM_SPEC,
    None: pl.BlockSpec(memory_space=pl.ANY),
}


def kernel_call(body, ins, outs, scratch, cost):
    flops, moved = cost
    return pl.pallas_call(
        body,
        out_shape=[jax.ShapeDtypeStruct(*out) for out in outs],
        in_specs=[SPECS[far] for _, far in ins],
        out_specs=[VMEM_SPEC] * len(outs),
        scratch_shapes=scratch,
        compiler_params=pltpu.CompilerParams(vmem_limit_bytes=VMEM_LIMIT),
        cost_estimate=pl.CostEstimate(flops=flops, bytes_accessed=moved, transcendentals=0),
    )(
        *(
            pltpu.with_memory_space_constraint(x, pltpu.HBM) if far else x
            for x, far in ins
        )
    )


def per_device(n, eigvecs, lanczos, bands, band_order):
    cols, depth = eigvecs.shape
    lanc = lanczos.shape[0]
    per_chunk = band_order.shape[0] // n
    rows = band_order.shape[0] * lanc
    spans = split_columns(cols)
    cuts = [0] + [end for _, end in spans]
    widths = [end - at for at, end in spans]
    bf16 = jnp.bfloat16

    def exchange(value, p, stage):
        pairs = []
        for i in range(n):
            for core in range(2):
                bit = PLAN[p][1 + core][stage] if stage < 3 else stage
                pairs.append((2 * i + core, 2 * (i ^ (1 << bit)) + core))
        return lax.ppermute(value, ("grid", "eig"), pairs)

    def flops(width):
        return rows * width * depth

    other = lax.ppermute(bands, "eig", [(0, 1), (1, 0)])
    pick, own, lanc16, eig = kernel_call(
        functools.partial(setup_kernel, n, per_chunk, lanc, widths[0]),
        [(band_order, True), (bands, True), (lanczos, True), (eigvecs, True)],
        [
            ((rows, 2 * bands.shape[0]), bf16),
            (bands.shape, bf16),
            (lanczos.shape, bf16),
            ((widths[0], depth), bf16),
        ],
        [pltpu.SMEM(band_order.shape, jnp.int32), pltpu.SemaphoreType.DMA((4,))],
        (0, 2 * widths[0] * depth),
    )
    sources = [(x, False) for x in (pick, own, other, lanc16)]
    send, half, eig_next = kernel_call(
        functools.partial(first_kernel, cuts[1]),
        sources + [(eig, False), (eigvecs, True)],
        [((rows // 2, widths[0]), bf16), ((rows // 2, depth), bf16), ((widths[1], depth), bf16)],
        [pltpu.VMEM((rows // 2, widths[0]), jnp.float32), pltpu.SemaphoreType.DMA((1,))],
        (flops(widths[0]), 2 * widths[0] * depth),
    )
    *sends, prod, eig_rest = kernel_call(
        functools.partial(send_kernel, cuts[2]),
        sources + [(half, False), (eig_next, False), (eigvecs, True)],
        [((rows // 2, w), bf16) for w in widths[1:]]
        + [((rows, depth), bf16), ((cols - cuts[2], depth), bf16)],
        [pltpu.VMEM((rows // 2, max(widths[1:])), jnp.float32), pltpu.SemaphoreType.DMA((1,))],
        (flops(sum(widths[1:])), 2 * sum(widths[1:]) * depth),
    )
    eigs = [eig, eig_next] + [eig_rest] * (len(PLAN) - 2)
    got = [exchange(s, p, 0) for p, s in enumerate([send, *sends])]
    value = []
    for p, width in enumerate(widths):
        value += kernel_call(
            functools.partial(keep_kernel, p, cuts[p] - cuts[min(p, 2)]),
            [(prod, False), (eigs[p], False)],
            [((rows // 2, width), jnp.float32)],
            [],
            (flops(width), 2 * width * depth),
        )
    later = range(3, n.bit_length() - 1)
    token = prod
    for p, stage in ORDER + [(p, stage) for stage in later for p in range(len(PLAN))]:
        part = value[p].shape[0] // 2
        size = part * widths[p]
        leave, value[p] = kernel_call(
            add_kernel,
            [(value[p], False), (got[p], False), (token, None)],
            [((part, widths[p]), bf16 if stage < 3 else jnp.float32)]
            + [((part, widths[p]), jnp.float32)],
            [],
            (2 * size, 18 * size),
        )
        token = leave
        got[p] = exchange(leave, p, stage)
    outs = list(zip(value, got))
    (result,) = kernel_call(
        functools.partial(finish_kernel, spans),
        [(value, False) for value, _ in outs] + [(came, False) for _, came in outs],
        [((rows // n, cols), jnp.float32)],
        [],
        (rows // n * cols, 12 * rows // n * cols),
    )
    return result.reshape(per_chunk, lanc, cols)


def solution(mesh):
    in_specs = (
        P("eig", ("rep", "grid")),
        P(None, ("rep", "grid")),
        P("eig", ("rep", "grid")),
        P("rep"),
    )
    out_specs = P(("rep", "grid"), None, "eig")
    return jax.shard_map(
        functools.partial(per_device, mesh.shape["grid"]),
        mesh=mesh,
        in_specs=in_specs,
        out_specs=out_specs,
        check_vma=False,
    )
```

```python
import functools

import jax
import jax.numpy as jnp
from jax import lax
from jax.experimental import pallas as pl
from jax.experimental.pallas import tpu as pltpu
from jax.sharding import PartitionSpec as P

TILE = 256
VMEM_LIMIT = 32 * 1024 * 1024
X, NEAR, FAR = 0, 1, 2
PLAN = [
    (3, (NEAR, X, FAR), (X, FAR, NEAR)),
    (2, (X, NEAR, FAR), (FAR, X, NEAR)),
    (2, (NEAR, X, FAR), (X, FAR, NEAR)),
]
ORDER = [(piece, stage) for stage in (1, 2) for piece in range(len(PLAN))]


def ranked(bits, fixed=0):
    out = [fixed]
    for b in reversed(bits):
        out = [c | (1 << b) for c in out] + out
    return out


def split_columns(cols):
    unit = 128
    total = sum(plan[0] for plan in PLAN)
    ends, done = [], 0
    for share, *_ in PLAN[:-1]:
        done += share
        ends.append(int(round(cols * done / total / unit)) * unit)
    ends.append(cols)
    return list(zip([0] + ends[:-1], ends))


def halves(bits):
    keep = ranked(bits[1:])
    return keep, [c | (1 << bits[0]) for c in keep]


def places(p, core, kept):
    keep, leave = halves(PLAN[0][1 + core])
    return [(leave + keep).index(c) for c in halves(PLAN[p][1 + core])[0 if kept else 1]]


def rows_of(prod, p, kept):
    block = prod.shape[0] // 8
    core = lax.axis_index("eig")
    parts = []
    for a, b in zip(places(p, 0, kept), places(p, 1, kept)):
        at = a * block if a == b else pl.multiple_of(jnp.where(core == 0, a, b) * block, block)
        parts.append(prod[pl.ds(at, block), :])
    return jnp.concatenate(parts, axis=0)


def dot_tiles(out, rows, eig, first):
    width = out.shape[1]
    for at in range(0, width, TILE):
        size = min(TILE, width - at)
        out[:, at : at + size] = lax.dot_general(
            rows,
            eig[first + at : first + at + size, :],
            (((1,), (1,)), ((), ())),
            preferred_element_type=jnp.float32,
        )


def setup_kernel(n, per_chunk, lanc, width, order_hbm, own_hbm, lanc_hbm, eig_hbm, *rest):
    pick, own, lanc16, eig, order, sem = rest
    copies = [
        pltpu.make_async_copy(src, dst, sem.at[i])
        for i, (src, dst) in enumerate(
            [
                (order_hbm, order),
                (own_hbm, own),
                (lanc_hbm, lanc16),
                (eig_hbm.at[pl.ds(0, width)], eig),
            ]
        )
    ]
    for copy in copies:
        copy.start()
    me = lax.axis_index("grid")
    core = lax.axis_index("eig")
    bands = pick.shape[1]
    rest_bits = list(range(3, n.bit_length() - 1))
    classes = zip(*(sum(reversed(halves(PLAN[0][1 + i])), []) for i in range(2)))
    slots = []
    for pair in classes:
        for both in zip(*(ranked(rest_bits, c) for c in pair)):
            slots += [(both, j) for j in range(per_chunk)]
    col = lax.broadcasted_iota(jnp.int32, (2 * lanc, bands), 1)
    upper = lax.broadcasted_iota(jnp.int32, (2 * lanc, bands), 0) < lanc
    copies[0].wait()
    for i in range(0, len(slots), 2):
        want = []
        for r, j in slots[i : i + 2]:
            offset = jnp.where(core == 0, r[0], r[1])
            band = order[(me ^ offset) * per_chunk + j]
            want.append(lax.rem(band + core * (bands // 2), bands))
        hit = col == jnp.where(upper, want[0], want[1])
        pick[i * lanc : (i + 2) * lanc, :] = hit.astype(jnp.float32).astype(jnp.bfloat16)
    for copy in copies[1:]:
        copy.wait()


def make_rows(prod, pick, own, other, lanc16, first):
    lanc = lanc16[...].astype(jnp.float32)
    chosen = lax.dot_general(
        pick[first : first + prod.shape[0], :],
        jnp.concatenate([own[...], other[...]], axis=0),
        (((1,), (0,)), ((), ())),
        preferred_element_type=jnp.float32,
    )
    value = chosen.reshape(-1, *lanc.shape) * lanc[None]
    prod[...] = value.reshape(chosen.shape).astype(jnp.bfloat16)


def first_kernel(cut, pick, own, other, lanc16, eig, eig_hbm, out, prod, eig_next, acc, sem):
    copy = pltpu.make_async_copy(
        eig_hbm.at[pl.ds(cut, eig_next.shape[0])], eig_next, sem.at[0]
    )
    copy.start()
    make_rows(prod, pick, own, other, lanc16, 0)
    dot_tiles(acc, prod[...], eig, 0)
    out[...] = acc[...].astype(out.dtype)
    copy.wait()


def send_kernel(cut, pick, own, other, lanc16, half, eig, eig_hbm, *rest):
    *outs, prod, eig_rest, acc, sem = rest
    copy = pltpu.make_async_copy(
        eig_hbm.at[pl.ds(cut, eig_rest.shape[0])], eig_rest, sem.at[0]
    )
    copy.start()
    first = half.shape[0]
    prod[:first, :] = half[...]
    make_rows(prod.at[first:, :], pick, own, other, lanc16, first)
    at = 0
    for i, out in enumerate(outs):
        part = acc.at[:, : out.shape[1]]
        if i == 1:
            copy.wait()
        dot_tiles(part, rows_of(prod, i + 1, False), eig_rest if i else eig, at)
        out[...] = part[...].astype(out.dtype)
        at += out.shape[1] if i else 0


def keep_kernel(p, first, prod, eig, out):
    dot_tiles(out, rows_of(prod, p, True), eig, first)


def add_kernel(kept, got, _, leave, keep):
    mid = leave.shape[0]
    leave[...] = (kept[:mid, :] + got[:mid, :].astype(jnp.float32)).astype(leave.dtype)
    keep[...] = kept[mid:, :] + got[mid:, :].astype(jnp.float32)


def write_sums(first, kept, came, out, held, sem):
    at = 0
    for a, b in zip(kept, came):
        end = at + a.shape[1]
        held[:, at:end] = a[...] + b[...].astype(jnp.float32)
        at = end
    copy = pltpu.make_async_copy(held, out.at[:, pl.ds(first, at)], sem.at[0])
    copy.start()
    copy.wait()


def early_kernel(count, *refs):
    write_sums(0, refs[:count], refs[count : 2 * count], *refs[2 * count :])


def finish_kernel(first, _, kept, came, out, held, sem):
    write_sums(first, [kept], [came], out, held, sem)


VMEM_SPEC = pl.BlockSpec(memory_space=pltpu.VMEM)
SPECS = {
    True: pl.BlockSpec(memory_space=pltpu.HBM),
    False: VMEM_SPEC,
    None: pl.BlockSpec(memory_space=pl.ANY),
}


def kernel_call(body, ins, outs, scratch, cost, far_out=False, aliases={}):
    flops, moved = cost
    return pl.pallas_call(
        body,
        out_shape=[jax.ShapeDtypeStruct(*out) for out in outs],
        in_specs=[SPECS[far] for _, far in ins],
        out_specs=[SPECS[far_out]] * len(outs),
        scratch_shapes=scratch,
        input_output_aliases=aliases,
        compiler_params=pltpu.CompilerParams(vmem_limit_bytes=VMEM_LIMIT),
        cost_estimate=pl.CostEstimate(flops=flops, bytes_accessed=moved, transcendentals=0),
    )(
        *(
            pltpu.with_memory_space_constraint(x, pltpu.HBM) if far else x
            for x, far in ins
        )
    )


def per_device(n, eigvecs, lanczos, bands, band_order):
    cols, depth = eigvecs.shape
    lanc = lanczos.shape[0]
    per_chunk = band_order.shape[0] // n
    rows = band_order.shape[0] * lanc
    spans = split_columns(cols)
    cuts = [0] + [end for _, end in spans]
    widths = [end - at for at, end in spans]
    bf16 = jnp.bfloat16

    def exchange(value, p, stage):
        pairs = []
        for i in range(n):
            for core in range(2):
                bit = PLAN[p][1 + core][stage] if stage < 3 else stage
                pairs.append((2 * i + core, 2 * (i ^ (1 << bit)) + core))
        return lax.ppermute(value, ("grid", "eig"), pairs)

    def flops(width):
        return rows * width * depth

    other = lax.ppermute(bands, "eig", [(0, 1), (1, 0)])
    pick, own, lanc16, eig = kernel_call(
        functools.partial(setup_kernel, n, per_chunk, lanc, widths[0]),
        [(band_order, True), (bands, True), (lanczos, True), (eigvecs, True)],
        [
            ((rows, 2 * bands.shape[0]), bf16),
            (bands.shape, bf16),
            (lanczos.shape, bf16),
            ((widths[0], depth), bf16),
        ],
        [pltpu.SMEM(band_order.shape, jnp.int32), pltpu.SemaphoreType.DMA((4,))],
        (0, 2 * widths[0] * depth),
    )
    sources = [(x, False) for x in (pick, own, other, lanc16)]
    send, half, eig_next = kernel_call(
        functools.partial(first_kernel, cuts[1]),
        sources + [(eig, False), (eigvecs, True)],
        [((rows // 2, widths[0]), bf16), ((rows // 2, depth), bf16), ((widths[1], depth), bf16)],
        [pltpu.VMEM((rows // 2, widths[0]), jnp.float32), pltpu.SemaphoreType.DMA((1,))],
        (flops(widths[0]), 2 * widths[0] * depth),
    )
    *sends, prod, eig_rest = kernel_call(
        functools.partial(send_kernel, cuts[2]),
        sources + [(half, False), (eig_next, False), (eigvecs, True)],
        [((rows // 2, w), bf16) for w in widths[1:]]
        + [((rows, depth), bf16), ((cols - cuts[2], depth), bf16)],
        [pltpu.VMEM((rows // 2, max(widths[1:])), jnp.float32), pltpu.SemaphoreType.DMA((1,))],
        (flops(sum(widths[1:])), 2 * sum(widths[1:]) * depth),
    )
    eigs = [eig, eig_next] + [eig_rest] * (len(PLAN) - 2)
    got = [exchange(s, p, 0) for p, s in enumerate([send, *sends])]
    value = []
    for p, width in enumerate(widths):
        value += kernel_call(
            functools.partial(keep_kernel, p, cuts[p] - cuts[min(p, 2)]),
            [(prod, False), (eigs[p], False)],
            [((rows // 2, width), jnp.float32)],
            [],
            (flops(width), 2 * width * depth),
        )
    later = range(3, n.bit_length() - 1)
    token = prod
    for p, stage in ORDER + [(p, stage) for stage in later for p in range(len(PLAN))]:
        part = value[p].shape[0] // 2
        size = part * widths[p]
        leave, value[p] = kernel_call(
            add_kernel,
            [(value[p], False), (got[p], False), (token, None)],
            [((part, widths[p]), bf16 if stage < 3 else jnp.float32)]
            + [((part, widths[p]), jnp.float32)],
            [],
            (2 * size, 18 * size),
        )
        token = leave
        got[p] = exchange(leave, p, stage)
    value = [v[v.shape[0] - rows // n :, :] for v in value]
    last = len(PLAN) - 1
    result = kernel_call(
        functools.partial(early_kernel, last),
        [(v, False) for v in value[:last]] + [(g, False) for g in got[:last]],
        [((rows // n, cols), jnp.float32)],
        [pltpu.VMEM((rows // n, cuts[last]), jnp.float32), pltpu.SemaphoreType.DMA((1,))],
        (rows // n * cuts[last], 10 * rows // n * cuts[last]),
        far_out=True,
    )
    (result,) = kernel_call(
        functools.partial(finish_kernel, cuts[last]),
        [(result[0], True), (value[last], False), (got[last], False)],
        [((rows // n, cols), jnp.float32)],
        [pltpu.VMEM((rows // n, widths[last]), jnp.float32), pltpu.SemaphoreType.DMA((1,))],
        (rows // n * widths[last], 10 * rows // n * widths[last]),
        far_out=True,
        aliases={0: 0},
    )
    return result.reshape(per_chunk, lanc, cols)


def solution(mesh):
    in_specs = (
        P("eig", ("rep", "grid")),
        P(None, ("rep", "grid")),
        P("eig", ("rep", "grid")),
        P("rep"),
    )
    out_specs = P(("rep", "grid"), None, "eig")
    return jax.shard_map(
        functools.partial(per_device, mesh.shape["grid"]),
        mesh=mesh,
        in_specs=in_specs,
        out_specs=out_specs,
        check_vma=False,
    )
```

```python
import functools

import jax
import jax.numpy as jnp
from jax import lax
from jax.experimental import pallas as pl
from jax.experimental.pallas import tpu as pltpu
from jax.sharding import PartitionSpec as P

TILE = 256
VMEM_LIMIT = 32 * 1024 * 1024
X, NEAR, FAR = 0, 1, 2
PLAN = [
    (3, (NEAR, X, FAR), (X, FAR, NEAR)),
    (2, (X, NEAR, FAR), (FAR, X, NEAR)),
    (2, (NEAR, X, FAR), (X, FAR, NEAR)),
]
ORDER = [(piece, stage) for stage in (1, 2) for piece in range(len(PLAN))]


def ranked(bits, fixed=0):
    out = [fixed]
    for b in reversed(bits):
        out = [c | (1 << b) for c in out] + out
    return out


def split_columns(cols):
    unit = 128
    total = sum(plan[0] for plan in PLAN)
    ends, done = [], 0
    for share, *_ in PLAN[:-1]:
        done += share
        ends.append(int(round(cols * done / total / unit)) * unit)
    ends.append(cols)
    return list(zip([0] + ends[:-1], ends))


def halves(bits):
    keep = ranked(bits[1:])
    return keep, [c | (1 << bits[0]) for c in keep]


def places(p, core, kept):
    keep, leave = halves(PLAN[0][1 + core])
    return [(leave + keep).index(c) for c in halves(PLAN[p][1 + core])[0 if kept else 1]]


def rows_of(prod, p, kept):
    block = prod.shape[0] // 8
    core = lax.axis_index("eig")
    parts = []
    for a, b in zip(places(p, 0, kept), places(p, 1, kept)):
        at = a * block if a == b else pl.multiple_of(jnp.where(core == 0, a, b) * block, block)
        parts.append(prod[pl.ds(at, block), :])
    return jnp.concatenate(parts, axis=0)


def dot_tiles(out, rows, eig, first):
    width = out.shape[1]
    for at in range(0, width, TILE):
        size = min(TILE, width - at)
        out[:, at : at + size] = lax.dot_general(
            rows,
            eig[first + at : first + at + size, :],
            (((1,), (1,)), ((), ())),
            preferred_element_type=jnp.float32,
        )


def setup_kernel(n, per_chunk, lanc, width, order_hbm, own_hbm, lanc_hbm, eig_hbm, *rest):
    pick, own, lanc16, eig, order, sem = rest
    copies = [
        pltpu.make_async_copy(src, dst, sem.at[i])
        for i, (src, dst) in enumerate(
            [
                (order_hbm, order),
                (own_hbm, own),
                (lanc_hbm, lanc16),
                (eig_hbm.at[pl.ds(0, width)], eig),
            ]
        )
    ]
    for copy in copies:
        copy.start()
    me = lax.axis_index("grid")
    core = lax.axis_index("eig")
    bands = pick.shape[1]
    rest_bits = list(range(3, n.bit_length() - 1))
    classes = zip(*(sum(reversed(halves(PLAN[0][1 + i])), []) for i in range(2)))
    slots = []
    for pair in classes:
        for both in zip(*(ranked(rest_bits, c) for c in pair)):
            slots += [(both, j) for j in range(per_chunk)]
    col = lax.broadcasted_iota(jnp.int32, (2 * lanc, bands), 1)
    upper = lax.broadcasted_iota(jnp.int32, (2 * lanc, bands), 0) < lanc
    copies[0].wait()
    for i in range(0, len(slots), 2):
        want = []
        for r, j in slots[i : i + 2]:
            offset = jnp.where(core == 0, r[0], r[1])
            band = order[(me ^ offset) * per_chunk + j]
            want.append(lax.rem(band + core * (bands // 2), bands))
        hit = col == jnp.where(upper, want[0], want[1])
        pick[i * lanc : (i + 2) * lanc, :] = hit.astype(jnp.float32).astype(jnp.bfloat16)
    for copy in copies[1:]:
        copy.wait()


def make_rows(prod, pick, own, other, lanc16, first):
    lanc = lanc16[...].astype(jnp.float32)
    chosen = lax.dot_general(
        pick[first : first + prod.shape[0], :],
        jnp.concatenate([own[...], other[...]], axis=0),
        (((1,), (0,)), ((), ())),
        preferred_element_type=jnp.float32,
    )
    value = chosen.reshape(-1, *lanc.shape) * lanc[None]
    prod[...] = value.reshape(chosen.shape).astype(jnp.bfloat16)


def first_kernel(cut, pick, own, other, lanc16, eig, eig_hbm, out, prod, eig_next, acc, sem):
    copy = pltpu.make_async_copy(
        eig_hbm.at[pl.ds(cut, eig_next.shape[0])], eig_next, sem.at[0]
    )
    copy.start()
    make_rows(prod, pick, own, other, lanc16, 0)
    dot_tiles(acc, prod[...], eig, 0)
    out[...] = acc[...].astype(out.dtype)
    copy.wait()


def second_kernel(cut, pick, own, other, lanc16, half, eig, eig_hbm, out, prod, eig_rest, acc, sem):
    copy = pltpu.make_async_copy(
        eig_hbm.at[pl.ds(cut, eig_rest.shape[0])], eig_rest, sem.at[0]
    )
    copy.start()
    first = half.shape[0]
    prod[:first, :] = half[...]
    make_rows(prod.at[first:, :], pick, own, other, lanc16, first)
    dot_tiles(acc, rows_of(prod, 1, False), eig, 0)
    out[...] = acc[...].astype(out.dtype)
    copy.wait()


def send_kernel(p, first, prod, eig, _, out, acc):
    dot_tiles(acc, rows_of(prod, p, False), eig, first)
    out[...] = acc[...].astype(out.dtype)


def keep_kernel(p, first, prod, eig, out):
    dot_tiles(out, rows_of(prod, p, True), eig, first)


def add_kernel(kept, got, _, leave, keep):
    mid = leave.shape[0]
    leave[...] = (kept[:mid, :] + got[:mid, :].astype(jnp.float32)).astype(leave.dtype)
    keep[...] = kept[mid:, :] + got[mid:, :].astype(jnp.float32)


def write_sums(first, kept, came, out, held, sem):
    at = 0
    for a, b in zip(kept, came):
        end = at + a.shape[1]
        held[:, at:end] = a[...] + b[...].astype(jnp.float32)
        at = end
    copy = pltpu.make_async_copy(held, out.at[:, pl.ds(first, at)], sem.at[0])
    copy.start()
    copy.wait()


def early_kernel(count, *refs):
    write_sums(0, refs[:count], refs[count : 2 * count], *refs[2 * count :])


def finish_kernel(first, _, kept, came, out, held, sem):
    write_sums(first, [kept], [came], out, held, sem)


VMEM_SPEC = pl.BlockSpec(memory_space=pltpu.VMEM)
SPECS = {
    True: pl.BlockSpec(memory_space=pltpu.HBM),
    False: VMEM_SPEC,
    None: pl.BlockSpec(memory_space=pl.ANY),
}


def kernel_call(body, ins, outs, scratch, cost, far_out=False, aliases={}):
    flops, moved = cost
    return pl.pallas_call(
        body,
        out_shape=[jax.ShapeDtypeStruct(*out) for out in outs],
        in_specs=[SPECS[far] for _, far in ins],
        out_specs=[SPECS[far_out]] * len(outs),
        scratch_shapes=scratch,
        input_output_aliases=aliases,
        compiler_params=pltpu.CompilerParams(vmem_limit_bytes=VMEM_LIMIT),
        cost_estimate=pl.CostEstimate(flops=flops, bytes_accessed=moved, transcendentals=0),
    )(
        *(
            pltpu.with_memory_space_constraint(x, pltpu.HBM) if far else x
            for x, far in ins
        )
    )


def per_device(n, eigvecs, lanczos, bands, band_order):
    cols, depth = eigvecs.shape
    lanc = lanczos.shape[0]
    per_chunk = band_order.shape[0] // n
    rows = band_order.shape[0] * lanc
    spans = split_columns(cols)
    cuts = [0] + [end for _, end in spans]
    widths = [end - at for at, end in spans]
    bf16 = jnp.bfloat16

    def exchange(value, p, stage):
        pairs = []
        for i in range(n):
            for core in range(2):
                bit = PLAN[p][1 + core][stage] if stage < 3 else stage
                pairs.append((2 * i + core, 2 * (i ^ (1 << bit)) + core))
        return lax.ppermute(value, ("grid", "eig"), pairs)

    def flops(width):
        return rows * width * depth

    other = lax.ppermute(bands, "eig", [(0, 1), (1, 0)])
    pick, own, lanc16, eig = kernel_call(
        functools.partial(setup_kernel, n, per_chunk, lanc, widths[0]),
        [(band_order, True), (bands, True), (lanczos, True), (eigvecs, True)],
        [
            ((rows, 2 * bands.shape[0]), bf16),
            (bands.shape, bf16),
            (lanczos.shape, bf16),
            ((widths[0], depth), bf16),
        ],
        [pltpu.SMEM(band_order.shape, jnp.int32), pltpu.SemaphoreType.DMA((4,))],
        (0, 2 * widths[0] * depth),
    )
    sources = [(x, False) for x in (pick, own, other, lanc16)]
    send, half, eig_next = kernel_call(
        functools.partial(first_kernel, cuts[1]),
        sources + [(eig, False), (eigvecs, True)],
        [((rows // 2, widths[0]), bf16), ((rows // 2, depth), bf16), ((widths[1], depth), bf16)],
        [pltpu.VMEM((rows // 2, widths[0]), jnp.float32), pltpu.SemaphoreType.DMA((1,))],
        (flops(widths[0]), 2 * widths[0] * depth),
    )
    second, prod, eig_rest = kernel_call(
        functools.partial(second_kernel, cuts[2]),
        sources + [(half, False), (eig_next, False), (eigvecs, True)],
        [((rows // 2, widths[1]), bf16), ((rows, depth), bf16), ((cols - cuts[2], depth), bf16)],
        [pltpu.VMEM((rows // 2, widths[1]), jnp.float32), pltpu.SemaphoreType.DMA((1,))],
        (flops(widths[1]), 2 * (cols - cuts[2]) * depth),
    )
    eigs = [eig, eig_next] + [eig_rest] * (len(PLAN) - 2)
    sends = [send, second]
    for p in range(2, len(PLAN)):
        sends += kernel_call(
            functools.partial(send_kernel, p, cuts[p] - cuts[2]),
            [(prod, False), (eig_rest, False), (sends[-1], None)],
            [((rows // 2, widths[p]), bf16)],
            [pltpu.VMEM((rows // 2, widths[p]), jnp.float32)],
            (flops(widths[p]), 2 * widths[p] * depth),
        )
    got = [exchange(s, p, 0) for p, s in enumerate(sends)]
    value = []
    for p, width in enumerate(widths):
        value += kernel_call(
            functools.partial(keep_kernel, p, cuts[p] - cuts[min(p, 2)]),
            [(prod, False), (eigs[p], False)],
            [((rows // 2, width), jnp.float32)],
            [],
            (flops(width), 2 * width * depth),
        )
    later = range(3, n.bit_length() - 1)
    token = sends[-1]
    for p, stage in ORDER + [(p, stage) for stage in later for p in range(len(PLAN))]:
        part = value[p].shape[0] // 2
        size = part * widths[p]
        leave, value[p] = kernel_call(
            add_kernel,
            [(value[p], False), (got[p], False), (token, None)],
            [((part, widths[p]), bf16 if stage < 3 else jnp.float32)]
            + [((part, widths[p]), jnp.float32)],
            [],
            (2 * size, 18 * size),
        )
        token = leave
        got[p] = exchange(leave, p, stage)
    value = [v[v.shape[0] - rows // n :, :] for v in value]
    last = len(PLAN) - 1
    result = kernel_call(
        functools.partial(early_kernel, last),
        [(v, False) for v in value[:last]] + [(g, False) for g in got[:last]],
        [((rows // n, cols), jnp.float32)],
        [pltpu.VMEM((rows // n, cuts[last]), jnp.float32), pltpu.SemaphoreType.DMA((1,))],
        (rows // n * cuts[last], 10 * rows // n * cuts[last]),
        far_out=True,
    )
    (result,) = kernel_call(
        functools.partial(finish_kernel, cuts[last]),
        [(result[0], True), (value[last], False), (got[last], False)],
        [((rows // n, cols), jnp.float32)],
        [pltpu.VMEM((rows // n, widths[last]), jnp.float32), pltpu.SemaphoreType.DMA((1,))],
        (rows // n * widths[last], 10 * rows // n * widths[last]),
        far_out=True,
        aliases={0: 0},
    )
    return result.reshape(per_chunk, lanc, cols)


def solution(mesh):
    in_specs = (
        P("eig", ("rep", "grid")),
        P(None, ("rep", "grid")),
        P("eig", ("rep", "grid")),
        P("rep"),
    )
    out_specs = P(("rep", "grid"), None, "eig")
    return jax.shard_map(
        functools.partial(per_device, mesh.shape["grid"]),
        mesh=mesh,
        in_specs=in_specs,
        out_specs=out_specs,
        check_vma=False,
    )
```

```python
import functools

import jax
import jax.numpy as jnp
from jax import lax
from jax.experimental import pallas as pl
from jax.experimental.pallas import tpu as pltpu
from jax.sharding import PartitionSpec as P

TILE = 256
VMEM_LIMIT = 32 * 1024 * 1024
X, NEAR, FAR = 0, 1, 2
PLAN = [
    (3, (NEAR, X, FAR), (X, FAR, NEAR)),
    (2, (X, NEAR, FAR), (FAR, X, NEAR)),
    (2, (NEAR, FAR, X), (X, NEAR, FAR)),
]
ORDER = [(piece, stage) for stage in (1, 2) for piece in range(len(PLAN))]


def ranked(bits, fixed=0):
    out = [fixed]
    for b in reversed(bits):
        out = [c | (1 << b) for c in out] + out
    return out


def split_columns(cols):
    unit = 128
    total = sum(plan[0] for plan in PLAN)
    ends, done = [], 0
    for share, *_ in PLAN[:-1]:
        done += share
        ends.append(int(round(cols * done / total / unit)) * unit)
    ends.append(cols)
    return list(zip([0] + ends[:-1], ends))


def halves(bits):
    keep = ranked(bits[1:])
    return keep, [c | (1 << bits[0]) for c in keep]


def places(p, core, kept):
    keep, leave = halves(PLAN[0][1 + core])
    return [(leave + keep).index(c) for c in halves(PLAN[p][1 + core])[0 if kept else 1]]


def rows_of(prod, p, kept):
    block = prod.shape[0] // 8
    core = lax.axis_index("eig")
    parts = []
    for a, b in zip(places(p, 0, kept), places(p, 1, kept)):
        at = a * block if a == b else pl.multiple_of(jnp.where(core == 0, a, b) * block, block)
        parts.append(prod[pl.ds(at, block), :])
    return jnp.concatenate(parts, axis=0)


def dot_tiles(out, rows, eig, first):
    width = out.shape[1]
    for at in range(0, width, TILE):
        size = min(TILE, width - at)
        out[:, at : at + size] = lax.dot_general(
            rows,
            eig[first + at : first + at + size, :],
            (((1,), (1,)), ((), ())),
            preferred_element_type=jnp.float32,
        )


def setup_kernel(n, per_chunk, lanc, width, order_hbm, own_hbm, lanc_hbm, eig_hbm, *rest):
    pick, own, lanc16, eig, order, sem = rest
    copies = [
        pltpu.make_async_copy(src, dst, sem.at[i])
        for i, (src, dst) in enumerate(
            [
                (order_hbm, order),
                (own_hbm, own),
                (lanc_hbm, lanc16),
                (eig_hbm.at[pl.ds(0, width)], eig),
            ]
        )
    ]
    for copy in copies:
        copy.start()
    me = lax.axis_index("grid")
    core = lax.axis_index("eig")
    bands = pick.shape[1]
    rest_bits = list(range(3, n.bit_length() - 1))
    classes = zip(*(sum(reversed(halves(PLAN[0][1 + i])), []) for i in range(2)))
    slots = []
    for pair in classes:
        for both in zip(*(ranked(rest_bits, c) for c in pair)):
            slots += [(both, j) for j in range(per_chunk)]
    col = lax.broadcasted_iota(jnp.int32, (2 * lanc, bands), 1)
    upper = lax.broadcasted_iota(jnp.int32, (2 * lanc, bands), 0) < lanc
    copies[0].wait()
    for i in range(0, len(slots), 2):
        want = []
        for r, j in slots[i : i + 2]:
            offset = jnp.where(core == 0, r[0], r[1])
            band = order[(me ^ offset) * per_chunk + j]
            want.append(lax.rem(band + core * (bands // 2), bands))
        hit = col == jnp.where(upper, want[0], want[1])
        pick[i * lanc : (i + 2) * lanc, :] = hit.astype(jnp.float32).astype(jnp.bfloat16)
    for copy in copies[1:]:
        copy.wait()


def make_rows(prod, pick, own, other, lanc16, first):
    lanc = lanc16[...].astype(jnp.float32)
    chosen = lax.dot_general(
        pick[first : first + prod.shape[0], :],
        jnp.concatenate([own[...], other[...]], axis=0),
        (((1,), (0,)), ((), ())),
        preferred_element_type=jnp.float32,
    )
    value = chosen.reshape(-1, *lanc.shape) * lanc[None]
    prod[...] = value.reshape(chosen.shape).astype(jnp.bfloat16)


def first_kernel(cut, pick, own, other, lanc16, eig, eig_hbm, out, prod, eig_next, acc, sem):
    copy = pltpu.make_async_copy(
        eig_hbm.at[pl.ds(cut, eig_next.shape[0])], eig_next, sem.at[0]
    )
    copy.start()
    make_rows(prod, pick, own, other, lanc16, 0)
    dot_tiles(acc, prod[...], eig, 0)
    out[...] = acc[...].astype(out.dtype)
    copy.wait()


def second_kernel(cut, pick, own, other, lanc16, half, eig, eig_hbm, out, prod, eig_rest, acc, sem):
    copy = pltpu.make_async_copy(
        eig_hbm.at[pl.ds(cut, eig_rest.shape[0])], eig_rest, sem.at[0]
    )
    copy.start()
    first = half.shape[0]
    prod[:first, :] = half[...]
    make_rows(prod.at[first:, :], pick, own, other, lanc16, first)
    dot_tiles(acc, rows_of(prod, 1, False), eig, 0)
    out[...] = acc[...].astype(out.dtype)
    copy.wait()


def send_kernel(p, first, prod, eig, _, out, acc):
    dot_tiles(acc, rows_of(prod, p, False), eig, first)
    out[...] = acc[...].astype(out.dtype)


def keep_kernel(p, first, prod, eig, out):
    dot_tiles(out, rows_of(prod, p, True), eig, first)


def add_kernel(kept, got, _, leave, keep):
    mid = leave.shape[0]
    leave[...] = (kept[:mid, :] + got[:mid, :].astype(jnp.float32)).astype(leave.dtype)
    keep[...] = kept[mid:, :] + got[mid:, :].astype(jnp.float32)


def write_sums(first, kept, came, out, held, sem):
    at = 0
    for a, b in zip(kept, came):
        end = at + a.shape[1]
        held[:, at:end] = a[...] + b[...].astype(jnp.float32)
        at = end
    copy = pltpu.make_async_copy(held, out.at[:, pl.ds(first, at)], sem.at[0])
    copy.start()
    copy.wait()


def early_kernel(count, *refs):
    write_sums(0, refs[:count], refs[count : 2 * count], *refs[2 * count :])


def finish_kernel(first, _, kept, came, out, held, sem):
    write_sums(first, [kept], [came], out, held, sem)


VMEM_SPEC = pl.BlockSpec(memory_space=pltpu.VMEM)
SPECS = {
    True: pl.BlockSpec(memory_space=pltpu.HBM),
    False: VMEM_SPEC,
    None: pl.BlockSpec(memory_space=pl.ANY),
}


def kernel_call(body, ins, outs, scratch, cost, far_out=False, aliases={}):
    flops, moved = cost
    return pl.pallas_call(
        body,
        out_shape=[jax.ShapeDtypeStruct(*out) for out in outs],
        in_specs=[SPECS[far] for _, far in ins],
        out_specs=[SPECS[far_out]] * len(outs),
        scratch_shapes=scratch,
        input_output_aliases=aliases,
        compiler_params=pltpu.CompilerParams(vmem_limit_bytes=VMEM_LIMIT),
        cost_estimate=pl.CostEstimate(flops=flops, bytes_accessed=moved, transcendentals=0),
    )(
        *(
            pltpu.with_memory_space_constraint(x, pltpu.HBM) if far else x
            for x, far in ins
        )
    )


def per_device(n, eigvecs, lanczos, bands, band_order):
    cols, depth = eigvecs.shape
    lanc = lanczos.shape[0]
    per_chunk = band_order.shape[0] // n
    rows = band_order.shape[0] * lanc
    spans = split_columns(cols)
    cuts = [0] + [end for _, end in spans]
    widths = [end - at for at, end in spans]
    bf16 = jnp.bfloat16

    def exchange(value, p, stage):
        pairs = []
        for i in range(n):
            for core in range(2):
                bit = PLAN[p][1 + core][stage] if stage < 3 else stage
                pairs.append((2 * i + core, 2 * (i ^ (1 << bit)) + core))
        return lax.ppermute(value, ("grid", "eig"), pairs)

    def flops(width):
        return rows * width * depth

    other = lax.ppermute(bands, "eig", [(0, 1), (1, 0)])
    pick, own, lanc16, eig = kernel_call(
        functools.partial(setup_kernel, n, per_chunk, lanc, widths[0]),
        [(band_order, True), (bands, True), (lanczos, True), (eigvecs, True)],
        [
            ((rows, 2 * bands.shape[0]), bf16),
            (bands.shape, bf16),
            (lanczos.shape, bf16),
            ((widths[0], depth), bf16),
        ],
        [pltpu.SMEM(band_order.shape, jnp.int32), pltpu.SemaphoreType.DMA((4,))],
        (0, 2 * widths[0] * depth),
    )
    sources = [(x, False) for x in (pick, own, other, lanc16)]
    send, half, eig_next = kernel_call(
        functools.partial(first_kernel, cuts[1]),
        sources + [(eig, False), (eigvecs, True)],
        [((rows // 2, widths[0]), bf16), ((rows // 2, depth), bf16), ((widths[1], depth), bf16)],
        [pltpu.VMEM((rows // 2, widths[0]), jnp.float32), pltpu.SemaphoreType.DMA((1,))],
        (flops(widths[0]), 2 * widths[0] * depth),
    )
    second, prod, eig_rest = kernel_call(
        functools.partial(second_kernel, cuts[2]),
        sources + [(half, False), (eig_next, False), (eigvecs, True)],
        [((rows // 2, widths[1]), bf16), ((rows, depth), bf16), ((cols - cuts[2], depth), bf16)],
        [pltpu.VMEM((rows // 2, widths[1]), jnp.float32), pltpu.SemaphoreType.DMA((1,))],
        (flops(widths[1]), 2 * (cols - cuts[2]) * depth),
    )
    eigs = [eig, eig_next] + [eig_rest] * (len(PLAN) - 2)
    sends = [send, second]
    for p in range(2, len(PLAN)):
        sends += kernel_call(
            functools.partial(send_kernel, p, cuts[p] - cuts[2]),
            [(prod, False), (eig_rest, False), (sends[-1], None)],
            [((rows // 2, widths[p]), bf16)],
            [pltpu.VMEM((rows // 2, widths[p]), jnp.float32)],
            (flops(widths[p]), 2 * widths[p] * depth),
        )
    got = [exchange(s, p, 0) for p, s in enumerate(sends)]
    value = []
    for p, width in enumerate(widths):
        value += kernel_call(
            functools.partial(keep_kernel, p, cuts[p] - cuts[min(p, 2)]),
            [(prod, False), (eigs[p], False)],
            [((rows // 2, width), jnp.float32)],
            [],
            (flops(width), 2 * width * depth),
        )
    later = range(3, n.bit_length() - 1)
    token = sends[-1]
    for p, stage in ORDER + [(p, stage) for stage in later for p in range(len(PLAN))]:
        part = value[p].shape[0] // 2
        size = part * widths[p]
        leave, value[p] = kernel_call(
            add_kernel,
            [(value[p], False), (got[p], False), (token, None)],
            [((part, widths[p]), bf16 if stage < 3 else jnp.float32)]
            + [((part, widths[p]), jnp.float32)],
            [],
            (2 * size, 18 * size),
        )
        token = leave
        got[p] = exchange(leave, p, stage)
    value = [v[v.shape[0] - rows // n :, :] for v in value]
    last = len(PLAN) - 1
    result = kernel_call(
        functools.partial(early_kernel, last),
        [(v, False) for v in value[:last]] + [(g, False) for g in got[:last]],
        [((rows // n, cols), jnp.float32)],
        [pltpu.VMEM((rows // n, cuts[last]), jnp.float32), pltpu.SemaphoreType.DMA((1,))],
        (rows // n * cuts[last], 10 * rows // n * cuts[last]),
        far_out=True,
    )
    (result,) = kernel_call(
        functools.partial(finish_kernel, cuts[last]),
        [(result[0], True), (value[last], False), (got[last], False)],
        [((rows // n, cols), jnp.float32)],
        [pltpu.VMEM((rows // n, widths[last]), jnp.float32), pltpu.SemaphoreType.DMA((1,))],
        (rows // n * widths[last], 10 * rows // n * widths[last]),
        far_out=True,
        aliases={0: 0},
    )
    return result.reshape(per_chunk, lanc, cols)


def solution(mesh):
    in_specs = (
        P("eig", ("rep", "grid")),
        P(None, ("rep", "grid")),
        P("eig", ("rep", "grid")),
        P("rep"),
    )
    out_specs = P(("rep", "grid"), None, "eig")
    return jax.shard_map(
        functools.partial(per_device, mesh.shape["grid"]),
        mesh=mesh,
        in_specs=in_specs,
        out_specs=out_specs,
        check_vma=False,
    )
```

```python
import functools

import jax
import jax.numpy as jnp
from jax import lax
from jax.experimental import pallas as pl
from jax.experimental.pallas import tpu as pltpu
from jax.sharding import PartitionSpec as P

TILE = 256
VMEM_LIMIT = 32 * 1024 * 1024
X, NEAR, FAR = 0, 1, 2
PLAN = [
    (3.5, (NEAR, X, FAR), (X, FAR, NEAR)),
    (2, (X, NEAR, FAR), (FAR, X, NEAR)),
    (1.5, (NEAR, X, FAR), (X, FAR, NEAR)),
]
ORDER = [(piece, stage) for stage in (1, 2) for piece in range(len(PLAN))]


def ranked(bits, fixed=0):
    out = [fixed]
    for b in reversed(bits):
        out = [c | (1 << b) for c in out] + out
    return out


def split_columns(cols):
    unit = 128
    total = sum(plan[0] for plan in PLAN)
    ends, done = [], 0
    for share, *_ in PLAN[:-1]:
        done += share
        ends.append(int(round(cols * done / total / unit)) * unit)
    ends.append(cols)
    return list(zip([0] + ends[:-1], ends))


def halves(bits):
    keep = ranked(bits[1:])
    return keep, [c | (1 << bits[0]) for c in keep]


def places(p, core, kept):
    keep, leave = halves(PLAN[0][1 + core])
    return [(leave + keep).index(c) for c in halves(PLAN[p][1 + core])[0 if kept else 1]]


def rows_of(prod, p, kept):
    block = prod.shape[0] // 8
    core = lax.axis_index("eig")
    parts = []
    for a, b in zip(places(p, 0, kept), places(p, 1, kept)):
        at = a * block if a == b else pl.multiple_of(jnp.where(core == 0, a, b) * block, block)
        parts.append(prod[pl.ds(at, block), :])
    return jnp.concatenate(parts, axis=0)


def dot_tiles(out, rows, eig, first):
    width = out.shape[1]
    for at in range(0, width, TILE):
        size = min(TILE, width - at)
        out[:, at : at + size] = lax.dot_general(
            rows,
            eig[first + at : first + at + size, :],
            (((1,), (1,)), ((), ())),
            preferred_element_type=jnp.float32,
        )


def setup_kernel(n, per_chunk, lanc, width, order_hbm, own_hbm, lanc_hbm, eig_hbm, *rest):
    pick, own, lanc16, eig, order, sem = rest
    copies = [
        pltpu.make_async_copy(src, dst, sem.at[i])
        for i, (src, dst) in enumerate(
            [
                (order_hbm, order),
                (own_hbm, own),
                (lanc_hbm, lanc16),
                (eig_hbm.at[pl.ds(0, width)], eig),
            ]
        )
    ]
    for copy in copies:
        copy.start()
    me = lax.axis_index("grid")
    core = lax.axis_index("eig")
    bands = pick.shape[1]
    rest_bits = list(range(3, n.bit_length() - 1))
    classes = zip(*(sum(reversed(halves(PLAN[0][1 + i])), []) for i in range(2)))
    slots = []
    for pair in classes:
        for both in zip(*(ranked(rest_bits, c) for c in pair)):
            slots += [(both, j) for j in range(per_chunk)]
    col = lax.broadcasted_iota(jnp.int32, (2 * lanc, bands), 1)
    upper = lax.broadcasted_iota(jnp.int32, (2 * lanc, bands), 0) < lanc
    copies[0].wait()
    for i in range(0, len(slots), 2):
        want = []
        for r, j in slots[i : i + 2]:
            offset = jnp.where(core == 0, r[0], r[1])
            band = order[(me ^ offset) * per_chunk + j]
            want.append(lax.rem(band + core * (bands // 2), bands))
        hit = col == jnp.where(upper, want[0], want[1])
        pick[i * lanc : (i + 2) * lanc, :] = hit.astype(jnp.float32).astype(jnp.bfloat16)
    for copy in copies[1:]:
        copy.wait()


def make_rows(prod, pick, own, other, lanc16, first):
    lanc = lanc16[...].astype(jnp.float32)
    chosen = lax.dot_general(
        pick[first : first + prod.shape[0], :],
        jnp.concatenate([own[...], other[...]], axis=0),
        (((1,), (0,)), ((), ())),
        preferred_element_type=jnp.float32,
    )
    value = chosen.reshape(-1, *lanc.shape) * lanc[None]
    prod[...] = value.reshape(chosen.shape).astype(jnp.bfloat16)


def first_kernel(cut, pick, own, other, lanc16, eig, eig_hbm, out, prod, eig_next, acc, sem):
    copy = pltpu.make_async_copy(
        eig_hbm.at[pl.ds(cut, eig_next.shape[0])], eig_next, sem.at[0]
    )
    copy.start()
    make_rows(prod, pick, own, other, lanc16, 0)
    dot_tiles(acc, prod[...], eig, 0)
    out[...] = acc[...].astype(out.dtype)
    copy.wait()


def second_kernel(cut, pick, own, other, lanc16, half, eig, eig_hbm, out, prod, eig_rest, acc, sem):
    copy = pltpu.make_async_copy(
        eig_hbm.at[pl.ds(cut, eig_rest.shape[0])], eig_rest, sem.at[0]
    )
    copy.start()
    first = half.shape[0]
    prod[:first, :] = half[...]
    make_rows(prod.at[first:, :], pick, own, other, lanc16, first)
    dot_tiles(acc, rows_of(prod, 1, False), eig, 0)
    out[...] = acc[...].astype(out.dtype)
    copy.wait()


def send_kernel(p, first, prod, eig, _, out, acc):
    dot_tiles(acc, rows_of(prod, p, False), eig, first)
    out[...] = acc[...].astype(out.dtype)


def keep_kernel(p, first, prod, eig, out):
    dot_tiles(out, rows_of(prod, p, True), eig, first)


def add_kernel(kept, got, _, leave, keep):
    mid = leave.shape[0]
    leave[...] = (kept[:mid, :] + got[:mid, :].astype(jnp.float32)).astype(leave.dtype)
    keep[...] = kept[mid:, :] + got[mid:, :].astype(jnp.float32)


def write_sums(first, kept, came, out, held, sem):
    at = 0
    for a, b in zip(kept, came):
        end = at + a.shape[1]
        held[:, at:end] = a[...] + b[...].astype(jnp.float32)
        at = end
    copy = pltpu.make_async_copy(held, out.at[:, pl.ds(first, at)], sem.at[0])
    copy.start()
    copy.wait()


def early_kernel(count, *refs):
    write_sums(0, refs[:count], refs[count : 2 * count], *refs[2 * count :])


def finish_kernel(first, _, kept, came, out, held, sem):
    write_sums(first, [kept], [came], out, held, sem)


VMEM_SPEC = pl.BlockSpec(memory_space=pltpu.VMEM)
SPECS = {
    True: pl.BlockSpec(memory_space=pltpu.HBM),
    False: VMEM_SPEC,
    None: pl.BlockSpec(memory_space=pl.ANY),
}


def kernel_call(body, ins, outs, scratch, cost, far_out=False, aliases={}):
    flops, moved = cost
    return pl.pallas_call(
        body,
        out_shape=[jax.ShapeDtypeStruct(*out) for out in outs],
        in_specs=[SPECS[far] for _, far in ins],
        out_specs=[SPECS[far_out]] * len(outs),
        scratch_shapes=scratch,
        input_output_aliases=aliases,
        compiler_params=pltpu.CompilerParams(vmem_limit_bytes=VMEM_LIMIT),
        cost_estimate=pl.CostEstimate(flops=flops, bytes_accessed=moved, transcendentals=0),
    )(
        *(
            pltpu.with_memory_space_constraint(x, pltpu.HBM) if far else x
            for x, far in ins
        )
    )


def per_device(n, eigvecs, lanczos, bands, band_order):
    cols, depth = eigvecs.shape
    lanc = lanczos.shape[0]
    per_chunk = band_order.shape[0] // n
    rows = band_order.shape[0] * lanc
    spans = split_columns(cols)
    cuts = [0] + [end for _, end in spans]
    widths = [end - at for at, end in spans]
    bf16 = jnp.bfloat16

    def exchange(value, p, stage):
        pairs = []
        for i in range(n):
            for core in range(2):
                bit = PLAN[p][1 + core][stage] if stage < 3 else stage
                pairs.append((2 * i + core, 2 * (i ^ (1 << bit)) + core))
        return lax.ppermute(value, ("grid", "eig"), pairs)

    def flops(width):
        return rows * width * depth

    other = lax.ppermute(bands, "eig", [(0, 1), (1, 0)])
    pick, own, lanc16, eig = kernel_call(
        functools.partial(setup_kernel, n, per_chunk, lanc, widths[0]),
        [(band_order, True), (bands, True), (lanczos, True), (eigvecs, True)],
        [
            ((rows, 2 * bands.shape[0]), bf16),
            (bands.shape, bf16),
            (lanczos.shape, bf16),
            ((widths[0], depth), bf16),
        ],
        [pltpu.SMEM(band_order.shape, jnp.int32), pltpu.SemaphoreType.DMA((4,))],
        (0, 2 * widths[0] * depth),
    )
    sources = [(x, False) for x in (pick, own, other, lanc16)]
    send, half, eig_next = kernel_call(
        functools.partial(first_kernel, cuts[1]),
        sources + [(eig, False), (eigvecs, True)],
        [((rows // 2, widths[0]), bf16), ((rows // 2, depth), bf16), ((widths[1], depth), bf16)],
        [pltpu.VMEM((rows // 2, widths[0]), jnp.float32), pltpu.SemaphoreType.DMA((1,))],
        (flops(widths[0]), 2 * widths[0] * depth),
    )
    second, prod, eig_rest = kernel_call(
        functools.partial(second_kernel, cuts[2]),
        sources + [(half, False), (eig_next, False), (eigvecs, True)],
        [((rows // 2, widths[1]), bf16), ((rows, depth), bf16), ((cols - cuts[2], depth), bf16)],
        [pltpu.VMEM((rows // 2, widths[1]), jnp.float32), pltpu.SemaphoreType.DMA((1,))],
        (flops(widths[1]), 2 * (cols - cuts[2]) * depth),
    )
    eigs = [eig, eig_next] + [eig_rest] * (len(PLAN) - 2)
    sends = [send, second]
    for p in range(2, len(PLAN)):
        sends += kernel_call(
            functools.partial(send_kernel, p, cuts[p] - cuts[2]),
            [(prod, False), (eig_rest, False), (sends[-1], None)],
            [((rows // 2, widths[p]), bf16)],
            [pltpu.VMEM((rows // 2, widths[p]), jnp.float32)],
            (flops(widths[p]), 2 * widths[p] * depth),
        )
    got = [exchange(s, p, 0) for p, s in enumerate(sends)]
    value = []
    for p, width in enumerate(widths):
        value += kernel_call(
            functools.partial(keep_kernel, p, cuts[p] - cuts[min(p, 2)]),
            [(prod, False), (eigs[p], False)],
            [((rows // 2, width), jnp.float32)],
            [],
            (flops(width), 2 * width * depth),
        )
    later = range(3, n.bit_length() - 1)
    token = sends[-1]
    for p, stage in ORDER + [(p, stage) for stage in later for p in range(len(PLAN))]:
        part = value[p].shape[0] // 2
        size = part * widths[p]
        leave, value[p] = kernel_call(
            add_kernel,
            [(value[p], False), (got[p], False), (token, None)],
            [((part, widths[p]), bf16 if stage < 3 else jnp.float32)]
            + [((part, widths[p]), jnp.float32)],
            [],
            (2 * size, 18 * size),
        )
        token = leave
        got[p] = exchange(leave, p, stage)
    value = [v[v.shape[0] - rows // n :, :] for v in value]
    last = len(PLAN) - 1
    result = kernel_call(
        functools.partial(early_kernel, last),
        [(v, False) for v in value[:last]] + [(g, False) for g in got[:last]],
        [((rows // n, cols), jnp.float32)],
        [pltpu.VMEM((rows // n, cuts[last]), jnp.float32), pltpu.SemaphoreType.DMA((1,))],
        (rows // n * cuts[last], 10 * rows // n * cuts[last]),
        far_out=True,
    )
    (result,) = kernel_call(
        functools.partial(finish_kernel, cuts[last]),
        [(result[0], True), (value[last], False), (got[last], False)],
        [((rows // n, cols), jnp.float32)],
        [pltpu.VMEM((rows // n, widths[last]), jnp.float32), pltpu.SemaphoreType.DMA((1,))],
        (rows // n * widths[last], 10 * rows // n * widths[last]),
        far_out=True,
        aliases={0: 0},
    )
    return result.reshape(per_chunk, lanc, cols)


def solution(mesh):
    in_specs = (
        P("eig", ("rep", "grid")),
        P(None, ("rep", "grid")),
        P("eig", ("rep", "grid")),
        P("rep"),
    )
    out_specs = P(("rep", "grid"), None, "eig")
    return jax.shard_map(
        functools.partial(per_device, mesh.shape["grid"]),
        mesh=mesh,
        in_specs=in_specs,
        out_specs=out_specs,
        check_vma=False,
    )
```

```python
import functools

import jax
import jax.numpy as jnp
from jax import lax
from jax.experimental import pallas as pl
from jax.experimental.pallas import tpu as pltpu
from jax.sharding import PartitionSpec as P

TILE = 256
VMEM_LIMIT = 32 * 1024 * 1024
X, NEAR, FAR = 0, 1, 2
PLAN = [
    (3, (NEAR, X, FAR), (X, FAR, NEAR)),
    (2, (X, NEAR, FAR), (FAR, X, NEAR)),
    (2, (X, FAR, NEAR), (NEAR, X, FAR)),
]
ORDER = [(piece, stage) for stage in (1, 2) for piece in range(len(PLAN))]


def ranked(bits, fixed=0):
    out = [fixed]
    for b in reversed(bits):
        out = [c | (1 << b) for c in out] + out
    return out


def split_columns(cols):
    unit = 128
    total = sum(plan[0] for plan in PLAN)
    ends, done = [], 0
    for share, *_ in PLAN[:-1]:
        done += share
        ends.append(int(round(cols * done / total / unit)) * unit)
    ends.append(cols)
    return list(zip([0] + ends[:-1], ends))


def halves(bits):
    keep = ranked(bits[1:])
    return keep, [c | (1 << bits[0]) for c in keep]


def places(p, core, kept):
    keep, leave = halves(PLAN[0][1 + core])
    return [(leave + keep).index(c) for c in halves(PLAN[p][1 + core])[0 if kept else 1]]


def rows_of(prod, p, kept):
    block = prod.shape[0] // 8
    core = lax.axis_index("eig")
    parts = []
    for a, b in zip(places(p, 0, kept), places(p, 1, kept)):
        at = a * block if a == b else pl.multiple_of(jnp.where(core == 0, a, b) * block, block)
        parts.append(prod[pl.ds(at, block), :])
    return jnp.concatenate(parts, axis=0)


def dot_tiles(out, rows, eig, first):
    width = out.shape[1]
    for at in range(0, width, TILE):
        size = min(TILE, width - at)
        out[:, at : at + size] = lax.dot_general(
            rows,
            eig[first + at : first + at + size, :],
            (((1,), (1,)), ((), ())),
            preferred_element_type=jnp.float32,
        )


def setup_kernel(n, per_chunk, lanc, width, order_hbm, own_hbm, lanc_hbm, eig_hbm, *rest):
    pick, own, lanc16, eig, order, sem = rest
    copies = [
        pltpu.make_async_copy(src, dst, sem.at[i])
        for i, (src, dst) in enumerate(
            [
                (order_hbm, order),
                (own_hbm, own),
                (lanc_hbm, lanc16),
                (eig_hbm.at[pl.ds(0, width)], eig),
            ]
        )
    ]
    for copy in copies:
        copy.start()
    me = lax.axis_index("grid")
    core = lax.axis_index("eig")
    bands = pick.shape[1]
    rest_bits = list(range(3, n.bit_length() - 1))
    classes = zip(*(sum(reversed(halves(PLAN[0][1 + i])), []) for i in range(2)))
    slots = []
    for pair in classes:
        for both in zip(*(ranked(rest_bits, c) for c in pair)):
            slots += [(both, j) for j in range(per_chunk)]
    col = lax.broadcasted_iota(jnp.int32, (2 * lanc, bands), 1)
    upper = lax.broadcasted_iota(jnp.int32, (2 * lanc, bands), 0) < lanc
    copies[0].wait()
    for i in range(0, len(slots), 2):
        want = []
        for r, j in slots[i : i + 2]:
            offset = jnp.where(core == 0, r[0], r[1])
            band = order[(me ^ offset) * per_chunk + j]
            want.append(lax.rem(band + core * (bands // 2), bands))
        hit = col == jnp.where(upper, want[0], want[1])
        pick[i * lanc : (i + 2) * lanc, :] = hit.astype(jnp.float32).astype(jnp.bfloat16)
    for copy in copies[1:]:
        copy.wait()


def make_rows(prod, pick, own, other, lanc16, first):
    lanc = lanc16[...].astype(jnp.float32)
    chosen = lax.dot_general(
        pick[first : first + prod.shape[0], :],
        jnp.concatenate([own[...], other[...]], axis=0),
        (((1,), (0,)), ((), ())),
        preferred_element_type=jnp.float32,
    )
    value = chosen.reshape(-1, *lanc.shape) * lanc[None]
    prod[...] = value.reshape(chosen.shape).astype(jnp.bfloat16)


def first_kernel(cut, pick, own, other, lanc16, eig, eig_hbm, out, prod, eig_next, acc, sem):
    copy = pltpu.make_async_copy(
        eig_hbm.at[pl.ds(cut, eig_next.shape[0])], eig_next, sem.at[0]
    )
    copy.start()
    make_rows(prod, pick, own, other, lanc16, 0)
    dot_tiles(acc, prod[...], eig, 0)
    out[...] = acc[...].astype(out.dtype)
    copy.wait()


def send_kernel(cut, pick, own, other, lanc16, half, eig, eig_hbm, *rest):
    *outs, prod, eig_rest, acc, sem = rest
    copy = pltpu.make_async_copy(
        eig_hbm.at[pl.ds(cut, eig_rest.shape[0])], eig_rest, sem.at[0]
    )
    copy.start()
    first = half.shape[0]
    prod[:first, :] = half[...]
    make_rows(prod.at[first:, :], pick, own, other, lanc16, first)
    at = 0
    for i, out in enumerate(outs):
        part = acc.at[:, : out.shape[1]]
        if i == 1:
            copy.wait()
        dot_tiles(part, rows_of(prod, i + 1, False), eig_rest if i else eig, at)
        out[...] = part[...].astype(out.dtype)
        at += out.shape[1] if i else 0


def keep_kernel(p, first, prod, eig, out):
    dot_tiles(out, rows_of(prod, p, True), eig, first)


def add_kernel(kept, got, _, leave, keep):
    mid = leave.shape[0]
    leave[...] = (kept[:mid, :] + got[:mid, :].astype(jnp.float32)).astype(leave.dtype)
    keep[...] = kept[mid:, :] + got[mid:, :].astype(jnp.float32)


def write_sums(first, kept, came, out, held, sem):
    at = 0
    for a, b in zip(kept, came):
        end = at + a.shape[1]
        held[:, at:end] = a[...] + b[...].astype(jnp.float32)
        at = end
    copy = pltpu.make_async_copy(held, out.at[:, pl.ds(first, at)], sem.at[0])
    copy.start()
    copy.wait()


def early_kernel(count, *refs):
    write_sums(0, refs[:count], refs[count : 2 * count], *refs[2 * count :])


def finish_kernel(first, _, kept, came, out, held, sem):
    write_sums(first, [kept], [came], out, held, sem)


VMEM_SPEC = pl.BlockSpec(memory_space=pltpu.VMEM)
SPECS = {
    True: pl.BlockSpec(memory_space=pltpu.HBM),
    False: VMEM_SPEC,
    None: pl.BlockSpec(memory_space=pl.ANY),
}


def kernel_call(body, ins, outs, scratch, cost, far_out=False, aliases={}):
    flops, moved = cost
    return pl.pallas_call(
        body,
        out_shape=[jax.ShapeDtypeStruct(*out) for out in outs],
        in_specs=[SPECS[far] for _, far in ins],
        out_specs=[SPECS[far_out]] * len(outs),
        scratch_shapes=scratch,
        input_output_aliases=aliases,
        compiler_params=pltpu.CompilerParams(vmem_limit_bytes=VMEM_LIMIT),
        cost_estimate=pl.CostEstimate(flops=flops, bytes_accessed=moved, transcendentals=0),
    )(
        *(
            pltpu.with_memory_space_constraint(x, pltpu.HBM) if far else x
            for x, far in ins
        )
    )


def per_device(n, eigvecs, lanczos, bands, band_order):
    cols, depth = eigvecs.shape
    lanc = lanczos.shape[0]
    per_chunk = band_order.shape[0] // n
    rows = band_order.shape[0] * lanc
    spans = split_columns(cols)
    cuts = [0] + [end for _, end in spans]
    widths = [end - at for at, end in spans]
    bf16 = jnp.bfloat16

    def exchange(value, p, stage):
        pairs = []
        for i in range(n):
            for core in range(2):
                bit = PLAN[p][1 + core][stage] if stage < 3 else stage
                pairs.append((2 * i + core, 2 * (i ^ (1 << bit)) + core))
        return lax.ppermute(value, ("grid", "eig"), pairs)

    def flops(width):
        return rows * width * depth

    other = lax.ppermute(bands, "eig", [(0, 1), (1, 0)])
    pick, own, lanc16, eig = kernel_call(
        functools.partial(setup_kernel, n, per_chunk, lanc, widths[0]),
        [(band_order, True), (bands, True), (lanczos, True), (eigvecs, True)],
        [
            ((rows, 2 * bands.shape[0]), bf16),
            (bands.shape, bf16),
            (lanczos.shape, bf16),
            ((widths[0], depth), bf16),
        ],
        [pltpu.SMEM(band_order.shape, jnp.int32), pltpu.SemaphoreType.DMA((4,))],
        (0, 2 * widths[0] * depth),
    )
    sources = [(x, False) for x in (pick, own, other, lanc16)]
    send, half, eig_next = kernel_call(
        functools.partial(first_kernel, cuts[1]),
        sources + [(eig, False), (eigvecs, True)],
        [((rows // 2, widths[0]), bf16), ((rows // 2, depth), bf16), ((widths[1], depth), bf16)],
        [pltpu.VMEM((rows // 2, widths[0]), jnp.float32), pltpu.SemaphoreType.DMA((1,))],
        (flops(widths[0]), 2 * widths[0] * depth),
    )
    *sends, prod, eig_rest = kernel_call(
        functools.partial(send_kernel, cuts[2]),
        sources + [(half, False), (eig_next, False), (eigvecs, True)],
        [((rows // 2, w), bf16) for w in widths[1:]]
        + [((rows, depth), bf16), ((cols - cuts[2], depth), bf16)],
        [pltpu.VMEM((rows // 2, max(widths[1:])), jnp.float32), pltpu.SemaphoreType.DMA((1,))],
        (flops(sum(widths[1:])), 2 * sum(widths[1:]) * depth),
    )
    eigs = [eig, eig_next] + [eig_rest] * (len(PLAN) - 2)
    got = [exchange(s, p, 0) for p, s in enumerate([send, *sends])]
    value = []
    for p, width in enumerate(widths):
        value += kernel_call(
            functools.partial(keep_kernel, p, cuts[p] - cuts[min(p, 2)]),
            [(prod, False), (eigs[p], False)],
            [((rows // 2, width), jnp.float32)],
            [],
            (flops(width), 2 * width * depth),
        )
    later = range(3, n.bit_length() - 1)
    token = prod
    for p, stage in ORDER + [(p, stage) for stage in later for p in range(len(PLAN))]:
        part = value[p].shape[0] // 2
        size = part * widths[p]
        leave, value[p] = kernel_call(
            add_kernel,
            [(value[p], False), (got[p], False), (token, None)],
            [((part, widths[p]), bf16 if stage < 3 else jnp.float32)]
            + [((part, widths[p]), jnp.float32)],
            [],
            (2 * size, 18 * size),
        )
        token = leave
        got[p] = exchange(leave, p, stage)
    value = [v[v.shape[0] - rows // n :, :] for v in value]
    last = len(PLAN) - 1
    result = kernel_call(
        functools.partial(early_kernel, last),
        [(v, False) for v in value[:last]] + [(g, False) for g in got[:last]],
        [((rows // n, cols), jnp.float32)],
        [pltpu.VMEM((rows // n, cuts[last]), jnp.float32), pltpu.SemaphoreType.DMA((1,))],
        (rows // n * cuts[last], 10 * rows // n * cuts[last]),
        far_out=True,
    )
    (result,) = kernel_call(
        functools.partial(finish_kernel, cuts[last]),
        [(result[0], True), (value[last], False), (got[last], False)],
        [((rows // n, cols), jnp.float32)],
        [pltpu.VMEM((rows // n, widths[last]), jnp.float32), pltpu.SemaphoreType.DMA((1,))],
        (rows // n * widths[last], 10 * rows // n * widths[last]),
        far_out=True,
        aliases={0: 0},
    )
    return result.reshape(per_chunk, lanc, cols)


def solution(mesh):
    in_specs = (
        P("eig", ("rep", "grid")),
        P(None, ("rep", "grid")),
        P("eig", ("rep", "grid")),
        P("rep"),
    )
    out_specs = P(("rep", "grid"), None, "eig")
    return jax.shard_map(
        functools.partial(per_device, mesh.shape["grid"]),
        mesh=mesh,
        in_specs=in_specs,
        out_specs=out_specs,
        check_vma=False,
    )
```

```python
import functools

import jax
import jax.numpy as jnp
from jax import lax
from jax.experimental import pallas as pl
from jax.experimental.pallas import tpu as pltpu
from jax.sharding import PartitionSpec as P

TILE = 256
VMEM_LIMIT = 32 * 1024 * 1024
X, NEAR, FAR = 0, 1, 2
PLAN = [
    (3, (NEAR, X, FAR), (X, FAR, NEAR)),
    (2, (X, NEAR, FAR), (X, FAR, NEAR)),
    (2, (NEAR, X, FAR), (FAR, X, NEAR)),
]
ORDER = [(piece, stage) for stage in (1, 2) for piece in range(len(PLAN))]


def ranked(bits, fixed=0):
    out = [fixed]
    for b in reversed(bits):
        out = [c | (1 << b) for c in out] + out
    return out


def split_columns(cols):
    unit = 128
    total = sum(plan[0] for plan in PLAN)
    ends, done = [], 0
    for share, *_ in PLAN[:-1]:
        done += share
        ends.append(int(round(cols * done / total / unit)) * unit)
    ends.append(cols)
    return list(zip([0] + ends[:-1], ends))


def halves(bits):
    keep = ranked(bits[1:])
    return keep, [c | (1 << bits[0]) for c in keep]


def places(p, core, kept):
    keep, leave = halves(PLAN[0][1 + core])
    return [(leave + keep).index(c) for c in halves(PLAN[p][1 + core])[0 if kept else 1]]


def rows_of(prod, p, kept):
    block = prod.shape[0] // 8
    core = lax.axis_index("eig")
    parts = []
    for a, b in zip(places(p, 0, kept), places(p, 1, kept)):
        at = a * block if a == b else pl.multiple_of(jnp.where(core == 0, a, b) * block, block)
        parts.append(prod[pl.ds(at, block), :])
    return jnp.concatenate(parts, axis=0)


def dot_tiles(out, rows, eig, first):
    width = out.shape[1]
    for at in range(0, width, TILE):
        size = min(TILE, width - at)
        out[:, at : at + size] = lax.dot_general(
            rows,
            eig[first + at : first + at + size, :],
            (((1,), (1,)), ((), ())),
            preferred_element_type=jnp.float32,
        )


def setup_kernel(n, per_chunk, lanc, width, order_hbm, own_hbm, lanc_hbm, eig_hbm, *rest):
    pick, own, lanc16, eig, order, sem = rest
    copies = [
        pltpu.make_async_copy(src, dst, sem.at[i])
        for i, (src, dst) in enumerate(
            [
                (order_hbm, order),
                (own_hbm, own),
                (lanc_hbm, lanc16),
                (eig_hbm.at[pl.ds(0, width)], eig),
            ]
        )
    ]
    for copy in copies:
        copy.start()
    me = lax.axis_index("grid")
    core = lax.axis_index("eig")
    bands = pick.shape[1]
    rest_bits = list(range(3, n.bit_length() - 1))
    classes = zip(*(sum(reversed(halves(PLAN[0][1 + i])), []) for i in range(2)))
    slots = []
    for pair in classes:
        for both in zip(*(ranked(rest_bits, c) for c in pair)):
            slots += [(both, j) for j in range(per_chunk)]
    col = lax.broadcasted_iota(jnp.int32, (2 * lanc, bands), 1)
    upper = lax.broadcasted_iota(jnp.int32, (2 * lanc, bands), 0) < lanc
    copies[0].wait()
    for i in range(0, len(slots), 2):
        want = []
        for r, j in slots[i : i + 2]:
            offset = jnp.where(core == 0, r[0], r[1])
            band = order[(me ^ offset) * per_chunk + j]
            want.append(lax.rem(band + core * (bands // 2), bands))
        hit = col == jnp.where(upper, want[0], want[1])
        pick[i * lanc : (i + 2) * lanc, :] = hit.astype(jnp.float32).astype(jnp.bfloat16)
    for copy in copies[1:]:
        copy.wait()


def make_rows(prod, pick, own, other, lanc16, first):
    lanc = lanc16[...].astype(jnp.float32)
    chosen = lax.dot_general(
        pick[first : first + prod.shape[0], :],
        jnp.concatenate([own[...], other[...]], axis=0),
        (((1,), (0,)), ((), ())),
        preferred_element_type=jnp.float32,
    )
    value = chosen.reshape(-1, *lanc.shape) * lanc[None]
    prod[...] = value.reshape(chosen.shape).astype(jnp.bfloat16)


def first_kernel(cut, pick, own, other, lanc16, eig, eig_hbm, out, prod, eig_next, acc, sem):
    copy = pltpu.make_async_copy(
        eig_hbm.at[pl.ds(cut, eig_next.shape[0])], eig_next, sem.at[0]
    )
    copy.start()
    make_rows(prod, pick, own, other, lanc16, 0)
    dot_tiles(acc, prod[...], eig, 0)
    out[...] = acc[...].astype(out.dtype)
    copy.wait()


def send_kernel(cut, pick, own, other, lanc16, half, eig, eig_hbm, *rest):
    *outs, prod, eig_rest, acc, sem = rest
    copy = pltpu.make_async_copy(
        eig_hbm.at[pl.ds(cut, eig_rest.shape[0])], eig_rest, sem.at[0]
    )
    copy.start()
    first = half.shape[0]
    prod[:first, :] = half[...]
    make_rows(prod.at[first:, :], pick, own, other, lanc16, first)
    at = 0
    for i, out in enumerate(outs):
        part = acc.at[:, : out.shape[1]]
        if i == 1:
            copy.wait()
        dot_tiles(part, rows_of(prod, i + 1, False), eig_rest if i else eig, at)
        out[...] = part[...].astype(out.dtype)
        at += out.shape[1] if i else 0


def keep_kernel(p, first, prod, eig, out):
    dot_tiles(out, rows_of(prod, p, True), eig, first)


def add_kernel(kept, got, _, leave, keep):
    mid = leave.shape[0]
    leave[...] = (kept[:mid, :] + got[:mid, :].astype(jnp.float32)).astype(leave.dtype)
    keep[...] = kept[mid:, :] + got[mid:, :].astype(jnp.float32)


def write_sums(first, kept, came, out, held, sem):
    at = 0
    for a, b in zip(kept, came):
        end = at + a.shape[1]
        held[:, at:end] = a[...] + b[...].astype(jnp.float32)
        at = end
    copy = pltpu.make_async_copy(held, out.at[:, pl.ds(first, at)], sem.at[0])
    copy.start()
    copy.wait()


def early_kernel(count, *refs):
    write_sums(0, refs[:count], refs[count : 2 * count], *refs[2 * count :])


def finish_kernel(first, _, kept, came, out, held, sem):
    write_sums(first, [kept], [came], out, held, sem)


VMEM_SPEC = pl.BlockSpec(memory_space=pltpu.VMEM)
SPECS = {
    True: pl.BlockSpec(memory_space=pltpu.HBM),
    False: VMEM_SPEC,
    None: pl.BlockSpec(memory_space=pl.ANY),
}


def kernel_call(body, ins, outs, scratch, cost, far_out=False, aliases={}):
    flops, moved = cost
    return pl.pallas_call(
        body,
        out_shape=[jax.ShapeDtypeStruct(*out) for out in outs],
        in_specs=[SPECS[far] for _, far in ins],
        out_specs=[SPECS[far_out]] * len(outs),
        scratch_shapes=scratch,
        input_output_aliases=aliases,
        compiler_params=pltpu.CompilerParams(vmem_limit_bytes=VMEM_LIMIT),
        cost_estimate=pl.CostEstimate(flops=flops, bytes_accessed=moved, transcendentals=0),
    )(
        *(
            pltpu.with_memory_space_constraint(x, pltpu.HBM) if far else x
            for x, far in ins
        )
    )


def per_device(n, eigvecs, lanczos, bands, band_order):
    cols, depth = eigvecs.shape
    lanc = lanczos.shape[0]
    per_chunk = band_order.shape[0] // n
    rows = band_order.shape[0] * lanc
    spans = split_columns(cols)
    cuts = [0] + [end for _, end in spans]
    widths = [end - at for at, end in spans]
    bf16 = jnp.bfloat16

    def exchange(value, p, stage):
        pairs = []
        for i in range(n):
            for core in range(2):
                bit = PLAN[p][1 + core][stage] if stage < 3 else stage
                pairs.append((2 * i + core, 2 * (i ^ (1 << bit)) + core))
        return lax.ppermute(value, ("grid", "eig"), pairs)

    def flops(width):
        return rows * width * depth

    other = lax.ppermute(bands, "eig", [(0, 1), (1, 0)])
    pick, own, lanc16, eig = kernel_call(
        functools.partial(setup_kernel, n, per_chunk, lanc, widths[0]),
        [(band_order, True), (bands, True), (lanczos, True), (eigvecs, True)],
        [
            ((rows, 2 * bands.shape[0]), bf16),
            (bands.shape, bf16),
            (lanczos.shape, bf16),
            ((widths[0], depth), bf16),
        ],
        [pltpu.SMEM(band_order.shape, jnp.int32), pltpu.SemaphoreType.DMA((4,))],
        (0, 2 * widths[0] * depth),
    )
    sources = [(x, False) for x in (pick, own, other, lanc16)]
    send, half, eig_next = kernel_call(
        functools.partial(first_kernel, cuts[1]),
        sources + [(eig, False), (eigvecs, True)],
        [((rows // 2, widths[0]), bf16), ((rows // 2, depth), bf16), ((widths[1], depth), bf16)],
        [pltpu.VMEM((rows // 2, widths[0]), jnp.float32), pltpu.SemaphoreType.DMA((1,))],
        (flops(widths[0]), 2 * widths[0] * depth),
    )
    *sends, prod, eig_rest = kernel_call(
        functools.partial(send_kernel, cuts[2]),
        sources + [(half, False), (eig_next, False), (eigvecs, True)],
        [((rows // 2, w), bf16) for w in widths[1:]]
        + [((rows, depth), bf16), ((cols - cuts[2], depth), bf16)],
        [pltpu.VMEM((rows // 2, max(widths[1:])), jnp.float32), pltpu.SemaphoreType.DMA((1,))],
        (flops(sum(widths[1:])), 2 * sum(widths[1:]) * depth),
    )
    eigs = [eig, eig_next] + [eig_rest] * (len(PLAN) - 2)
    got = [exchange(s, p, 0) for p, s in enumerate([send, *sends])]
    value = []
    for p, width in enumerate(widths):
        value += kernel_call(
            functools.partial(keep_kernel, p, cuts[p] - cuts[min(p, 2)]),
            [(prod, False), (eigs[p], False)],
            [((rows // 2, width), jnp.float32)],
            [],
            (flops(width), 2 * width * depth),
        )
    later = range(3, n.bit_length() - 1)
    token = prod
    for p, stage in ORDER + [(p, stage) for stage in later for p in range(len(PLAN))]:
        part = value[p].shape[0] // 2
        size = part * widths[p]
        leave, value[p] = kernel_call(
            add_kernel,
            [(value[p], False), (got[p], False), (token, None)],
            [((part, widths[p]), bf16 if stage < 3 else jnp.float32)]
            + [((part, widths[p]), jnp.float32)],
            [],
            (2 * size, 18 * size),
        )
        token = leave
        got[p] = exchange(leave, p, stage)
    value = [v[v.shape[0] - rows // n :, :] for v in value]
    last = len(PLAN) - 1
    result = kernel_call(
        functools.partial(early_kernel, last),
        [(v, False) for v in value[:last]] + [(g, False) for g in got[:last]],
        [((rows // n, cols), jnp.float32)],
        [pltpu.VMEM((rows // n, cuts[last]), jnp.float32), pltpu.SemaphoreType.DMA((1,))],
        (rows // n * cuts[last], 10 * rows // n * cuts[last]),
        far_out=True,
    )
    (result,) = kernel_call(
        functools.partial(finish_kernel, cuts[last]),
        [(result[0], True), (value[last], False), (got[last], False)],
        [((rows // n, cols), jnp.float32)],
        [pltpu.VMEM((rows // n, widths[last]), jnp.float32), pltpu.SemaphoreType.DMA((1,))],
        (rows // n * widths[last], 10 * rows // n * widths[last]),
        far_out=True,
        aliases={0: 0},
    )
    return result.reshape(per_chunk, lanc, cols)


def solution(mesh):
    in_specs = (
        P("eig", ("rep", "grid")),
        P(None, ("rep", "grid")),
        P("eig", ("rep", "grid")),
        P("rep"),
    )
    out_specs = P(("rep", "grid"), None, "eig")
    return jax.shard_map(
        functools.partial(per_device, mesh.shape["grid"]),
        mesh=mesh,
        in_specs=in_specs,
        out_specs=out_specs,
        check_vma=False,
    )
```

```python
import functools

import jax
import jax.numpy as jnp
from jax import lax
from jax.experimental import pallas as pl
from jax.experimental.pallas import tpu as pltpu
from jax.sharding import PartitionSpec as P

TILE = 256
VMEM_LIMIT = 32 * 1024 * 1024
X, NEAR, FAR = 0, 1, 2
PLAN = [
    (3.5, (NEAR, X, FAR), (X, FAR, NEAR)),
    (2, (X, NEAR, FAR), (X, FAR, NEAR)),
    (1.5, (NEAR, X, FAR), (FAR, X, NEAR)),
]
ORDER = [(piece, stage) for stage in (1, 2) for piece in range(len(PLAN))]


def ranked(bits, fixed=0):
    out = [fixed]
    for b in reversed(bits):
        out = [c | (1 << b) for c in out] + out
    return out


def split_columns(cols):
    unit = 128
    total = sum(plan[0] for plan in PLAN)
    ends, done = [], 0
    for share, *_ in PLAN[:-1]:
        done += share
        ends.append(int(round(cols * done / total / unit)) * unit)
    ends.append(cols)
    return list(zip([0] + ends[:-1], ends))


def halves(bits):
    keep = ranked(bits[1:])
    return keep, [c | (1 << bits[0]) for c in keep]


def places(p, core, kept):
    keep, leave = halves(PLAN[0][1 + core])
    return [(leave + keep).index(c) for c in halves(PLAN[p][1 + core])[0 if kept else 1]]


def rows_of(prod, p, kept):
    block = prod.shape[0] // 8
    core = lax.axis_index("eig")
    parts = []
    for a, b in zip(places(p, 0, kept), places(p, 1, kept)):
        at = a * block if a == b else pl.multiple_of(jnp.where(core == 0, a, b) * block, block)
        parts.append(prod[pl.ds(at, block), :])
    return jnp.concatenate(parts, axis=0)


def dot_tiles(out, rows, eig, first):
    width = out.shape[1]
    for at in range(0, width, TILE):
        size = min(TILE, width - at)
        out[:, at : at + size] = lax.dot_general(
            rows,
            eig[first + at : first + at + size, :],
            (((1,), (1,)), ((), ())),
            preferred_element_type=jnp.float32,
        )


def setup_kernel(n, per_chunk, lanc, width, order_hbm, own_hbm, lanc_hbm, eig_hbm, *rest):
    pick, own, lanc16, eig, order, sem = rest
    copies = [
        pltpu.make_async_copy(src, dst, sem.at[i])
        for i, (src, dst) in enumerate(
            [
                (order_hbm, order),
                (own_hbm, own),
                (lanc_hbm, lanc16),
                (eig_hbm.at[pl.ds(0, width)], eig),
            ]
        )
    ]
    for copy in copies:
        copy.start()
    me = lax.axis_index("grid")
    core = lax.axis_index("eig")
    bands = pick.shape[1]
    rest_bits = list(range(3, n.bit_length() - 1))
    classes = zip(*(sum(reversed(halves(PLAN[0][1 + i])), []) for i in range(2)))
    slots = []
    for pair in classes:
        for both in zip(*(ranked(rest_bits, c) for c in pair)):
            slots += [(both, j) for j in range(per_chunk)]
    col = lax.broadcasted_iota(jnp.int32, (2 * lanc, bands), 1)
    upper = lax.broadcasted_iota(jnp.int32, (2 * lanc, bands), 0) < lanc
    copies[0].wait()
    for i in range(0, len(slots), 2):
        want = []
        for r, j in slots[i : i + 2]:
            offset = jnp.where(core == 0, r[0], r[1])
            band = order[(me ^ offset) * per_chunk + j]
            want.append(lax.rem(band + core * (bands // 2), bands))
        hit = col == jnp.where(upper, want[0], want[1])
        pick[i * lanc : (i + 2) * lanc, :] = hit.astype(jnp.float32).astype(jnp.bfloat16)
    for copy in copies[1:]:
        copy.wait()


def make_rows(prod, pick, own, other, lanc16, first):
    lanc = lanc16[...].astype(jnp.float32)
    chosen = lax.dot_general(
        pick[first : first + prod.shape[0], :],
        jnp.concatenate([own[...], other[...]], axis=0),
        (((1,), (0,)), ((), ())),
        preferred_element_type=jnp.float32,
    )
    value = chosen.reshape(-1, *lanc.shape) * lanc[None]
    prod[...] = value.reshape(chosen.shape).astype(jnp.bfloat16)


def first_kernel(cut, pick, own, other, lanc16, eig, eig_hbm, out, prod, eig_next, acc, sem):
    copy = pltpu.make_async_copy(
        eig_hbm.at[pl.ds(cut, eig_next.shape[0])], eig_next, sem.at[0]
    )
    copy.start()
    make_rows(prod, pick, own, other, lanc16, 0)
    dot_tiles(acc, prod[...], eig, 0)
    out[...] = acc[...].astype(out.dtype)
    copy.wait()


def send_kernel(cut, pick, own, other, lanc16, half, eig, eig_hbm, *rest):
    *outs, prod, eig_rest, acc, sem = rest
    copy = pltpu.make_async_copy(
        eig_hbm.at[pl.ds(cut, eig_rest.shape[0])], eig_rest, sem.at[0]
    )
    copy.start()
    first = half.shape[0]
    prod[:first, :] = half[...]
    make_rows(prod.at[first:, :], pick, own, other, lanc16, first)
    at = 0
    for i, out in enumerate(outs):
        part = acc.at[:, : out.shape[1]]
        if i == 1:
            copy.wait()
        dot_tiles(part, rows_of(prod, i + 1, False), eig_rest if i else eig, at)
        out[...] = part[...].astype(out.dtype)
        at += out.shape[1] if i else 0


def keep_kernel(p, first, prod, eig, out):
    dot_tiles(out, rows_of(prod, p, True), eig, first)


def add_kernel(kept, got, _, leave, keep):
    mid = leave.shape[0]
    leave[...] = (kept[:mid, :] + got[:mid, :].astype(jnp.float32)).astype(leave.dtype)
    keep[...] = kept[mid:, :] + got[mid:, :].astype(jnp.float32)


def finish_kernel(spans, *refs):
    count = len(spans)
    kept, came, out = refs[:count], refs[count : 2 * count], refs[-1]
    for (at, end), a, b in zip(spans, kept, came):
        out[:, at:end] = a[a.shape[0] - out.shape[0] :, :] + b[...].astype(jnp.float32)


VMEM_SPEC = pl.BlockSpec(memory_space=pltpu.VMEM)
SPECS = {
    True: pl.BlockSpec(memory_space=pltpu.HBM),
    False: VMEM_SPEC,
    None: pl.BlockSpec(memory_space=pl.ANY),
}


def kernel_call(body, ins, outs, scratch, cost):
    flops, moved = cost
    return pl.pallas_call(
        body,
        out_shape=[jax.ShapeDtypeStruct(*out) for out in outs],
        in_specs=[SPECS[far] for _, far in ins],
        out_specs=[VMEM_SPEC] * len(outs),
        scratch_shapes=scratch,
        compiler_params=pltpu.CompilerParams(vmem_limit_bytes=VMEM_LIMIT),
        cost_estimate=pl.CostEstimate(flops=flops, bytes_accessed=moved, transcendentals=0),
    )(
        *(
            pltpu.with_memory_space_constraint(x, pltpu.HBM) if far else x
            for x, far in ins
        )
    )


def per_device(n, eigvecs, lanczos, bands, band_order):
    cols, depth = eigvecs.shape
    lanc = lanczos.shape[0]
    per_chunk = band_order.shape[0] // n
    rows = band_order.shape[0] * lanc
    spans = split_columns(cols)
    cuts = [0] + [end for _, end in spans]
    widths = [end - at for at, end in spans]
    bf16 = jnp.bfloat16

    def exchange(value, p, stage):
        pairs = []
        for i in range(n):
            for core in range(2):
                bit = PLAN[p][1 + core][stage] if stage < 3 else stage
                pairs.append((2 * i + core, 2 * (i ^ (1 << bit)) + core))
        return lax.ppermute(value, ("grid", "eig"), pairs)

    def flops(width):
        return rows * width * depth

    other = lax.ppermute(bands, "eig", [(0, 1), (1, 0)])
    pick, own, lanc16, eig = kernel_call(
        functools.partial(setup_kernel, n, per_chunk, lanc, widths[0]),
        [(band_order, True), (bands, True), (lanczos, True), (eigvecs, True)],
        [
            ((rows, 2 * bands.shape[0]), bf16),
            (bands.shape, bf16),
            (lanczos.shape, bf16),
            ((widths[0], depth), bf16),
        ],
        [pltpu.SMEM(band_order.shape, jnp.int32), pltpu.SemaphoreType.DMA((4,))],
        (0, 2 * widths[0] * depth),
    )
    sources = [(x, False) for x in (pick, own, other, lanc16)]
    send, half, eig_next = kernel_call(
        functools.partial(first_kernel, cuts[1]),
        sources + [(eig, False), (eigvecs, True)],
        [((rows // 2, widths[0]), bf16), ((rows // 2, depth), bf16), ((widths[1], depth), bf16)],
        [pltpu.VMEM((rows // 2, widths[0]), jnp.float32), pltpu.SemaphoreType.DMA((1,))],
        (flops(widths[0]), 2 * widths[0] * depth),
    )
    *sends, prod, eig_rest = kernel_call(
        functools.partial(send_kernel, cuts[2]),
        sources + [(half, False), (eig_next, False), (eigvecs, True)],
        [((rows // 2, w), bf16) for w in widths[1:]]
        + [((rows, depth), bf16), ((cols - cuts[2], depth), bf16)],
        [pltpu.VMEM((rows // 2, max(widths[1:])), jnp.float32), pltpu.SemaphoreType.DMA((1,))],
        (flops(sum(widths[1:])), 2 * sum(widths[1:]) * depth),
    )
    eigs = [eig, eig_next] + [eig_rest] * (len(PLAN) - 2)
    got = [exchange(s, p, 0) for p, s in enumerate([send, *sends])]
    value = []
    for p, width in enumerate(widths):
        value += kernel_call(
            functools.partial(keep_kernel, p, cuts[p] - cuts[min(p, 2)]),
            [(prod, False), (eigs[p], False)],
            [((rows // 2, width), jnp.float32)],
            [],
            (flops(width), 2 * width * depth),
        )
    later = range(3, n.bit_length() - 1)
    token = prod
    for p, stage in ORDER + [(p, stage) for stage in later for p in range(len(PLAN))]:
        part = value[p].shape[0] // 2
        size = part * widths[p]
        leave, value[p] = kernel_call(
            add_kernel,
            [(value[p], False), (got[p], False), (token, None)],
            [((part, widths[p]), bf16 if stage < 3 else jnp.float32)]
            + [((part, widths[p]), jnp.float32)],
            [],
            (2 * size, 18 * size),
        )
        token = leave
        got[p] = exchange(leave, p, stage)
    outs = list(zip(value, got))
    (result,) = kernel_call(
        functools.partial(finish_kernel, spans),
        [(value, False) for value, _ in outs] + [(came, False) for _, came in outs],
        [((rows // n, cols), jnp.float32)],
        [],
        (rows // n * cols, 12 * rows // n * cols),
    )
    return result.reshape(per_chunk, lanc, cols)


def solution(mesh):
    in_specs = (
        P("eig", ("rep", "grid")),
        P(None, ("rep", "grid")),
        P("eig", ("rep", "grid")),
        P("rep"),
    )
    out_specs = P(("rep", "grid"), None, "eig")
    return jax.shard_map(
        functools.partial(per_device, mesh.shape["grid"]),
        mesh=mesh,
        in_specs=in_specs,
        out_specs=out_specs,
        check_vma=False,
    )
```

```python
import functools

import jax
import jax.numpy as jnp
from jax import lax
from jax.experimental import pallas as pl
from jax.experimental.pallas import tpu as pltpu
from jax.sharding import PartitionSpec as P

TILE = 256
VMEM_LIMIT = 32 * 1024 * 1024
X, NEAR, FAR = 0, 1, 2
PLAN = [
    (3, (NEAR, X, FAR), (X, FAR, NEAR)),
    (2, (X, NEAR, FAR), (FAR, X, NEAR)),
    (2, (X, NEAR, FAR), (X, FAR, NEAR)),
]
ORDER = [(piece, stage) for stage in (1, 2) for piece in range(len(PLAN))]


def ranked(bits, fixed=0):
    out = [fixed]
    for b in reversed(bits):
        out = [c | (1 << b) for c in out] + out
    return out


def split_columns(cols):
    unit = 128
    total = sum(plan[0] for plan in PLAN)
    ends, done = [], 0
    for share, *_ in PLAN[:-1]:
        done += share
        ends.append(int(round(cols * done / total / unit)) * unit)
    ends.append(cols)
    return list(zip([0] + ends[:-1], ends))


def halves(bits):
    keep = ranked(bits[1:])
    return keep, [c | (1 << bits[0]) for c in keep]


def places(p, core, kept):
    keep, leave = halves(PLAN[0][1 + core])
    return [(leave + keep).index(c) for c in halves(PLAN[p][1 + core])[0 if kept else 1]]


def rows_of(prod, p, kept):
    block = prod.shape[0] // 8
    core = lax.axis_index("eig")
    parts = []
    for a, b in zip(places(p, 0, kept), places(p, 1, kept)):
        at = a * block if a == b else pl.multiple_of(jnp.where(core == 0, a, b) * block, block)
        parts.append(prod[pl.ds(at, block), :])
    return jnp.concatenate(parts, axis=0)


def dot_tiles(out, rows, eig, first):
    width = out.shape[1]
    for at in range(0, width, TILE):
        size = min(TILE, width - at)
        out[:, at : at + size] = lax.dot_general(
            rows,
            eig[first + at : first + at + size, :],
            (((1,), (1,)), ((), ())),
            preferred_element_type=jnp.float32,
        )


def setup_kernel(n, per_chunk, lanc, width, order_hbm, own_hbm, lanc_hbm, eig_hbm, *rest):
    pick, own, lanc16, eig, order, sem = rest
    copies = [
        pltpu.make_async_copy(src, dst, sem.at[i])
        for i, (src, dst) in enumerate(
            [
                (order_hbm, order),
                (own_hbm, own),
                (lanc_hbm, lanc16),
                (eig_hbm.at[pl.ds(0, width)], eig),
            ]
        )
    ]
    for copy in copies:
        copy.start()
    me = lax.axis_index("grid")
    core = lax.axis_index("eig")
    bands = pick.shape[1]
    rest_bits = list(range(3, n.bit_length() - 1))
    classes = zip(*(sum(reversed(halves(PLAN[0][1 + i])), []) for i in range(2)))
    slots = []
    for pair in classes:
        for both in zip(*(ranked(rest_bits, c) for c in pair)):
            slots += [(both, j) for j in range(per_chunk)]
    col = lax.broadcasted_iota(jnp.int32, (2 * lanc, bands), 1)
    upper = lax.broadcasted_iota(jnp.int32, (2 * lanc, bands), 0) < lanc
    copies[0].wait()
    for i in range(0, len(slots), 2):
        want = []
        for r, j in slots[i : i + 2]:
            offset = jnp.where(core == 0, r[0], r[1])
            band = order[(me ^ offset) * per_chunk + j]
            want.append(lax.rem(band + core * (bands // 2), bands))
        hit = col == jnp.where(upper, want[0], want[1])
        pick[i * lanc : (i + 2) * lanc, :] = hit.astype(jnp.float32).astype(jnp.bfloat16)
    for copy in copies[1:]:
        copy.wait()


def make_rows(prod, pick, own, other, lanc16, first):
    lanc = lanc16[...].astype(jnp.float32)
    chosen = lax.dot_general(
        pick[first : first + prod.shape[0], :],
        jnp.concatenate([own[...], other[...]], axis=0),
        (((1,), (0,)), ((), ())),
        preferred_element_type=jnp.float32,
    )
    value = chosen.reshape(-1, *lanc.shape) * lanc[None]
    prod[...] = value.reshape(chosen.shape).astype(jnp.bfloat16)


def first_kernel(cut, pick, own, other, lanc16, eig, eig_hbm, out, prod, eig_next, acc, sem):
    copy = pltpu.make_async_copy(
        eig_hbm.at[pl.ds(cut, eig_next.shape[0])], eig_next, sem.at[0]
    )
    copy.start()
    make_rows(prod, pick, own, other, lanc16, 0)
    dot_tiles(acc, prod[...], eig, 0)
    out[...] = acc[...].astype(out.dtype)
    copy.wait()


def send_kernel(cut, pick, own, other, lanc16, half, eig, eig_hbm, *rest):
    *outs, prod, eig_rest, acc, sem = rest
    copy = pltpu.make_async_copy(
        eig_hbm.at[pl.ds(cut, eig_rest.shape[0])], eig_rest, sem.at[0]
    )
    copy.start()
    first = half.shape[0]
    prod[:first, :] = half[...]
    make_rows(prod.at[first:, :], pick, own, other, lanc16, first)
    at = 0
    for i, out in enumerate(outs):
        part = acc.at[:, : out.shape[1]]
        if i == 1:
            copy.wait()
        dot_tiles(part, rows_of(prod, i + 1, False), eig_rest if i else eig, at)
        out[...] = part[...].astype(out.dtype)
        at += out.shape[1] if i else 0


def keep_kernel(p, first, prod, eig, out):
    dot_tiles(out, rows_of(prod, p, True), eig, first)


def add_kernel(kept, got, _, leave, keep):
    mid = leave.shape[0]
    leave[...] = (kept[:mid, :] + got[:mid, :].astype(jnp.float32)).astype(leave.dtype)
    keep[...] = kept[mid:, :] + got[mid:, :].astype(jnp.float32)


def write_sums(first, kept, came, out, held, sem):
    at = 0
    for a, b in zip(kept, came):
        end = at + a.shape[1]
        held[:, at:end] = a[...] + b[...].astype(jnp.float32)
        at = end
    copy = pltpu.make_async_copy(held, out.at[:, pl.ds(first, at)], sem.at[0])
    copy.start()
    copy.wait()


def early_kernel(count, *refs):
    write_sums(0, refs[:count], refs[count : 2 * count], *refs[2 * count :])


def finish_kernel(first, _, kept, came, out, held, sem):
    write_sums(first, [kept], [came], out, held, sem)


VMEM_SPEC = pl.BlockSpec(memory_space=pltpu.VMEM)
SPECS = {
    True: pl.BlockSpec(memory_space=pltpu.HBM),
    False: VMEM_SPEC,
    None: pl.BlockSpec(memory_space=pl.ANY),
}


def kernel_call(body, ins, outs, scratch, cost, far_out=False, aliases={}):
    flops, moved = cost
    return pl.pallas_call(
        body,
        out_shape=[jax.ShapeDtypeStruct(*out) for out in outs],
        in_specs=[SPECS[far] for _, far in ins],
        out_specs=[SPECS[far_out]] * len(outs),
        scratch_shapes=scratch,
        input_output_aliases=aliases,
        compiler_params=pltpu.CompilerParams(vmem_limit_bytes=VMEM_LIMIT),
        cost_estimate=pl.CostEstimate(flops=flops, bytes_accessed=moved, transcendentals=0),
    )(
        *(
            pltpu.with_memory_space_constraint(x, pltpu.HBM) if far else x
            for x, far in ins
        )
    )


def per_device(n, eigvecs, lanczos, bands, band_order):
    cols, depth = eigvecs.shape
    lanc = lanczos.shape[0]
    per_chunk = band_order.shape[0] // n
    rows = band_order.shape[0] * lanc
    spans = split_columns(cols)
    cuts = [0] + [end for _, end in spans]
    widths = [end - at for at, end in spans]
    bf16 = jnp.bfloat16

    def exchange(value, p, stage):
        pairs = []
        for i in range(n):
            for core in range(2):
                bit = PLAN[p][1 + core][stage] if stage < 3 else stage
                pairs.append((2 * i + core, 2 * (i ^ (1 << bit)) + core))
        return lax.ppermute(value, ("grid", "eig"), pairs)

    def flops(width):
        return rows * width * depth

    other = lax.ppermute(bands, "eig", [(0, 1), (1, 0)])
    pick, own, lanc16, eig = kernel_call(
        functools.partial(setup_kernel, n, per_chunk, lanc, widths[0]),
        [(band_order, True), (bands, True), (lanczos, True), (eigvecs, True)],
        [
            ((rows, 2 * bands.shape[0]), bf16),
            (bands.shape, bf16),
            (lanczos.shape, bf16),
            ((widths[0], depth), bf16),
        ],
        [pltpu.SMEM(band_order.shape, jnp.int32), pltpu.SemaphoreType.DMA((4,))],
        (0, 2 * widths[0] * depth),
    )
    sources = [(x, False) for x in (pick, own, other, lanc16)]
    send, half, eig_next = kernel_call(
        functools.partial(first_kernel, cuts[1]),
        sources + [(eig, False), (eigvecs, True)],
        [((rows // 2, widths[0]), bf16), ((rows // 2, depth), bf16), ((widths[1], depth), bf16)],
        [pltpu.VMEM((rows // 2, widths[0]), jnp.float32), pltpu.SemaphoreType.DMA((1,))],
        (flops(widths[0]), 2 * widths[0] * depth),
    )
    *sends, prod, eig_rest = kernel_call(
        functools.partial(send_kernel, cuts[2]),
        sources + [(half, False), (eig_next, False), (eigvecs, True)],
        [((rows // 2, w), bf16) for w in widths[1:]]
        + [((rows, depth), bf16), ((cols - cuts[2], depth), bf16)],
        [pltpu.VMEM((rows // 2, max(widths[1:])), jnp.float32), pltpu.SemaphoreType.DMA((1,))],
        (flops(sum(widths[1:])), 2 * sum(widths[1:]) * depth),
    )
    eigs = [eig, eig_next] + [eig_rest] * (len(PLAN) - 2)
    got = [exchange(s, p, 0) for p, s in enumerate([send, *sends])]
    value = []
    for p, width in enumerate(widths):
        value += kernel_call(
            functools.partial(keep_kernel, p, cuts[p] - cuts[min(p, 2)]),
            [(prod, False), (eigs[p], False)],
            [((rows // 2, width), jnp.float32)],
            [],
            (flops(width), 2 * width * depth),
        )
    later = range(3, n.bit_length() - 1)
    token = prod
    for p, stage in ORDER + [(p, stage) for stage in later for p in range(len(PLAN))]:
        part = value[p].shape[0] // 2
        size = part * widths[p]
        leave, value[p] = kernel_call(
            add_kernel,
            [(value[p], False), (got[p], False), (token, None)],
            [((part, widths[p]), bf16 if stage < 3 else jnp.float32)]
            + [((part, widths[p]), jnp.float32)],
            [],
            (2 * size, 18 * size),
        )
        token = leave
        got[p] = exchange(leave, p, stage)
    value = [v[v.shape[0] - rows // n :, :] for v in value]
    last = len(PLAN) - 1
    result = kernel_call(
        functools.partial(early_kernel, last),
        [(v, False) for v in value[:last]] + [(g, False) for g in got[:last]],
        [((rows // n, cols), jnp.float32)],
        [pltpu.VMEM((rows // n, cuts[last]), jnp.float32), pltpu.SemaphoreType.DMA((1,))],
        (rows // n * cuts[last], 10 * rows // n * cuts[last]),
        far_out=True,
    )
    (result,) = kernel_call(
        functools.partial(finish_kernel, cuts[last]),
        [(result[0], True), (value[last], False), (got[last], False)],
        [((rows // n, cols), jnp.float32)],
        [pltpu.VMEM((rows // n, widths[last]), jnp.float32), pltpu.SemaphoreType.DMA((1,))],
        (rows // n * widths[last], 10 * rows // n * widths[last]),
        far_out=True,
        aliases={0: 0},
    )
    return result.reshape(per_chunk, lanc, cols)


def solution(mesh):
    in_specs = (
        P("eig", ("rep", "grid")),
        P(None, ("rep", "grid")),
        P("eig", ("rep", "grid")),
        P("rep"),
    )
    out_specs = P(("rep", "grid"), None, "eig")
    return jax.shard_map(
        functools.partial(per_device, mesh.shape["grid"]),
        mesh=mesh,
        in_specs=in_specs,
        out_specs=out_specs,
        check_vma=False,
    )
```

```python
import functools

import jax
import jax.numpy as jnp
from jax import lax
from jax.experimental import pallas as pl
from jax.experimental.pallas import tpu as pltpu
from jax.sharding import PartitionSpec as P

TILE = 256
VMEM_LIMIT = 32 * 1024 * 1024
X, NEAR, FAR = 0, 1, 2
PLAN = [
    (3, (NEAR, X, FAR), (X, FAR, NEAR)),
    (2, (NEAR, X, FAR), (X, FAR, NEAR)),
    (2, (X, NEAR, FAR), (FAR, X, NEAR)),
]
ORDER = [(piece, stage) for stage in (1, 2) for piece in range(len(PLAN))]


def ranked(bits, fixed=0):
    out = [fixed]
    for b in reversed(bits):
        out = [c | (1 << b) for c in out] + out
    return out


def split_columns(cols):
    unit = 128
    total = sum(plan[0] for plan in PLAN)
    ends, done = [], 0
    for share, *_ in PLAN[:-1]:
        done += share
        ends.append(int(round(cols * done / total / unit)) * unit)
    ends.append(cols)
    return list(zip([0] + ends[:-1], ends))


def halves(bits):
    keep = ranked(bits[1:])
    return keep, [c | (1 << bits[0]) for c in keep]


def places(p, core, kept):
    keep, leave = halves(PLAN[0][1 + core])
    return [(leave + keep).index(c) for c in halves(PLAN[p][1 + core])[0 if kept else 1]]


def rows_of(prod, p, kept):
    block = prod.shape[0] // 8
    core = lax.axis_index("eig")
    parts = []
    for a, b in zip(places(p, 0, kept), places(p, 1, kept)):
        at = a * block if a == b else pl.multiple_of(jnp.where(core == 0, a, b) * block, block)
        parts.append(prod[pl.ds(at, block), :])
    return jnp.concatenate(parts, axis=0)


def dot_tiles(out, rows, eig, first):
    width = out.shape[1]
    for at in range(0, width, TILE):
        size = min(TILE, width - at)
        out[:, at : at + size] = lax.dot_general(
            rows,
            eig[first + at : first + at + size, :],
            (((1,), (1,)), ((), ())),
            preferred_element_type=jnp.float32,
        )


def setup_kernel(n, per_chunk, lanc, width, order_hbm, own_hbm, lanc_hbm, eig_hbm, *rest):
    pick, own, lanc16, eig, order, sem = rest
    copies = [
        pltpu.make_async_copy(src, dst, sem.at[i])
        for i, (src, dst) in enumerate(
            [
                (order_hbm, order),
                (own_hbm, own),
                (lanc_hbm, lanc16),
                (eig_hbm.at[pl.ds(0, width)], eig),
            ]
        )
    ]
    for copy in copies:
        copy.start()
    me = lax.axis_index("grid")
    core = lax.axis_index("eig")
    bands = pick.shape[1]
    rest_bits = list(range(3, n.bit_length() - 1))
    classes = zip(*(sum(reversed(halves(PLAN[0][1 + i])), []) for i in range(2)))
    slots = []
    for pair in classes:
        for both in zip(*(ranked(rest_bits, c) for c in pair)):
            slots += [(both, j) for j in range(per_chunk)]
    col = lax.broadcasted_iota(jnp.int32, (2 * lanc, bands), 1)
    upper = lax.broadcasted_iota(jnp.int32, (2 * lanc, bands), 0) < lanc
    copies[0].wait()
    for i in range(0, len(slots), 2):
        want = []
        for r, j in slots[i : i + 2]:
            offset = jnp.where(core == 0, r[0], r[1])
            band = order[(me ^ offset) * per_chunk + j]
            want.append(lax.rem(band + core * (bands // 2), bands))
        hit = col == jnp.where(upper, want[0], want[1])
        pick[i * lanc : (i + 2) * lanc, :] = hit.astype(jnp.float32).astype(jnp.bfloat16)
    for copy in copies[1:]:
        copy.wait()


def make_rows(prod, pick, own, other, lanc16, first):
    lanc = lanc16[...].astype(jnp.float32)
    chosen = lax.dot_general(
        pick[first : first + prod.shape[0], :],
        jnp.concatenate([own[...], other[...]], axis=0),
        (((1,), (0,)), ((), ())),
        preferred_element_type=jnp.float32,
    )
    value = chosen.reshape(-1, *lanc.shape) * lanc[None]
    prod[...] = value.reshape(chosen.shape).astype(jnp.bfloat16)


def first_kernel(cut, pick, own, other, lanc16, eig, eig_hbm, out, prod, eig_next, acc, sem):
    copy = pltpu.make_async_copy(
        eig_hbm.at[pl.ds(cut, eig_next.shape[0])], eig_next, sem.at[0]
    )
    copy.start()
    make_rows(prod, pick, own, other, lanc16, 0)
    dot_tiles(acc, prod[...], eig, 0)
    out[...] = acc[...].astype(out.dtype)
    copy.wait()


def send_kernel(cut, pick, own, other, lanc16, half, eig, eig_hbm, *rest):
    *outs, prod, eig_rest, acc, sem = rest
    copy = pltpu.make_async_copy(
        eig_hbm.at[pl.ds(cut, eig_rest.shape[0])], eig_rest, sem.at[0]
    )
    copy.start()
    first = half.shape[0]
    prod[:first, :] = half[...]
    make_rows(prod.at[first:, :], pick, own, other, lanc16, first)
    at = 0
    for i, out in enumerate(outs):
        part = acc.at[:, : out.shape[1]]
        if i == 1:
            copy.wait()
        dot_tiles(part, rows_of(prod, i + 1, False), eig_rest if i else eig, at)
        out[...] = part[...].astype(out.dtype)
        at += out.shape[1] if i else 0


def keep_kernel(p, first, prod, eig, out):
    dot_tiles(out, rows_of(prod, p, True), eig, first)


def add_kernel(kept, got, _, leave, keep):
    mid = leave.shape[0]
    leave[...] = (kept[:mid, :] + got[:mid, :].astype(jnp.float32)).astype(leave.dtype)
    keep[...] = kept[mid:, :] + got[mid:, :].astype(jnp.float32)


def write_sums(first, kept, came, out, held, sem):
    at = 0
    for a, b in zip(kept, came):
        end = at + a.shape[1]
        held[:, at:end] = a[...] + b[...].astype(jnp.float32)
        at = end
    copy = pltpu.make_async_copy(held, out.at[:, pl.ds(first, at)], sem.at[0])
    copy.start()
    copy.wait()


def early_kernel(count, *refs):
    write_sums(0, refs[:count], refs[count : 2 * count], *refs[2 * count :])


def finish_kernel(first, _, kept, came, out, held, sem):
    write_sums(first, [kept], [came], out, held, sem)


VMEM_SPEC = pl.BlockSpec(memory_space=pltpu.VMEM)
SPECS = {
    True: pl.BlockSpec(memory_space=pltpu.HBM),
    False: VMEM_SPEC,
    None: pl.BlockSpec(memory_space=pl.ANY),
}


def kernel_call(body, ins, outs, scratch, cost, far_out=False, aliases={}):
    flops, moved = cost
    return pl.pallas_call(
        body,
        out_shape=[jax.ShapeDtypeStruct(*out) for out in outs],
        in_specs=[SPECS[far] for _, far in ins],
        out_specs=[SPECS[far_out]] * len(outs),
        scratch_shapes=scratch,
        input_output_aliases=aliases,
        compiler_params=pltpu.CompilerParams(vmem_limit_bytes=VMEM_LIMIT),
        cost_estimate=pl.CostEstimate(flops=flops, bytes_accessed=moved, transcendentals=0),
    )(
        *(
            pltpu.with_memory_space_constraint(x, pltpu.HBM) if far else x
            for x, far in ins
        )
    )


def per_device(n, eigvecs, lanczos, bands, band_order):
    cols, depth = eigvecs.shape
    lanc = lanczos.shape[0]
    per_chunk = band_order.shape[0] // n
    rows = band_order.shape[0] * lanc
    spans = split_columns(cols)
    cuts = [0] + [end for _, end in spans]
    widths = [end - at for at, end in spans]
    bf16 = jnp.bfloat16

    def exchange(value, p, stage):
        pairs = []
        for i in range(n):
            for core in range(2):
                bit = PLAN[p][1 + core][stage] if stage < 3 else stage
                pairs.append((2 * i + core, 2 * (i ^ (1 << bit)) + core))
        return lax.ppermute(value, ("grid", "eig"), pairs)

    def flops(width):
        return rows * width * depth

    other = lax.ppermute(bands, "eig", [(0, 1), (1, 0)])
    pick, own, lanc16, eig = kernel_call(
        functools.partial(setup_kernel, n, per_chunk, lanc, widths[0]),
        [(band_order, True), (bands, True), (lanczos, True), (eigvecs, True)],
        [
            ((rows, 2 * bands.shape[0]), bf16),
            (bands.shape, bf16),
            (lanczos.shape, bf16),
            ((widths[0], depth), bf16),
        ],
        [pltpu.SMEM(band_order.shape, jnp.int32), pltpu.SemaphoreType.DMA((4,))],
        (0, 2 * widths[0] * depth),
    )
    sources = [(x, False) for x in (pick, own, other, lanc16)]
    send, half, eig_next = kernel_call(
        functools.partial(first_kernel, cuts[1]),
        sources + [(eig, False), (eigvecs, True)],
        [((rows // 2, widths[0]), bf16), ((rows // 2, depth), bf16), ((widths[1], depth), bf16)],
        [pltpu.VMEM((rows // 2, widths[0]), jnp.float32), pltpu.SemaphoreType.DMA((1,))],
        (flops(widths[0]), 2 * widths[0] * depth),
    )
    *sends, prod, eig_rest = kernel_call(
        functools.partial(send_kernel, cuts[2]),
        sources + [(half, False), (eig_next, False), (eigvecs, True)],
        [((rows // 2, w), bf16) for w in widths[1:]]
        + [((rows, depth), bf16), ((cols - cuts[2], depth), bf16)],
        [pltpu.VMEM((rows // 2, max(widths[1:])), jnp.float32), pltpu.SemaphoreType.DMA((1,))],
        (flops(sum(widths[1:])), 2 * sum(widths[1:]) * depth),
    )
    eigs = [eig, eig_next] + [eig_rest] * (len(PLAN) - 2)
    got = [exchange(s, p, 0) for p, s in enumerate([send, *sends])]
    value = []
    for p, width in enumerate(widths):
        value += kernel_call(
            functools.partial(keep_kernel, p, cuts[p] - cuts[min(p, 2)]),
            [(prod, False), (eigs[p], False)],
            [((rows // 2, width), jnp.float32)],
            [],
            (flops(width), 2 * width * depth),
        )
    later = range(3, n.bit_length() - 1)
    token = prod
    for p, stage in ORDER + [(p, stage) for stage in later for p in range(len(PLAN))]:
        part = value[p].shape[0] // 2
        size = part * widths[p]
        leave, value[p] = kernel_call(
            add_kernel,
            [(value[p], False), (got[p], False), (token, None)],
            [((part, widths[p]), bf16 if stage < 3 else jnp.float32)]
            + [((part, widths[p]), jnp.float32)],
            [],
            (2 * size, 18 * size),
        )
        token = leave
        got[p] = exchange(leave, p, stage)
    value = [v[v.shape[0] - rows // n :, :] for v in value]
    last = len(PLAN) - 1
    result = kernel_call(
        functools.partial(early_kernel, last),
        [(v, False) for v in value[:last]] + [(g, False) for g in got[:last]],
        [((rows // n, cols), jnp.float32)],
        [pltpu.VMEM((rows // n, cuts[last]), jnp.float32), pltpu.SemaphoreType.DMA((1,))],
        (rows // n * cuts[last], 10 * rows // n * cuts[last]),
        far_out=True,
    )
    (result,) = kernel_call(
        functools.partial(finish_kernel, cuts[last]),
        [(result[0], True), (value[last], False), (got[last], False)],
        [((rows // n, cols), jnp.float32)],
        [pltpu.VMEM((rows // n, widths[last]), jnp.float32), pltpu.SemaphoreType.DMA((1,))],
        (rows // n * widths[last], 10 * rows // n * widths[last]),
        far_out=True,
        aliases={0: 0},
    )
    return result.reshape(per_chunk, lanc, cols)


def solution(mesh):
    in_specs = (
        P("eig", ("rep", "grid")),
        P(None, ("rep", "grid")),
        P("eig", ("rep", "grid")),
        P("rep"),
    )
    out_specs = P(("rep", "grid"), None, "eig")
    return jax.shard_map(
        functools.partial(per_device, mesh.shape["grid"]),
        mesh=mesh,
        in_specs=in_specs,
        out_specs=out_specs,
        check_vma=False,
    )
```

```python
import functools

import jax
import jax.numpy as jnp
from jax import lax
from jax.experimental import pallas as pl
from jax.experimental.pallas import tpu as pltpu
from jax.sharding import PartitionSpec as P

TILE = 256
VMEM_LIMIT = 32 * 1024 * 1024
X, NEAR, FAR = 0, 1, 2
PLAN = [
    (3, (NEAR, X, FAR), (X, FAR, NEAR)),
    (2, (X, FAR, NEAR), (FAR, X, NEAR)),
    (2, (NEAR, X, FAR), (X, FAR, NEAR)),
]
ORDER = [(piece, stage) for stage in (1, 2) for piece in range(len(PLAN))]


def ranked(bits, fixed=0):
    out = [fixed]
    for b in reversed(bits):
        out = [c | (1 << b) for c in out] + out
    return out


def split_columns(cols):
    unit = 128
    total = sum(plan[0] for plan in PLAN)
    ends, done = [], 0
    for share, *_ in PLAN[:-1]:
        done += share
        ends.append(int(round(cols * done / total / unit)) * unit)
    ends.append(cols)
    return list(zip([0] + ends[:-1], ends))


def halves(bits):
    keep = ranked(bits[1:])
    return keep, [c | (1 << bits[0]) for c in keep]


def places(p, core, kept):
    keep, leave = halves(PLAN[0][1 + core])
    return [(leave + keep).index(c) for c in halves(PLAN[p][1 + core])[0 if kept else 1]]


def rows_of(prod, p, kept):
    block = prod.shape[0] // 8
    core = lax.axis_index("eig")
    parts = []
    for a, b in zip(places(p, 0, kept), places(p, 1, kept)):
        at = a * block if a == b else pl.multiple_of(jnp.where(core == 0, a, b) * block, block)
        parts.append(prod[pl.ds(at, block), :])
    return jnp.concatenate(parts, axis=0)


def dot_tiles(out, rows, eig, first):
    width = out.shape[1]
    for at in range(0, width, TILE):
        size = min(TILE, width - at)
        out[:, at : at + size] = lax.dot_general(
            rows,
            eig[first + at : first + at + size, :],
            (((1,), (1,)), ((), ())),
            preferred_element_type=jnp.float32,
        )


def setup_kernel(n, per_chunk, lanc, width, order_hbm, own_hbm, lanc_hbm, eig_hbm, *rest):
    pick, own, lanc16, eig, order, sem = rest
    copies = [
        pltpu.make_async_copy(src, dst, sem.at[i])
        for i, (src, dst) in enumerate(
            [
                (order_hbm, order),
                (own_hbm, own),
                (lanc_hbm, lanc16),
                (eig_hbm.at[pl.ds(0, width)], eig),
            ]
        )
    ]
    for copy in copies:
        copy.start()
    me = lax.axis_index("grid")
    core = lax.axis_index("eig")
    bands = pick.shape[1]
    rest_bits = list(range(3, n.bit_length() - 1))
    classes = zip(*(sum(reversed(halves(PLAN[0][1 + i])), []) for i in range(2)))
    slots = []
    for pair in classes:
        for both in zip(*(ranked(rest_bits, c) for c in pair)):
            slots += [(both, j) for j in range(per_chunk)]
    col = lax.broadcasted_iota(jnp.int32, (2 * lanc, bands), 1)
    upper = lax.broadcasted_iota(jnp.int32, (2 * lanc, bands), 0) < lanc
    copies[0].wait()
    for i in range(0, len(slots), 2):
        want = []
        for r, j in slots[i : i + 2]:
            offset = jnp.where(core == 0, r[0], r[1])
            band = order[(me ^ offset) * per_chunk + j]
            want.append(lax.rem(band + core * (bands // 2), bands))
        hit = col == jnp.where(upper, want[0], want[1])
        pick[i * lanc : (i + 2) * lanc, :] = hit.astype(jnp.float32).astype(jnp.bfloat16)
    for copy in copies[1:]:
        copy.wait()


def make_rows(prod, pick, own, other, lanc16, first):
    lanc = lanc16[...].astype(jnp.float32)
    chosen = lax.dot_general(
        pick[first : first + prod.shape[0], :],
        jnp.concatenate([own[...], other[...]], axis=0),
        (((1,), (0,)), ((), ())),
        preferred_element_type=jnp.float32,
    )
    value = chosen.reshape(-1, *lanc.shape) * lanc[None]
    prod[...] = value.reshape(chosen.shape).astype(jnp.bfloat16)


def first_kernel(cut, pick, own, other, lanc16, eig, eig_hbm, out, prod, eig_next, acc, sem):
    copy = pltpu.make_async_copy(
        eig_hbm.at[pl.ds(cut, eig_next.shape[0])], eig_next, sem.at[0]
    )
    copy.start()
    make_rows(prod, pick, own, other, lanc16, 0)
    dot_tiles(acc, prod[...], eig, 0)
    out[...] = acc[...].astype(out.dtype)
    copy.wait()


def send_kernel(cut, pick, own, other, lanc16, half, eig, eig_hbm, *rest):
    *outs, prod, eig_rest, acc, sem = rest
    copy = pltpu.make_async_copy(
        eig_hbm.at[pl.ds(cut, eig_rest.shape[0])], eig_rest, sem.at[0]
    )
    copy.start()
    first = half.shape[0]
    prod[:first, :] = half[...]
    make_rows(prod.at[first:, :], pick, own, other, lanc16, first)
    at = 0
    for i, out in enumerate(outs):
        part = acc.at[:, : out.shape[1]]
        if i == 1:
            copy.wait()
        dot_tiles(part, rows_of(prod, i + 1, False), eig_rest if i else eig, at)
        out[...] = part[...].astype(out.dtype)
        at += out.shape[1] if i else 0


def keep_kernel(p, first, prod, eig, out):
    dot_tiles(out, rows_of(prod, p, True), eig, first)


def add_kernel(kept, got, _, leave, keep):
    mid = leave.shape[0]
    leave[...] = (kept[:mid, :] + got[:mid, :].astype(jnp.float32)).astype(leave.dtype)
    keep[...] = kept[mid:, :] + got[mid:, :].astype(jnp.float32)


def write_sums(first, kept, came, out, held, sem):
    at = 0
    for a, b in zip(kept, came):
        end = at + a.shape[1]
        held[:, at:end] = a[...] + b[...].astype(jnp.float32)
        at = end
    copy = pltpu.make_async_copy(held, out.at[:, pl.ds(first, at)], sem.at[0])
    copy.start()
    copy.wait()


def early_kernel(count, *refs):
    write_sums(0, refs[:count], refs[count : 2 * count], *refs[2 * count :])


def finish_kernel(first, _, kept, came, out, held, sem):
    write_sums(first, [kept], [came], out, held, sem)


VMEM_SPEC = pl.BlockSpec(memory_space=pltpu.VMEM)
SPECS = {
    True: pl.BlockSpec(memory_space=pltpu.HBM),
    False: VMEM_SPEC,
    None: pl.BlockSpec(memory_space=pl.ANY),
}


def kernel_call(body, ins, outs, scratch, cost, far_out=False, aliases={}):
    flops, moved = cost
    return pl.pallas_call(
        body,
        out_shape=[jax.ShapeDtypeStruct(*out) for out in outs],
        in_specs=[SPECS[far] for _, far in ins],
        out_specs=[SPECS[far_out]] * len(outs),
        scratch_shapes=scratch,
        input_output_aliases=aliases,
        compiler_params=pltpu.CompilerParams(vmem_limit_bytes=VMEM_LIMIT),
        cost_estimate=pl.CostEstimate(flops=flops, bytes_accessed=moved, transcendentals=0),
    )(
        *(
            pltpu.with_memory_space_constraint(x, pltpu.HBM) if far else x
            for x, far in ins
        )
    )


def per_device(n, eigvecs, lanczos, bands, band_order):
    cols, depth = eigvecs.shape
    lanc = lanczos.shape[0]
    per_chunk = band_order.shape[0] // n
    rows = band_order.shape[0] * lanc
    spans = split_columns(cols)
    cuts = [0] + [end for _, end in spans]
    widths = [end - at for at, end in spans]
    bf16 = jnp.bfloat16

    def exchange(value, p, stage):
        pairs = []
        for i in range(n):
            for core in range(2):
                bit = PLAN[p][1 + core][stage] if stage < 3 else stage
                pairs.append((2 * i + core, 2 * (i ^ (1 << bit)) + core))
        return lax.ppermute(value, ("grid", "eig"), pairs)

    def flops(width):
        return rows * width * depth

    other = lax.ppermute(bands, "eig", [(0, 1), (1, 0)])
    pick, own, lanc16, eig = kernel_call(
        functools.partial(setup_kernel, n, per_chunk, lanc, widths[0]),
        [(band_order, True), (bands, True), (lanczos, True), (eigvecs, True)],
        [
            ((rows, 2 * bands.shape[0]), bf16),
            (bands.shape, bf16),
            (lanczos.shape, bf16),
            ((widths[0], depth), bf16),
        ],
        [pltpu.SMEM(band_order.shape, jnp.int32), pltpu.SemaphoreType.DMA((4,))],
        (0, 2 * widths[0] * depth),
    )
    sources = [(x, False) for x in (pick, own, other, lanc16)]
    send, half, eig_next = kernel_call(
        functools.partial(first_kernel, cuts[1]),
        sources + [(eig, False), (eigvecs, True)],
        [((rows // 2, widths[0]), bf16), ((rows // 2, depth), bf16), ((widths[1], depth), bf16)],
        [pltpu.VMEM((rows // 2, widths[0]), jnp.float32), pltpu.SemaphoreType.DMA((1,))],
        (flops(widths[0]), 2 * widths[0] * depth),
    )
    *sends, prod, eig_rest = kernel_call(
        functools.partial(send_kernel, cuts[2]),
        sources + [(half, False), (eig_next, False), (eigvecs, True)],
        [((rows // 2, w), bf16) for w in widths[1:]]
        + [((rows, depth), bf16), ((cols - cuts[2], depth), bf16)],
        [pltpu.VMEM((rows // 2, max(widths[1:])), jnp.float32), pltpu.SemaphoreType.DMA((1,))],
        (flops(sum(widths[1:])), 2 * sum(widths[1:]) * depth),
    )
    eigs = [eig, eig_next] + [eig_rest] * (len(PLAN) - 2)
    got = [exchange(s, p, 0) for p, s in enumerate([send, *sends])]
    value = []
    for p, width in enumerate(widths):
        value += kernel_call(
            functools.partial(keep_kernel, p, cuts[p] - cuts[min(p, 2)]),
            [(prod, False), (eigs[p], False)],
            [((rows // 2, width), jnp.float32)],
            [],
            (flops(width), 2 * width * depth),
        )
    later = range(3, n.bit_length() - 1)
    token = prod
    for p, stage in ORDER + [(p, stage) for stage in later for p in range(len(PLAN))]:
        part = value[p].shape[0] // 2
        size = part * widths[p]
        leave, value[p] = kernel_call(
            add_kernel,
            [(value[p], False), (got[p], False), (token, None)],
            [((part, widths[p]), bf16 if stage < 3 else jnp.float32)]
            + [((part, widths[p]), jnp.float32)],
            [],
            (2 * size, 18 * size),
        )
        token = leave
        got[p] = exchange(leave, p, stage)
    value = [v[v.shape[0] - rows // n :, :] for v in value]
    last = len(PLAN) - 1
    result = kernel_call(
        functools.partial(early_kernel, last),
        [(v, False) for v in value[:last]] + [(g, False) for g in got[:last]],
        [((rows // n, cols), jnp.float32)],
        [pltpu.VMEM((rows // n, cuts[last]), jnp.float32), pltpu.SemaphoreType.DMA((1,))],
        (rows // n * cuts[last], 10 * rows // n * cuts[last]),
        far_out=True,
    )
    (result,) = kernel_call(
        functools.partial(finish_kernel, cuts[last]),
        [(result[0], True), (value[last], False), (got[last], False)],
        [((rows // n, cols), jnp.float32)],
        [pltpu.VMEM((rows // n, widths[last]), jnp.float32), pltpu.SemaphoreType.DMA((1,))],
        (rows // n * widths[last], 10 * rows // n * widths[last]),
        far_out=True,
        aliases={0: 0},
    )
    return result.reshape(per_chunk, lanc, cols)


def solution(mesh):
    in_specs = (
        P("eig", ("rep", "grid")),
        P(None, ("rep", "grid")),
        P("eig", ("rep", "grid")),
        P("rep"),
    )
    out_specs = P(("rep", "grid"), None, "eig")
    return jax.shard_map(
        functools.partial(per_device, mesh.shape["grid"]),
        mesh=mesh,
        in_specs=in_specs,
        out_specs=out_specs,
        check_vma=False,
    )
```

```python
import functools

import jax
import jax.numpy as jnp
from jax import lax
from jax.experimental import pallas as pl
from jax.experimental.pallas import tpu as pltpu
from jax.sharding import PartitionSpec as P

TILE = 256
VMEM_LIMIT = 32 * 1024 * 1024
X, NEAR, FAR = 0, 1, 2
PLAN = [
    (3, (NEAR, X, FAR), (X, FAR, NEAR)),
    (2, (X, NEAR, FAR), (FAR, X, NEAR)),
    (2, (NEAR, X, FAR), (X, NEAR, FAR)),
]
ORDER = [(piece, stage) for stage in (1, 2) for piece in range(len(PLAN))]


def ranked(bits, fixed=0):
    out = [fixed]
    for b in reversed(bits):
        out = [c | (1 << b) for c in out] + out
    return out


def split_columns(cols):
    unit = 128
    total = sum(plan[0] for plan in PLAN)
    ends, done = [], 0
    for share, *_ in PLAN[:-1]:
        done += share
        ends.append(int(round(cols * done / total / unit)) * unit)
    ends.append(cols)
    return list(zip([0] + ends[:-1], ends))


def halves(bits):
    keep = ranked(bits[1:])
    return keep, [c | (1 << bits[0]) for c in keep]


def places(p, core, kept):
    keep, leave = halves(PLAN[0][1 + core])
    return [(leave + keep).index(c) for c in halves(PLAN[p][1 + core])[0 if kept else 1]]


def rows_of(prod, p, kept):
    block = prod.shape[0] // 8
    core = lax.axis_index("eig")
    parts = []
    for a, b in zip(places(p, 0, kept), places(p, 1, kept)):
        at = a * block if a == b else pl.multiple_of(jnp.where(core == 0, a, b) * block, block)
        parts.append(prod[pl.ds(at, block), :])
    return jnp.concatenate(parts, axis=0)


def dot_tiles(out, rows, eig, first):
    width = out.shape[1]
    for at in range(0, width, TILE):
        size = min(TILE, width - at)
        out[:, at : at + size] = lax.dot_general(
            rows,
            eig[first + at : first + at + size, :],
            (((1,), (1,)), ((), ())),
            preferred_element_type=jnp.float32,
        )


def setup_kernel(n, per_chunk, lanc, width, order_hbm, own_hbm, lanc_hbm, eig_hbm, *rest):
    pick, own, lanc16, eig, order, sem = rest
    copies = [
        pltpu.make_async_copy(src, dst, sem.at[i])
        for i, (src, dst) in enumerate(
            [
                (order_hbm, order),
                (own_hbm, own),
                (lanc_hbm, lanc16),
                (eig_hbm.at[pl.ds(0, width)], eig),
            ]
        )
    ]
    for copy in copies:
        copy.start()
    me = lax.axis_index("grid")
    core = lax.axis_index("eig")
    bands = pick.shape[1]
    rest_bits = list(range(3, n.bit_length() - 1))
    classes = zip(*(sum(reversed(halves(PLAN[0][1 + i])), []) for i in range(2)))
    slots = []
    for pair in classes:
        for both in zip(*(ranked(rest_bits, c) for c in pair)):
            slots += [(both, j) for j in range(per_chunk)]
    col = lax.broadcasted_iota(jnp.int32, (2 * lanc, bands), 1)
    upper = lax.broadcasted_iota(jnp.int32, (2 * lanc, bands), 0) < lanc
    copies[0].wait()
    for i in range(0, len(slots), 2):
        want = []
        for r, j in slots[i : i + 2]:
            offset = jnp.where(core == 0, r[0], r[1])
            band = order[(me ^ offset) * per_chunk + j]
            want.append(lax.rem(band + core * (bands // 2), bands))
        hit = col == jnp.where(upper, want[0], want[1])
        pick[i * lanc : (i + 2) * lanc, :] = hit.astype(jnp.float32).astype(jnp.bfloat16)
    for copy in copies[1:]:
        copy.wait()


def make_rows(prod, pick, own, other, lanc16, first):
    lanc = lanc16[...].astype(jnp.float32)
    chosen = lax.dot_general(
        pick[first : first + prod.shape[0], :],
        jnp.concatenate([own[...], other[...]], axis=0),
        (((1,), (0,)), ((), ())),
        preferred_element_type=jnp.float32,
    )
    value = chosen.reshape(-1, *lanc.shape) * lanc[None]
    prod[...] = value.reshape(chosen.shape).astype(jnp.bfloat16)


def first_kernel(cut, pick, own, other, lanc16, eig, eig_hbm, out, prod, eig_next, acc, sem):
    copy = pltpu.make_async_copy(
        eig_hbm.at[pl.ds(cut, eig_next.shape[0])], eig_next, sem.at[0]
    )
    copy.start()
    make_rows(prod, pick, own, other, lanc16, 0)
    dot_tiles(acc, prod[...], eig, 0)
    out[...] = acc[...].astype(out.dtype)
    copy.wait()


def send_kernel(cut, pick, own, other, lanc16, half, eig, eig_hbm, *rest):
    *outs, prod, eig_rest, acc, sem = rest
    copy = pltpu.make_async_copy(
        eig_hbm.at[pl.ds(cut, eig_rest.shape[0])], eig_rest, sem.at[0]
    )
    copy.start()
    first = half.shape[0]
    prod[:first, :] = half[...]
    make_rows(prod.at[first:, :], pick, own, other, lanc16, first)
    at = 0
    for i, out in enumerate(outs):
        part = acc.at[:, : out.shape[1]]
        if i == 1:
            copy.wait()
        dot_tiles(part, rows_of(prod, i + 1, False), eig_rest if i else eig, at)
        out[...] = part[...].astype(out.dtype)
        at += out.shape[1] if i else 0


def keep_kernel(p, first, prod, eig, out):
    dot_tiles(out, rows_of(prod, p, True), eig, first)


def add_kernel(kept, got, _, leave, keep):
    mid = leave.shape[0]
    leave[...] = (kept[:mid, :] + got[:mid, :].astype(jnp.float32)).astype(leave.dtype)
    keep[...] = kept[mid:, :] + got[mid:, :].astype(jnp.float32)


def write_sums(first, kept, came, out, held, sem):
    at = 0
    for a, b in zip(kept, came):
        end = at + a.shape[1]
        held[:, at:end] = a[...] + b[...].astype(jnp.float32)
        at = end
    copy = pltpu.make_async_copy(held, out.at[:, pl.ds(first, at)], sem.at[0])
    copy.start()
    copy.wait()


def early_kernel(count, *refs):
    write_sums(0, refs[:count], refs[count : 2 * count], *refs[2 * count :])


def finish_kernel(first, _, kept, came, out, held, sem):
    write_sums(first, [kept], [came], out, held, sem)


VMEM_SPEC = pl.BlockSpec(memory_space=pltpu.VMEM)
SPECS = {
    True: pl.BlockSpec(memory_space=pltpu.HBM),
    False: VMEM_SPEC,
    None: pl.BlockSpec(memory_space=pl.ANY),
}


def kernel_call(body, ins, outs, scratch, cost, far_out=False, aliases={}):
    flops, moved = cost
    return pl.pallas_call(
        body,
        out_shape=[jax.ShapeDtypeStruct(*out) for out in outs],
        in_specs=[SPECS[far] for _, far in ins],
        out_specs=[SPECS[far_out]] * len(outs),
        scratch_shapes=scratch,
        input_output_aliases=aliases,
        compiler_params=pltpu.CompilerParams(vmem_limit_bytes=VMEM_LIMIT),
        cost_estimate=pl.CostEstimate(flops=flops, bytes_accessed=moved, transcendentals=0),
    )(
        *(
            pltpu.with_memory_space_constraint(x, pltpu.HBM) if far else x
            for x, far in ins
        )
    )


def per_device(n, eigvecs, lanczos, bands, band_order):
    cols, depth = eigvecs.shape
    lanc = lanczos.shape[0]
    per_chunk = band_order.shape[0] // n
    rows = band_order.shape[0] * lanc
    spans = split_columns(cols)
    cuts = [0] + [end for _, end in spans]
    widths = [end - at for at, end in spans]
    bf16 = jnp.bfloat16

    def exchange(value, p, stage):
        pairs = []
        for i in range(n):
            for core in range(2):
                bit = PLAN[p][1 + core][stage] if stage < 3 else stage
                pairs.append((2 * i + core, 2 * (i ^ (1 << bit)) + core))
        return lax.ppermute(value, ("grid", "eig"), pairs)

    def flops(width):
        return rows * width * depth

    other = lax.ppermute(bands, "eig", [(0, 1), (1, 0)])
    pick, own, lanc16, eig = kernel_call(
        functools.partial(setup_kernel, n, per_chunk, lanc, widths[0]),
        [(band_order, True), (bands, True), (lanczos, True), (eigvecs, True)],
        [
            ((rows, 2 * bands.shape[0]), bf16),
            (bands.shape, bf16),
            (lanczos.shape, bf16),
            ((widths[0], depth), bf16),
        ],
        [pltpu.SMEM(band_order.shape, jnp.int32), pltpu.SemaphoreType.DMA((4,))],
        (0, 2 * widths[0] * depth),
    )
    sources = [(x, False) for x in (pick, own, other, lanc16)]
    send, half, eig_next = kernel_call(
        functools.partial(first_kernel, cuts[1]),
        sources + [(eig, False), (eigvecs, True)],
        [((rows // 2, widths[0]), bf16), ((rows // 2, depth), bf16), ((widths[1], depth), bf16)],
        [pltpu.VMEM((rows // 2, widths[0]), jnp.float32), pltpu.SemaphoreType.DMA((1,))],
        (flops(widths[0]), 2 * widths[0] * depth),
    )
    *sends, prod, eig_rest = kernel_call(
        functools.partial(send_kernel, cuts[2]),
        sources + [(half, False), (eig_next, False), (eigvecs, True)],
        [((rows // 2, w), bf16) for w in widths[1:]]
        + [((rows, depth), bf16), ((cols - cuts[2], depth), bf16)],
        [pltpu.VMEM((rows // 2, max(widths[1:])), jnp.float32), pltpu.SemaphoreType.DMA((1,))],
        (flops(sum(widths[1:])), 2 * sum(widths[1:]) * depth),
    )
    eigs = [eig, eig_next] + [eig_rest] * (len(PLAN) - 2)
    got = [exchange(s, p, 0) for p, s in enumerate([send, *sends])]
    value = []
    for p, width in enumerate(widths):
        value += kernel_call(
            functools.partial(keep_kernel, p, cuts[p] - cuts[min(p, 2)]),
            [(prod, False), (eigs[p], False)],
            [((rows // 2, width), jnp.float32)],
            [],
            (flops(width), 2 * width * depth),
        )
    later = range(3, n.bit_length() - 1)
    token = prod
    for p, stage in ORDER + [(p, stage) for stage in later for p in range(len(PLAN))]:
        part = value[p].shape[0] // 2
        size = part * widths[p]
        leave, value[p] = kernel_call(
            add_kernel,
            [(value[p], False), (got[p], False), (token, None)],
            [((part, widths[p]), bf16 if stage < 3 else jnp.float32)]
            + [((part, widths[p]), jnp.float32)],
            [],
            (2 * size, 18 * size),
        )
        token = leave
        got[p] = exchange(leave, p, stage)
    value = [v[v.shape[0] - rows // n :, :] for v in value]
    last = len(PLAN) - 1
    result = kernel_call(
        functools.partial(early_kernel, last),
        [(v, False) for v in value[:last]] + [(g, False) for g in got[:last]],
        [((rows // n, cols), jnp.float32)],
        [pltpu.VMEM((rows // n, cuts[last]), jnp.float32), pltpu.SemaphoreType.DMA((1,))],
        (rows // n * cuts[last], 10 * rows // n * cuts[last]),
        far_out=True,
    )
    (result,) = kernel_call(
        functools.partial(finish_kernel, cuts[last]),
        [(result[0], True), (value[last], False), (got[last], False)],
        [((rows // n, cols), jnp.float32)],
        [pltpu.VMEM((rows // n, widths[last]), jnp.float32), pltpu.SemaphoreType.DMA((1,))],
        (rows // n * widths[last], 10 * rows // n * widths[last]),
        far_out=True,
        aliases={0: 0},
    )
    return result.reshape(per_chunk, lanc, cols)


def solution(mesh):
    in_specs = (
        P("eig", ("rep", "grid")),
        P(None, ("rep", "grid")),
        P("eig", ("rep", "grid")),
        P("rep"),
    )
    out_specs = P(("rep", "grid"), None, "eig")
    return jax.shard_map(
        functools.partial(per_device, mesh.shape["grid"]),
        mesh=mesh,
        in_specs=in_specs,
        out_specs=out_specs,
        check_vma=False,
    )
```
